128 devices in a mesh: img: 8 (over x, core), pair: 16 (over y, z).
Axes of the slice: x: 4, y: 4, z: 4, core: 2. Of those that a mesh axis runs over, the one named last changes fastest.
Arguments:
- log_depth: float32 [64, 196608], P('pair', 'img'), may hold values from 0.5 to 1.5
- moment_one: float32 [64, 196608], P('pair', 'img'), may hold values from -6 to 6
- moment_two: float32 [64, 196608], P('pair', 'img'), may hold values from 1 to 16
- image_pose: float32 [7, 64], replicated, may hold values from -1 to 2, as said below
- pair_points: bfloat16 [128, 6, 196608], P('pair', None, 'img'), may hold values from -10 to 24
- confidence: bfloat16 [128, 2, 196608], P('pair', None, 'img'), may hold values from 1 to 8
- pair_pose: float32 [7, 128], P(None, 'pair'), may hold values from -1 to 2, as said below
- first_local: int32 [128], P('pair'), may hold values from 0 to 3
- second_owner: int32 [128, 1], P('pair'), may hold values from 0 to 15; in each aligned block of 8 rows (0 to 7, 8 to 15, ...) at most 2 rows name the same one
- second_local: int32 [128], P('pair'), may hold values from 0 to 3
Outputs:
- new_log_depth: float32 [64, 196608], P('pair', 'img')
- new_moment_one: float32 [64, 196608], P('pair', 'img')
- new_moment_two: float32 [64, 196608], P('pair', 'img')
- pair_scale: float32 [128], P('pair')
The draws below stay inside these ranges and needn't reach their ends.
Inputs may be any that keep to these rules, and one draw needn't show every extreme that they name: `second_owner`: among the 8 rows of one index of pair, no owner is named more than 2 times. `image_pose`: row 0 lies in 1 to 2. `pair_pose`: row 0 lies in 1 to 2.
All inputs are finite; a program needn't handle non-finite values.
Results may differ from the reference program's by a relative error of at most 0.0003.
The reference program's roundings to bfloat16 on the way (of `shared`) count: a program that leaves them out, or rounds other values in their place, can miss the bound.
Values may be sent and summed in bfloat16 or wider, within the bound.
A program may use at most 128 MiB of HBM per device.

```python
import math
import jax
import jax.numpy as jnp
import numpy as np
from jax import lax

ROWS = 384
COLS = 512
IMG_DEV = 4
PAIR_DEV = 8
MOST = 2
ITERS = 3
START = 100
OWNERS = 16
IMAGES = 64
PAIRS = 128
PIX = 196608


def pose_table(key, column_count, reach):
    keys = jax.random.split(key, 3)
    head = jax.random.uniform(keys[0], (1, column_count), jnp.float32, 1.0, 2.0)
    tilt = jax.random.uniform(keys[1], (3, column_count), jnp.float32, -0.3, 0.3)
    offset = jax.random.uniform(keys[2], (3, column_count), jnp.float32, -reach, reach)
    return jnp.concatenate([head, tilt, offset], axis=0)


def draw_image_pose(key, part):
    key = jax.random.fold_in(key, 11)
    return pose_table(key, IMAGES, 0.5)


def draw_pair_pose(key, part):
    key = jax.random.fold_in(key, 12)
    return pose_table(key, PAIRS, 1.0)


def draw_pair_points(key, part):
    key = jax.random.fold_in(key, 13)
    pixels = jnp.arange(PIX, dtype=jnp.int32)
    row_pos = (pixels // COLS).astype(jnp.float32)
    col_pos = (pixels % COLS).astype(jnp.float32)
    ray_x = (col_pos + 0.5 - COLS / 2) / COLS
    ray_y = (row_pos + 0.5 - ROWS / 2) / COLS
    ramp = 1.0 + 2.0 * row_pos / ROWS

    def single(index):
        keys = jax.random.split(jax.random.fold_in(key, index), 4)
        depths = jnp.exp(jax.random.uniform(keys[0], (2, PIX), jnp.float32, 0.0, 1.791759)) * ramp
        comp_x = depths * ray_x + jax.random.uniform(keys[1], (2, PIX), jnp.float32, -0.5, 0.5)
        comp_y = depths * ray_y + jax.random.uniform(keys[2], (2, PIX), jnp.float32, -0.5, 0.5)
        comp_z = depths * (1.0 + jax.random.uniform(keys[3], (2, PIX), jnp.float32, -0.3, 0.3))
        return jnp.stack([comp_x, comp_y, comp_z], axis=1).reshape(6, PIX).astype(jnp.bfloat16)
    return lax.map(single, jnp.arange(PAIRS, dtype=jnp.int32))


def with_ends(entries, stream_key, least, largest):
    index_at = [jax.random.randint(jax.random.fold_in(stream_key, axis), (), 0, length) for axis, length in enumerate(entries.shape)]
    widest = entries.shape.index(max(entries.shape))
    beside = index_at[:widest] + [(index_at[widest] + 1) % entries.shape[widest]] + index_at[widest + 1:]
    return entries.at[tuple(index_at)].set(least).at[tuple(beside)].set(largest)


def shard_levels(rng, extent, pieces, low, largest):
    loudness = 1.0
    for axis_at, shards_of in pieces:
        heights = jax.random.uniform(jax.random.fold_in(jax.random.fold_in(rng, 6), axis_at), (shards_of,), jnp.float32, low / len(pieces), largest / len(pieces))
        loudness = loudness * jnp.repeat(jnp.exp(heights), extent[axis_at] // shards_of).reshape((-1,) + (1,) * (len(extent) - 1 - axis_at))
    return loudness


def routed_block(stream_key, own, number, rows, count, top, most, slope):
    order = jax.random.permutation(stream_key, count)
    packed, ordinary = shares(count, rows * top, most, slope, True), shares(count, rows * top, most, slope, False)
    places = jnp.arange(count)

    def named(tallies, turn):
        used = int((tallies > 0).sum())
        fixed = max(1, used // 4)
        shifted = fixed + (places - fixed + turn * (used - fixed)) % max(1, count - fixed)
        return jnp.zeros((count,), jnp.int32).at[order[jnp.where(places < fixed, places, shifted)]].set(jnp.asarray(tallies, jnp.int32))

    tallies = jnp.where(number % 4 == 0, named(packed, number // 4), named(ordinary, number - number // 4 - 1))
    mixed = jax.random.permutation(jax.random.fold_in(own, 3), count)
    source_of, receiver = mixed[0:count // 2 * 2:2], mixed[1:count // 2 * 2:2]
    slack = jnp.minimum(tallies[source_of] - 1, most - tallies[receiver]) // 2
    slack = jnp.where((source_of == order[0]) | (receiver == order[0]) | (tallies[receiver] == 0), 0, jnp.maximum(slack, 0))
    shifted = jax.random.randint(jax.random.fold_in(own, 4), (count // 2,), 0, 1 << 20) % (slack + 1)
    tallies = tallies.at[source_of].add(-shifted).at[receiver].add(shifted)
    members = jnp.searchsorted(jnp.cumsum(tallies), jnp.arange(rows * top), side="right").astype(jnp.int32)
    listing = members.reshape(top, rows).T
    listing = listing[jax.random.permutation(jax.random.fold_in(own, 1), rows)]
    turn = jax.random.randint(jax.random.fold_in(own, 2), (rows, 1), 0, top)
    return jnp.take_along_axis(listing, (jnp.arange(top)[None, :] + turn) % top, axis=1)


def shares(amount, total, most, slope, full):
    weights = [(1 << 20) // math.isqrt(grade ** slope) + 1 for grade in range(1, amount + 1)]
    largest = most if full else min(most, max(-(-total // amount), total * weights[0] // sum(weights)))
    least = 1 if total - largest >= amount - 1 else 0
    given, surplus = [largest] + [least] * (amount - 1), total - largest - least * (amount - 1)
    while surplus > 0:
        movable = [i for i in range(1, amount) if given[i] < largest] or [i for i in range(1, amount) if given[i] < most]
        whole, remaining = sum([weights[i] for i in movable]), surplus
        for i in movable:
            addition = min(most - given[i], max(1, remaining * weights[i] // whole), surplus)
            given[i] = given[i] + addition
            surplus = surplus - addition
    return np.array(given)


def normal_values(key, extent, width, bound, cuts=(), kind=jnp.bfloat16):
    drawn = width * jax.random.normal(key, extent, jnp.float32)
    if cuts:
        drawn = drawn * shard_levels(key, extent, cuts, -0.22, 0.18)
    return jnp.clip(drawn, -bound, bound).astype(kind)


def setup_inputs(seed: int = 0) -> dict:
    arg_keys = jax.random.split(jax.random.key(seed), 11)
    log_depth = jnp.clip(0.5 + 1.0 * jax.random.uniform(arg_keys[0], (IMAGES, PIX), jnp.float32) ** shard_levels(arg_keys[0], (IMAGES, PIX), ((0, 16), (1, 8)), -0.2, 0.2), 0.5, 1.5)
    moment_one = normal_values(arg_keys[1], (IMAGES, PIX), 1.0, 6.0, ((0, 16), (1, 8)), jnp.float32)
    moment_two = jnp.clip(jnp.exp(math.log(16.0) - 2.7725887 * jax.random.uniform(arg_keys[2], (IMAGES, PIX), jnp.float32) ** shard_levels(arg_keys[2], (IMAGES, PIX), ((0, 16), (1, 8)), -0.2, 0.2)), 1.0, 16.0)
    image_pose = draw_image_pose(jax.random.fold_in(arg_keys[10], 71), 0)
    pair_points = draw_pair_points(jax.random.fold_in(arg_keys[10], 71), 0)
    confidence = jnp.clip(jnp.exp(math.log(8.0) - 2.0794415 * jax.random.uniform(arg_keys[5], (PAIRS, 2, PIX), jnp.float32) ** shard_levels(arg_keys[5], (PAIRS, 2, PIX), ((0, 16), (2, 8)), -0.2, 0.2)), 1.0, 8.0).astype(jnp.bfloat16)
    pair_pose = draw_pair_pose(jax.random.fold_in(arg_keys[10], 71), 0)
    first_local = with_ends(jax.random.randint(arg_keys[7], (PAIRS,), 0, IMG_DEV), jax.random.fold_in(arg_keys[7], 1), 0, IMG_DEV - 1).astype(jnp.int32)
    second_owner_keys = jax.random.split(jax.random.fold_in(arg_keys[8], 1), PAIRS // PAIR_DEV)
    second_owner_turns = jax.random.permutation(jax.random.fold_in(arg_keys[8], 3), PAIRS // PAIR_DEV)
    second_owner = jax.vmap(lambda own, number: routed_block(jax.random.fold_in(arg_keys[8], 2), own, number, PAIR_DEV, OWNERS, 1, MOST, 2))(second_owner_keys, second_owner_turns).reshape((PAIRS, 1))
    second_local = with_ends(jax.random.randint(arg_keys[9], (PAIRS,), 0, IMG_DEV), jax.random.fold_in(arg_keys[9], 1), 0, IMG_DEV - 1).astype(jnp.int32)
    return {"log_depth": log_depth, "moment_one": moment_one, "moment_two": moment_two, "image_pose": image_pose, "pair_points": pair_points, "confidence": confidence, "pair_pose": pair_pose, "first_local": first_local, "second_owner": second_owner, "second_local": second_local}


beta_one = 0.9
beta_two = 0.999
learn_rate = 0.01
adam_eps = 1e-08

def ray_dirs(pixels):
    row_pos = (pixels // COLS).astype(jnp.float32)
    col_pos = (pixels % COLS).astype(jnp.float32)
    return ((col_pos + 0.5 - COLS / 2) / COLS, (row_pos + 0.5 - ROWS / 2) / COLS)

def rotation(scalar_q, vec_a, vec_b, vec_c):
    magnitude = jnp.sqrt(scalar_q * scalar_q + vec_a * vec_a + vec_b * vec_b + vec_c * vec_c)
    unit_s = scalar_q / magnitude
    unit_a = vec_a / magnitude
    unit_b = vec_b / magnitude
    unit_c = vec_c / magnitude
    return ((1 - 2 * (unit_b * unit_b + unit_c * unit_c), 2 * (unit_a * unit_b - unit_s * unit_c), 2 * (unit_a * unit_c + unit_s * unit_b)), (2 * (unit_a * unit_b + unit_s * unit_c), 1 - 2 * (unit_a * unit_a + unit_c * unit_c), 2 * (unit_b * unit_c - unit_s * unit_a)), (2 * (unit_a * unit_c - unit_s * unit_b), 2 * (unit_b * unit_c + unit_s * unit_a), 1 - 2 * (unit_a * unit_a + unit_b * unit_b)))

def rigid_map(coords, pose_cols):
    matrix = rotation(pose_cols[0], pose_cols[1], pose_cols[2], pose_cols[3])
    rotated = [matrix[coord_id][0] * coords[0] + matrix[coord_id][1] * coords[1] + matrix[coord_id][2] * coords[2] for coord_id in range(3)]
    placed = [rotated[coord_id] + pose_cols[4 + coord_id] for coord_id in range(3)]
    return (placed, rotated)

def world_points(rows_f, pose_cols, ray_x, ray_y):
    depths = jnp.exp(rows_f)
    return rigid_map((depths * ray_x, depths * ray_y, depths), pose_cols)

def reference(log_depth, moment_one, moment_two, image_pose, pair_points, confidence, pair_pose, first_local, second_owner, second_local):
    pair_ids = jnp.arange(PAIRS, dtype=jnp.int32)
    first_global = pair_ids // PAIR_DEV * IMG_DEV + first_local
    second_global = second_owner[:, 0] * IMG_DEV + second_local
    ray_x, ray_y = ray_dirs(jnp.arange(PIX, dtype=jnp.int32))
    scales = jnp.zeros((PAIRS,), jnp.float32)
    for sweep in range(ITERS):
        shared = lax.optimization_barrier(log_depth.astype(jnp.bfloat16)).astype(jnp.float32)

        def visit(total, scanned):
            points, weight, pose_vec, first_img, second_img = scanned
            raw = points.astype(jnp.float32).reshape(2, 3, PIX)
            aligned_list, unused = rigid_map((raw[:, 0], raw[:, 1], raw[:, 2]), [pose_vec[k] for k in range(7)])
            aligned = jnp.stack(aligned_list, axis=1)
            world_one, lever_one = world_points(shared[first_img], [image_pose[k, first_img] for k in range(7)], ray_x, ray_y)
            world_two, lever_two = world_points(shared[second_img], [image_pose[k, second_img] for k in range(7)], ray_x, ray_y)
            world = jnp.stack([jnp.stack(world_one, axis=0), jnp.stack(world_two, axis=0)], axis=0)
            levers = jnp.stack([jnp.stack(lever_one, axis=0), jnp.stack(lever_two, axis=0)], axis=0)
            weights = weight.astype(jnp.float32)
            denominator = jnp.sum(weights * lax.optimization_barrier(jnp.sum(aligned * aligned, axis=1)))
            numerator = jnp.sum(weights * lax.optimization_barrier(jnp.sum(world * aligned, axis=1)))
            pair_scale = numerator / denominator
            residual = world - pair_scale * aligned
            gradient = 2.0 * weights * lax.optimization_barrier(jnp.sum(residual * levers, axis=1))
            total = total.at[first_img].add(gradient[0])
            total = total.at[second_img].add(gradient[1])
            return (total, pair_scale)
        gradient, scales = lax.scan(visit, jnp.zeros((IMAGES, PIX), jnp.float32), (pair_points, confidence, pair_pose.T, first_global, second_global))
        step_count = START + sweep + 1
        moment_one = beta_one * moment_one + (1 - beta_one) * gradient
        moment_two = beta_two * moment_two + (1 - beta_two) * gradient * gradient
        corrected_one = moment_one / (1 - beta_one ** step_count)
        corrected_two = moment_two / (1 - beta_two ** step_count)
        log_depth = log_depth - learn_rate * corrected_one / (jnp.sqrt(corrected_two) + adam_eps)
    return (log_depth, moment_one, moment_two, scales)
```

```python
import jax
import jax.numpy as jnp
from jax import lax
from jax.experimental import pallas as pl
from jax.experimental.pallas import tpu as pltpu
from jax.sharding import PartitionSpec as P

ROWS = 384
COLS = 512
ITERS = 3
START = 100
IMG_DEV = 4
PAIR_DEV = 8
MOST = 2
IMGS = 8
OWNERS = 16
YS = 4
ZS = 4
BAND = ROWS * COLS // IMGS
GROUPS = BAND // 128
BLOCKS = GROUPS // 8
BAND_ROWS = ROWS // IMGS
SLOTS = OWNERS * MOST
VIEWS = PAIR_DEV + SLOTS
CODE_ROWS = 2 * GROUPS + 16
TILE = 4
LEVELS = 32700.0
SCALE_STEPS = 64.0

beta_one = 0.9
beta_two = 0.999
learn_rate = 0.01
adam_eps = 1e-08
f32 = jnp.float32
MESH = pl.DeviceIdType.MESH


def rotation(scalar_q, vec_a, vec_b, vec_c):
    magnitude = jnp.sqrt(scalar_q * scalar_q + vec_a * vec_a + vec_b * vec_b + vec_c * vec_c)
    unit_s = scalar_q / magnitude
    unit_a = vec_a / magnitude
    unit_b = vec_b / magnitude
    unit_c = vec_c / magnitude
    return (
        (
            1 - 2 * (unit_b * unit_b + unit_c * unit_c),
            2 * (unit_a * unit_b - unit_s * unit_c),
            2 * (unit_a * unit_c + unit_s * unit_b),
        ),
        (
            2 * (unit_a * unit_b + unit_s * unit_c),
            1 - 2 * (unit_a * unit_a + unit_c * unit_c),
            2 * (unit_b * unit_c - unit_s * unit_a),
        ),
        (
            2 * (unit_a * unit_c - unit_s * unit_b),
            2 * (unit_b * unit_c + unit_s * unit_a),
            1 - 2 * (unit_a * unit_a + unit_b * unit_b),
        ),
    )


def kernel(
    log_ref,
    one_ref,
    two_ref,
    points_ref,
    conf_ref,
    image_pose,
    pair_pose,
    first_local,
    second_owner,
    second_local,
    log_out,
    one_out,
    two_out,
    scale_out,
    conf_f,
    stage_one,
    stage_two,
    codes,
    send_buf,
    recv_buf,
    meta,
    cu_ref,
    weight_sum,
    depth_ref,
    tau_ref,
    hot_ref,
    mask_ref,
    weight_ref,
    inner_ref,
    img_buf,
    pair_buf,
    image_tab,
    send_sem,
    recv_sem,
    meta_send,
    meta_recv,
    img_send,
    img_recv,
    pair_send,
    pair_recv,
):
    my_img = lax.axis_index("img")
    my_pair = lax.axis_index("pair")
    my_y = my_pair // ZS
    my_z = my_pair % ZS

    def pair_at(k, sign):
        return ((my_y + sign * (k // ZS) + YS) % YS) * ZS + (my_z + sign * (k % ZS) + ZS) % ZS

    barrier = pltpu.get_barrier_semaphore()

    def greet_pair(k, carry):
        pl.semaphore_signal(barrier, 1, device_id=(my_img, pair_at(k, -1)), device_id_type=MESH)
        return carry

    def greet_img(k, carry):
        pl.semaphore_signal(barrier, 1, device_id=((my_img + k) % IMGS, my_pair), device_id_type=MESH)
        return carry

    lax.fori_loop(1, OWNERS, greet_pair, 0)
    lax.fori_loop(1, IMGS, greet_img, 0)

    sub = lax.broadcasted_iota(jnp.int32, (8, 128), 0)
    lane = lax.broadcasted_iota(jnp.int32, (8, 128), 1)

    owners = [second_owner[e] for e in range(PAIR_DEV)]
    order = []
    for e in range(PAIR_DEV):
        rank = jnp.int32(0)
        for other in range(e):
            rank = rank + jnp.where(owners[other] == owners[e], 1, 0)
        order.append(owners[e] * MOST + rank)
    row = jnp.zeros((8, 128), jnp.int32)
    for e in range(PAIR_DEV):
        here = lane == my_pair * PAIR_DEV + e
        row = jnp.where(here & (sub == 0), order[e], row)
        row = jnp.where(here & (sub == 1), second_local[e], row)
    meta[0] = row

    def column(values):
        out = jnp.zeros((8, 128), f32)
        for e in range(PAIR_DEV):
            out = jnp.where(sub == e, values[e], out)
        return out

    pair_cols = [column([pair_pose[i, e] for e in range(PAIR_DEV)]) for i in range(7)]
    pair_rot = rotation(*pair_cols[:4])
    shift = pair_cols[4:]
    firsts = [my_pair * IMG_DEV + first_local[e] for e in range(PAIR_DEV)]
    seconds = [owners[e] * IMG_DEV + second_local[e] for e in range(PAIR_DEV)]
    lean = [2.0 * sum(pair_rot[i][j] * shift[i] for i in range(3)) for j in range(3)]
    shift_sq = sum(shift[i] * shift[i] for i in range(3))
    first_row = (my_img * BAND_ROWS).astype(f32)
    ray_y0 = (first_row + 0.5 - ROWS / 2) / COLS
    ray_x = [((lane + 128 * part).astype(f32) + 0.5 - COLS / 2) / COLS for part in range(4)]

    def widen(step, carry):
        rows = pl.ds(pl.multiple_of(step * 64, 64), 64)
        conf_f[rows, :] = conf_ref[rows, :].astype(f32)
        return carry

    lax.fori_loop(0, PAIR_DEV * 2 * GROUPS // 64, widen, 0)

    def prepare(view, images, stage, scaled):
        cols = [column([image_pose[i, images[e]] for e in range(PAIR_DEV)]) for i in range(7)]
        rot = rotation(*cols[:4])
        trans = cols[4:]
        both = [[sum(rot[l][i] * pair_rot[l][j] for l in range(3)) for j in range(3)] for i in range(3)]
        moved = [sum(rot[l][i] * shift[l] for l in range(3)) for i in range(3)]
        full = [[both[i][0], both[i][1], both[i][2], moved[i]] for i in range(3)]
        base = [[ray_x[part] * full[0][j] + (full[2][j] + ray_y0 * full[1][j]) for part in range(4)] for j in range(4)]
        slope = [full[1][j] * (1.0 / COLS) for j in range(4)]
        toward = [sum(trans[l] * pair_rot[l][j] for l in range(3)) for j in range(3)]
        offset = sum(trans[l] * shift[l] for l in range(3))

        def body(r, carry):
            total_sq, total_dot, total_conf = carry
            down = r.astype(f32)
            tilt = [slope[j] * down for j in range(4)]
            for part in range(4):
                at = pl.ds(pl.multiple_of(r * COLS + part * 128, 128), 128)
                x = [points_ref[3 * view + j, :, at].astype(f32) for j in range(3)]
                weight = conf_f[pl.ds((r * 4 + part) * 2 + view, 8, stride=2 * GROUPS), :]
                value = base[3][part] + tilt[3]
                for j in range(3):
                    value = value + (base[j][part] + tilt[j]) * x[j]
                if scaled:
                    value = value * weight
                stage[pl.ds(pl.multiple_of((r * 4 + part) * 8, 8), 8), :] = value
                square = x[0] * (x[0] + lean[0]) + x[1] * (x[1] + lean[1]) + x[2] * (x[2] + lean[2])
                dot = x[0] * toward[0] + x[1] * toward[1] + x[2] * toward[2]
                total_sq = total_sq + weight * square
                total_dot = total_dot + weight * dot
                total_conf = total_conf + weight
            return (total_sq, total_dot, total_conf)

        zero = jnp.zeros((8, 128), f32)
        total_sq, total_dot, total_conf = lax.fori_loop(0, BAND_ROWS, body, (zero, zero, zero))
        return (total_sq + total_conf * shift_sq, total_dot + total_conf * offset)

    square_two, dot_two = prepare(1, seconds, stage_two, False)

    def encode(e, carry):
        largest = jnp.full((8, 128), 1e-30, f32)
        for block in range(BLOCKS):
            largest = jnp.maximum(largest, jnp.abs(stage_two[pl.ds(block * 64 + e, 8, stride=8), :]))
        power = jnp.ceil(jnp.log(largest) * (SCALE_STEPS / 0.6931471805599453)).astype(jnp.int32)
        inverse = LEVELS / jnp.exp(power.astype(f32) * (0.6931471805599453 / SCALE_STEPS))
        inverse = jnp.concatenate([inverse, inverse], axis=0)
        for half in range(BLOCKS // 2):
            value = stage_two[pl.ds(half * 128 + e, 16, stride=8), :] * inverse
            value = jnp.floor(value + 0.5).astype(jnp.int32).astype(jnp.int16)
            codes[e, half * 16 : half * 16 + 16, :] = value
            weight = conf_f[pl.ds(e * 2 * GROUPS + half * 32 + 1, 16, stride=2), :] * 128.0
            codes[e, GROUPS + half * 16 : GROUPS + half * 16 + 16, :] = weight.astype(jnp.int32).astype(jnp.int16)
        codes[e, 2 * GROUPS : 2 * GROUPS + 16, :] = jnp.concatenate([power, power], axis=0).astype(jnp.int16)
        return carry

    lax.fori_loop(0, PAIR_DEV, encode, 0)

    def slot_pair(k, j):
        wanted = pair_at(k, 1) * MOST + j
        found = jnp.int32(0)
        for e in range(1, PAIR_DEV):
            found = found + jnp.where(order[e] == wanted, e, 0)
        return found

    for j in range(MOST):
        recv_buf[0, j] = codes[slot_pair(0, j)]

    pl.semaphore_wait(barrier, OWNERS - 1 + IMGS - 1)

    def meta_copy(k):
        return pltpu.make_async_remote_copy(
            src_ref=meta.at[0],
            dst_ref=meta.at[k],
            send_sem=meta_send.at[k],
            recv_sem=meta_recv.at[k],
            device_id=(my_img, pair_at(k, 1)),
            device_id_type=MESH,
        )

    def slot_copy(k):
        return pltpu.make_async_remote_copy(
            src_ref=send_buf.at[k],
            dst_ref=recv_buf.at[k],
            send_sem=send_sem.at[k],
            recv_sem=recv_sem.at[k],
            device_id=(my_img, pair_at(k, 1)),
            device_id_type=MESH,
        )

    def start_meta(k, carry):
        meta_copy(k).start()
        return carry

    def start_slots(k, carry):
        for j in range(MOST):
            send_buf[k, j] = codes[slot_pair(k, j)]
        slot_copy(k).start()
        return carry

    lax.fori_loop(1, OWNERS, start_meta, 0)
    lax.fori_loop(1, OWNERS, start_slots, 0)

    square_one, dot_one = prepare(0, firsts, stage_one, True)

    def depth_of(values):
        return jnp.exp(values.astype(jnp.bfloat16).astype(f32))

    def image_rows(block, v):
        return pl.ds(block * 32 + v, 8, stride=IMG_DEV)

    def block_rows(block):
        return pl.ds(pl.multiple_of(block * 8, 8), 8)

    def first_depth(block, carry):
        for v in range(IMG_DEV):
            depth_ref[v, block_rows(block), :] = depth_of(log_ref[image_rows(block, v), :])
        return carry

    lax.fori_loop(0, BLOCKS, first_depth, 0)

    own = [[image_pose[i, my_pair * IMG_DEV + min(v, IMG_DEV - 1)] for v in range(8)] for i in range(7)]
    own_cols = [column(own[i]) for i in range(7)]
    own_rot = rotation(*own_cols[:4])
    for i in range(3):
        tau_ref[i] = sum(own_rot[l][i] * own_cols[4 + l] for l in range(3))

    for k in range(1, OWNERS):
        meta_copy(k).wait_recv()
    known = meta[0]
    for k in range(1, OWNERS):
        known = known + meta[k]
    code_row = jnp.broadcast_to(known[0:1], (8, 128))
    local_row = jnp.broadcast_to(known[1:2], (8, 128))
    from_pair = lane // PAIR_DEV
    step_of = ((my_y - from_pair // ZS + YS) % YS) * ZS + (my_z - from_pair % ZS + ZS) % ZS
    slot_of = jnp.where(code_row // MOST == my_pair, step_of * MOST + code_row % MOST, -1)
    local_first = jnp.zeros((8, 128), jnp.int32)
    for e in range(PAIR_DEV):
        local_first = jnp.where(sub == e, first_local[e], local_first)
    own_mask = jnp.where(lane == my_pair * PAIR_DEV + sub, 1.0, 0.0)
    mask_ref[0:8, :] = own_mask
    for v in range(IMG_DEV):
        hot_ref[v, 0:8, :] = jnp.where(local_first == v, 1.0, 0.0)
    for group in range(SLOTS // 8):
        rows = pl.ds(8 + group * 8, 8)
        held = slot_of == sub + group * 8
        mask_ref[rows, :] = jnp.where(held, 1.0, 0.0)
        for v in range(IMG_DEV):
            found = jnp.where(held & (local_row == v), 1.0, 0.0)
            hot_ref[v, rows, :] = jnp.broadcast_to(jnp.sum(found, axis=1, keepdims=True), (8, 128))
    for e in range(PAIR_DEV):
        image_tab[e] = first_local[e]

    def find_image(r, carry):
        image_tab[PAIR_DEV + r] = jnp.sum(jnp.where((slot_of == r) & (sub == 0), local_row, 0))
        return carry

    lax.fori_loop(0, SLOTS, find_image, 0)

    def first_cu(e, block):
        return stage_one[pl.ds(block * 64 + e, 8, stride=8), :]

    def dot_first(e, carry):
        v = image_tab[e]
        total = jnp.zeros((8, 128), f32)
        for block in range(BLOCKS):
            total = total + first_cu(e, block) * depth_ref[v, block * 8 : block * 8 + 8, :]
        inner_ref[pl.ds(e, 1), :] = jnp.sum(total, axis=0, keepdims=True)
        return carry

    def dot_second(r, carry):
        v = image_tab[PAIR_DEV + r]
        total = jnp.zeros((8, 128), f32)
        for block in range(BLOCKS):
            total = total + cu_ref[r, block * 8 : block * 8 + 8, :] * depth_ref[v, block * 8 : block * 8 + 8, :]
        inner_ref[pl.ds(PAIR_DEV + r, 1), :] = jnp.sum(total, axis=0, keepdims=True)
        return carry

    lax.fori_loop(0, PAIR_DEV, dot_first, 0)

    def first_sums(block, carry):
        sums = [jnp.zeros((8, 128), f32) for v in range(IMG_DEV)]
        for e in range(PAIR_DEV):
            weight = conf_f[pl.ds(e * 2 * GROUPS + block * 16, 8, stride=2), :]
            for v in range(IMG_DEV):
                sums[v] = sums[v] + weight * hot_ref[v, e : e + 1, :]
        for v in range(IMG_DEV):
            weight_sum[v, block_rows(block), :] = sums[v]
        return carry

    lax.fori_loop(0, BLOCKS, first_sums, 0)

    def take(k, carry):
        @pl.when(k > 0)
        def _():
            slot_copy(k).wait_recv()

        units, hots, images = [], [], []
        for j in range(MOST):
            power = recv_buf[k, j, 2 * GROUPS : 2 * GROUPS + 16, :].astype(jnp.int32).astype(f32)
            unit = jnp.exp(power * (0.6931471805599453 / SCALE_STEPS)) * (1.0 / (LEVELS * 128.0))
            units.append(unit)
            slot = PAIR_DEV + k * MOST + j
            hots.append([hot_ref[v, pl.ds(slot, 1), :] * (1.0 / 128.0) for v in range(IMG_DEV)])
            images.append(image_tab[slot])

        def part(half, totals):
            totals = list(totals)
            rows = pl.ds(pl.multiple_of(half * 16, 16), 16)
            weight_rows = pl.ds(pl.multiple_of(GROUPS + half * 16, 16), 16)
            sums = [weight_sum[v, rows, :] for v in range(IMG_DEV)]
            for j in range(MOST):
                value = recv_buf[k, j, rows, :].astype(jnp.int32).astype(f32)
                weight = recv_buf[k, j, weight_rows, :].astype(jnp.int32).astype(f32)
                cu = value * units[j] * weight
                cu_ref[k * MOST + j, rows, :] = cu
                totals[j] = totals[j] + cu * depth_ref[images[j], rows, :]
                for v in range(IMG_DEV):
                    sums[v] = sums[v] + weight * hots[j][v]
            for v in range(IMG_DEV):
                weight_sum[v, rows, :] = sums[v]
            return tuple(totals)

        totals = lax.fori_loop(0, BLOCKS // 2, part, tuple(jnp.zeros((16, 128), f32) for j in range(MOST)))
        for j in range(MOST):
            inner_ref[pl.ds(PAIR_DEV + k * MOST + j, 1), :] = jnp.sum(totals[j], axis=0, keepdims=True)
        return carry

    lax.fori_loop(0, OWNERS, take, 0)

    def pair_row(col):
        return jnp.sum(jnp.sum(col, axis=1, keepdims=True) * own_mask, axis=0, keepdims=True)

    fixed_row = pair_row(dot_one + dot_two)
    square_row = pair_row(square_one + square_two)

    def img_copy(t, k):
        return pltpu.make_async_remote_copy(
            src_ref=img_buf.at[t, my_img],
            dst_ref=img_buf.at[t, my_img],
            send_sem=img_send.at[t, k],
            recv_sem=img_recv.at[t, my_img],
            device_id=((my_img + k) % IMGS, my_pair),
            device_id_type=MESH,
        )

    def img_arrival(t, k):
        source = (my_img + k) % IMGS
        return pltpu.make_async_remote_copy(
            src_ref=img_buf.at[t, source],
            dst_ref=img_buf.at[t, source],
            send_sem=img_send.at[t, k],
            recv_sem=img_recv.at[t, source],
            device_id=(source, my_pair),
            device_id_type=MESH,
        )

    def pair_copy(t, k):
        return pltpu.make_async_remote_copy(
            src_ref=pair_buf.at[t, my_pair],
            dst_ref=pair_buf.at[t, my_pair],
            send_sem=pair_send.at[t, k],
            recv_sem=pair_recv.at[t, my_pair],
            device_id=(my_img, pair_at(k, 1)),
            device_id_type=MESH,
        )

    def pair_arrival(t, k):
        source = pair_at(k, 1)
        return pltpu.make_async_remote_copy(
            src_ref=pair_buf.at[t, source],
            dst_ref=pair_buf.at[t, source],
            send_sem=pair_send.at[t, k],
            recv_sem=pair_recv.at[t, source],
            device_id=(my_img, source),
            device_id_type=MESH,
        )

    def sum_all(t, tile):
        img_buf[t, my_img] = tile
        for k in range(1, IMGS):
            img_copy(t, k).start()
        for k in range(1, IMGS):
            img_arrival(t, k).wait_recv()
        total = img_buf[t, 0]
        for k in range(1, IMGS):
            total = total + img_buf[t, k]
        pair_buf[t, my_pair] = total
        for k in range(1, OWNERS):
            pair_copy(t, k).start()
        for k in range(1, OWNERS):
            pair_arrival(t, k).wait_recv()
        total = pair_buf[t, 0]
        for k in range(1, OWNERS):
            total = total + pair_buf[t, k]
        return total

    denominator = None
    for sweep in range(ITERS):
        row = jnp.zeros((8, 128), f32)
        for group in range(VIEWS // 8):
            rows = slice(group * 8, group * 8 + 8)
            row = row + jnp.sum(inner_ref[rows, :], axis=1, keepdims=True) * mask_ref[rows, :]
        row = jnp.sum(row, axis=0, keepdims=True) + fixed_row
        tile = jnp.where(sub == 0, row, jnp.where(sub == 1, square_row, 0.0))
        total = sum_all(sweep, tile)
        if sweep == 0:
            denominator = total[1:2]
        scales = jnp.broadcast_to(total[0:1] / denominator, (8, 128))
        for group in range(VIEWS // 8):
            rows = slice(group * 8, group * 8 + 8)
            held = jnp.sum(scales * mask_ref[rows, :], axis=1, keepdims=True)
            if group == 0 and sweep == ITERS - 1:
                own_row = jnp.sum(jnp.where(lane == sub, held, 0.0), axis=0, keepdims=True)
                scale_out[...] = own_row[:, 0:PAIR_DEV]
            for v in range(IMG_DEV):
                weight_ref[v, rows, :] = held * hot_ref[v, rows, :]

        steps = START + sweep + 1
        bias_one = 1 - beta_one**steps
        bias_two = 1 - beta_two**steps
        last = sweep == ITERS - 1

        def update(tile_id, carry):
            start = tile_id * TILE

            def gather_first(e, sums):
                sums = list(sums)
                for n in range(TILE):
                    cu = first_cu(e, start + n)
                    for v in range(IMG_DEV):
                        sums[n * IMG_DEV + v] = sums[n * IMG_DEV + v] + cu * weight_ref[v, pl.ds(e, 1), :]
                return tuple(sums)

            def gather_second(r, sums):
                sums = list(sums)
                for n in range(TILE):
                    cu = cu_ref[r, block_rows(start + n), :]
                    for v in range(IMG_DEV):
                        sums[n * IMG_DEV + v] = sums[n * IMG_DEV + v] + cu * weight_ref[v, pl.ds(PAIR_DEV + r, 1), :]
                return tuple(sums)

            sums = tuple(jnp.zeros((8, 128), f32) for i in range(TILE * IMG_DEV))
            sums = lax.fori_loop(0, PAIR_DEV, gather_first, sums)
            sums = lax.fori_loop(0, SLOTS, gather_second, sums)
            for n in range(TILE):
                block = start + n
                down = (block * 2 + sub // 4).astype(f32) + first_row
                rays_y = (down + 0.5 - ROWS / 2) / COLS
                rays_x = (((sub % 4) * 128 + lane).astype(f32) + 0.5 - COLS / 2) / COLS
                length = rays_x * rays_x + rays_y * rays_y + 1.0
                for v in range(IMG_DEV):
                    depth = depth_ref[v, block_rows(block), :]
                    lever = rays_x * tau_ref[0, v : v + 1, :] + rays_y * tau_ref[1, v : v + 1, :] + tau_ref[2, v : v + 1, :]
                    pull = (depth * length + lever) * weight_sum[v, block_rows(block), :] - sums[n * IMG_DEV + v]
                    gradient = 2.0 * depth * pull
                    rows = image_rows(block, v)
                    old_one = (one_ref if sweep == 0 else one_out)[rows, :]
                    old_two = (two_ref if sweep == 0 else two_out)[rows, :]
                    old_log = (log_ref if sweep == 0 else log_out)[rows, :]
                    new_one = beta_one * old_one + (1 - beta_one) * gradient
                    new_two = beta_two * old_two + (1 - beta_two) * gradient * gradient
                    corrected_one = new_one * (1 / bias_one)
                    corrected_two = new_two * (1 / bias_two)
                    new_log = old_log - learn_rate * corrected_one / (jnp.sqrt(corrected_two) + adam_eps)
                    one_out[rows, :] = new_one
                    two_out[rows, :] = new_two
                    log_out[rows, :] = new_log
                    if not last:
                        depth_ref[v, block_rows(block), :] = depth_of(new_log)
            return carry

        lax.fori_loop(0, BLOCKS // TILE, update, 0)
        if not last:
            lax.fori_loop(0, PAIR_DEV, dot_first, 0)
            lax.fori_loop(0, SLOTS, dot_second, 0)

    def finish(k, carry):
        meta_copy(k).wait_send()
        slot_copy(k).wait_send()
        return carry

    lax.fori_loop(1, OWNERS, finish, 0)
    for t in range(ITERS):
        for k in range(1, IMGS):
            img_copy(t, k).wait_send()
        for k in range(1, OWNERS):
            pair_copy(t, k).wait_send()


def shards(
    log_depth,
    moment_one,
    moment_two,
    image_pose,
    pair_points,
    confidence,
    pair_pose,
    first_local,
    second_owner,
    second_local,
):
    def fold(a):
        return a.reshape(IMG_DEV, GROUPS, 128).transpose(1, 0, 2).reshape(GROUPS * IMG_DEV, 128)

    def unfold(a):
        return a.reshape(GROUPS, IMG_DEV, 128).transpose(1, 0, 2).reshape(IMG_DEV, BAND)

    points = pair_points.transpose(1, 0, 2)
    conf = confidence.reshape(PAIR_DEV, 2, GROUPS, 128).transpose(0, 2, 1, 3).reshape(PAIR_DEV * GROUPS * 2, 128)
    vmem = pl.BlockSpec(memory_space=pltpu.VMEM)
    smem = pl.BlockSpec(memory_space=pltpu.SMEM)
    band = jax.ShapeDtypeStruct((GROUPS * IMG_DEV, 128), f32)
    dma = pltpu.SemaphoreType.DMA
    out = pl.pallas_call(
        kernel,
        out_shape=(band, band, band, jax.ShapeDtypeStruct((1, PAIR_DEV), f32)),
        in_specs=[vmem] * 5 + [smem] * 5,
        out_specs=(vmem,) * 4,
        scratch_shapes=[
            pltpu.VMEM((PAIR_DEV * GROUPS * 2, 128), f32),
            pltpu.VMEM((PAIR_DEV * GROUPS, 128), f32),
            pltpu.VMEM((PAIR_DEV * GROUPS, 128), f32),
            pltpu.VMEM((PAIR_DEV, CODE_ROWS, 128), jnp.int16),
            pltpu.VMEM((OWNERS, MOST, CODE_ROWS, 128), jnp.int16),
            pltpu.VMEM((OWNERS, MOST, CODE_ROWS, 128), jnp.int16),
            pltpu.VMEM((OWNERS, 8, 128), jnp.int32),
            pltpu.VMEM((SLOTS, GROUPS, 128), f32),
            pltpu.VMEM((IMG_DEV, GROUPS, 128), f32),
            pltpu.VMEM((IMG_DEV, GROUPS, 128), f32),
            pltpu.VMEM((3, 8, 128), f32),
            pltpu.VMEM((IMG_DEV, VIEWS, 128), f32),
            pltpu.VMEM((VIEWS, 128), f32),
            pltpu.VMEM((IMG_DEV, VIEWS, 128), f32),
            pltpu.VMEM((VIEWS, 128), f32),
            pltpu.VMEM((ITERS, IMGS, 8, 128), f32),
            pltpu.VMEM((ITERS, OWNERS, 8, 128), f32),
            pltpu.SMEM((VIEWS,), jnp.int32),
            dma((OWNERS,)),
            dma((OWNERS,)),
            dma((OWNERS,)),
            dma((OWNERS,)),
            dma((ITERS, IMGS)),
            dma((ITERS, IMGS)),
            dma((ITERS, OWNERS)),
            dma((ITERS, OWNERS)),
        ],
        compiler_params=pltpu.CompilerParams(
            collective_id=0, has_side_effects=True, vmem_limit_bytes=48 * 2**20
        ),
        name="align",
    )(
        fold(log_depth),
        fold(moment_one),
        fold(moment_two),
        points,
        conf,
        image_pose,
        pair_pose,
        first_local,
        second_owner.reshape(PAIR_DEV),
        second_local,
    )
    return (unfold(out[0]), unfold(out[1]), unfold(out[2]), out[3].reshape(PAIR_DEV))


def solution(mesh):
    return jax.shard_map(
        shards,
        mesh=mesh,
        in_specs=(
            P("pair", "img"),
            P("pair", "img"),
            P("pair", "img"),
            P(),
            P("pair", None, "img"),
            P("pair", None, "img"),
            P(None, "pair"),
            P("pair"),
            P("pair", None),
            P("pair"),
        ),
        out_specs=(P("pair", "img"), P("pair", "img"), P("pair", "img"), P("pair")),
        check_vma=False,
    )
```

```python
import jax
import jax.numpy as jnp
from jax import lax
from jax.experimental import pallas as pl
from jax.experimental.pallas import tpu as pltpu
from jax.sharding import PartitionSpec as P

ROWS = 384
COLS = 512
ITERS = 3
START = 100
IMG_DEV = 4
PAIR_DEV = 8
MOST = 2
IMGS = 8
OWNERS = 16
XS = 4
YS = 4
ZS = 4
CHIPS = XS * YS * ZS
BAND = ROWS * COLS // IMGS
GROUPS = BAND // 128
BLOCKS = GROUPS // 8
BAND_ROWS = ROWS // IMGS
SLOTS = OWNERS * MOST
VIEWS = PAIR_DEV + SLOTS
CODE_ROWS = 2 * GROUPS + 16
TILE = 12
PART = 4
UNROLL = 4
LEVELS = 32700.0
SCALE_STEPS = 64.0

beta_one = 0.9
beta_two = 0.999
learn_rate = 0.01
adam_eps = 1e-08
f32 = jnp.float32
MESH = pl.DeviceIdType.MESH


def rotation(scalar_q, vec_a, vec_b, vec_c):
    magnitude = jnp.sqrt(scalar_q * scalar_q + vec_a * vec_a + vec_b * vec_b + vec_c * vec_c)
    unit_s = scalar_q / magnitude
    unit_a = vec_a / magnitude
    unit_b = vec_b / magnitude
    unit_c = vec_c / magnitude
    return (
        (
            1 - 2 * (unit_b * unit_b + unit_c * unit_c),
            2 * (unit_a * unit_b - unit_s * unit_c),
            2 * (unit_a * unit_c + unit_s * unit_b),
        ),
        (
            2 * (unit_a * unit_b + unit_s * unit_c),
            1 - 2 * (unit_a * unit_a + unit_c * unit_c),
            2 * (unit_b * unit_c - unit_s * unit_a),
        ),
        (
            2 * (unit_a * unit_c - unit_s * unit_b),
            2 * (unit_b * unit_c + unit_s * unit_a),
            1 - 2 * (unit_a * unit_a + unit_b * unit_b),
        ),
    )


def kernel(
    log_hbm,
    one_hbm,
    two_hbm,
    points_hbm,
    conf_hbm,
    image_pose_hbm,
    pair_pose_hbm,
    first_local_hbm,
    second_owner_hbm,
    second_local_hbm,
    log_out,
    one_out,
    two_out,
    scale_out,
    scale_ref,
    log_ref,
    one_ref,
    two_ref,
    points_ref,
    conf_ref,
    image_pose,
    pair_pose,
    first_local,
    second_owner,
    second_local,
    conf_f,
    stage_one,
    stage_two,
    codes,
    send_buf,
    recv_buf,
    meta,
    cu_ref,
    prefix_ref,
    weight_sum,
    depth_ref,
    tau_ref,
    hot_ref,
    mask_ref,
    weight_ref,
    inner_ref,
    core_buf,
    chip_buf,
    table_ref,
    table,
    load_sem,
    store_sem,
    table_sem,
    send_sem,
    recv_sem,
    meta_send,
    meta_recv,
    core_send,
    core_recv,
    chip_send,
    chip_recv,
):
    def load(n, src, dst):
        copy = pltpu.make_async_copy(src, dst, load_sem.at[n])
        copy.start()
        return copy

    small = [
        load(0, second_owner_hbm, second_owner),
        load(1, second_local_hbm, second_local),
        load(2, first_local_hbm, first_local),
        load(3, pair_pose_hbm, pair_pose),
        load(4, image_pose_hbm, image_pose),
    ]
    conf_load = load(5, conf_hbm, conf_ref)
    second_load = load(6, points_hbm.at[pl.ds(3, 3)], points_ref.at[pl.ds(3, 3)])
    first_load = load(7, points_hbm.at[pl.ds(0, 3)], points_ref.at[pl.ds(0, 3)])
    log_load = load(8, log_hbm, log_ref)
    state_loads = [load(9, one_hbm, one_ref), load(10, two_hbm, two_ref)]

    my_img = lax.axis_index("img")
    my_pair = lax.axis_index("pair")
    my_y = my_pair // ZS
    my_z = my_pair % ZS

    def pair_at(k, sign):
        return ((my_y + sign * (k // ZS) + YS) % YS) * ZS + (my_z + sign * (k % ZS) + ZS) % ZS

    barrier = pltpu.get_barrier_semaphore()

    my_x = my_img // 2
    my_core = my_img % 2
    my_chip = my_x * OWNERS + my_pair
    xs = [(my_x + d) % XS for d in range(XS)]
    ys = [(my_y + d) % YS for d in range(YS)]
    zs = [(my_z + d) % ZS for d in range(ZS)]
    offsets = [(a, b, c) for a in range(XS) for b in range(YS) for c in range(ZS) if (a, b, c) != (0, 0, 0)]
    offsets.sort(key=lambda o: -sum(min(d, 4 - d) for d in o))

    def greet_chip(k, carry):
        x = (my_x + k // OWNERS) % XS
        y = (my_y + k // ZS) % YS
        z = (my_z + k) % ZS
        pl.semaphore_signal(barrier, 1, device_id=(x * 2 + my_core, y * ZS + z), device_id_type=MESH)
        return carry

    pl.semaphore_signal(barrier, 1, device_id=(my_img + 1 - 2 * my_core, my_pair), device_id_type=MESH)
    lax.fori_loop(1, CHIPS, greet_chip, 0)

    sub = lax.broadcasted_iota(jnp.int32, (8, 128), 0)
    lane = lax.broadcasted_iota(jnp.int32, (8, 128), 1)

    for copy in small:
        copy.wait()

    owners = [second_owner[e] for e in range(PAIR_DEV)]
    order = []
    for e in range(PAIR_DEV):
        rank = jnp.int32(0)
        for other in range(e):
            rank = rank + jnp.where(owners[other] == owners[e], 1, 0)
        order.append(owners[e] * MOST + rank)
    row = jnp.zeros((8, 128), jnp.int32)
    for e in range(PAIR_DEV):
        here = lane == my_pair * PAIR_DEV + e
        row = jnp.where(here & (sub == 0), order[e], row)
        row = jnp.where(here & (sub == 1), second_local[e], row)
    meta[0] = row

    def column(values):
        out = jnp.zeros((8, 128), f32)
        for e in range(PAIR_DEV):
            out = jnp.where(sub == e, values[e], out)
        return out

    pair_cols = [column([pair_pose[i, e] for e in range(PAIR_DEV)]) for i in range(7)]
    pair_rot = rotation(*pair_cols[:4])
    shift = pair_cols[4:]
    firsts = [my_pair * IMG_DEV + first_local[e] for e in range(PAIR_DEV)]
    seconds = [owners[e] * IMG_DEV + second_local[e] for e in range(PAIR_DEV)]
    lean = [2.0 * sum(pair_rot[i][j] * shift[i] for i in range(3)) for j in range(3)]
    shift_sq = sum(shift[i] * shift[i] for i in range(3))
    first_row = (my_img * BAND_ROWS).astype(f32)
    ray_y0 = (first_row + 0.5 - ROWS / 2) / COLS
    ray_x = [((lane + 128 * part).astype(f32) + 0.5 - COLS / 2) / COLS for part in range(4)]

    def widen(step, carry):
        rows = pl.ds(pl.multiple_of(step * 64, 64), 64)
        conf_f[rows, :] = conf_ref[rows, :].astype(f32)
        return carry

    conf_load.wait()
    lax.fori_loop(0, PAIR_DEV * 2 * GROUPS // 64, widen, 0)
    second_load.wait()

    def prepare(view, images, stage, scaled):
        cols = [column([image_pose[i, images[e]] for e in range(PAIR_DEV)]) for i in range(7)]
        rot = rotation(*cols[:4])
        trans = cols[4:]
        both = [[sum(rot[l][i] * pair_rot[l][j] for l in range(3)) for j in range(3)] for i in range(3)]
        moved = [sum(rot[l][i] * shift[l] for l in range(3)) for i in range(3)]
        full = [[both[i][0], both[i][1], both[i][2], moved[i]] for i in range(3)]
        base = [[ray_x[part] * full[0][j] + (full[2][j] + ray_y0 * full[1][j]) for part in range(4)] for j in range(4)]
        slope = [full[1][j] * (1.0 / COLS) for j in range(4)]
        toward = [sum(trans[l] * pair_rot[l][j] for l in range(3)) for j in range(3)]
        offset = sum(trans[l] * shift[l] for l in range(3))

        def body(r, carry):
            total_sq, total_dot, total_conf = carry
            down = r.astype(f32)
            tilt = [slope[j] * down for j in range(4)]
            for part in range(4):
                at = pl.ds(pl.multiple_of(r * COLS + part * 128, 128), 128)
                x = [points_ref[3 * view + j, :, at].astype(f32) for j in range(3)]
                weight = conf_f[pl.ds((r * 4 + part) * 2 + view, 8, stride=2 * GROUPS), :]
                value = base[3][part] + tilt[3]
                for j in range(3):
                    value = value + (base[j][part] + tilt[j]) * x[j]
                if scaled:
                    value = value * weight
                stage[pl.ds(pl.multiple_of((r * 4 + part) * 8, 8), 8), :] = value
                square = x[0] * (x[0] + lean[0]) + x[1] * (x[1] + lean[1]) + x[2] * (x[2] + lean[2])
                dot = x[0] * toward[0] + x[1] * toward[1] + x[2] * toward[2]
                total_sq = total_sq + weight * square
                total_dot = total_dot + weight * dot
                total_conf = total_conf + weight
            return (total_sq, total_dot, total_conf)

        zero = jnp.zeros((8, 128), f32)
        total_sq, total_dot, total_conf = lax.fori_loop(0, BAND_ROWS, body, (zero, zero, zero))
        return (total_sq + total_conf * shift_sq, total_dot + total_conf * offset)

    square_two, dot_two = prepare(1, seconds, stage_two, False)

    def encode(e, carry):
        largest = jnp.full((8, 128), 1e-30, f32)
        for block in range(BLOCKS):
            largest = jnp.maximum(largest, jnp.abs(stage_two[pl.ds(block * 64 + e, 8, stride=8), :]))
        power = jnp.ceil(jnp.log(largest) * (SCALE_STEPS / 0.6931471805599453)).astype(jnp.int32)
        inverse = LEVELS / jnp.exp(power.astype(f32) * (0.6931471805599453 / SCALE_STEPS))
        inverse = jnp.concatenate([inverse, inverse], axis=0)
        for half in range(BLOCKS // 2):
            value = stage_two[pl.ds(half * 128 + e, 16, stride=8), :] * inverse
            value = jnp.floor(value + 0.5).astype(jnp.int32).astype(jnp.int16)
            codes[e, half * 16 : half * 16 + 16, :] = value
            weight = conf_f[pl.ds(e * 2 * GROUPS + half * 32 + 1, 16, stride=2), :] * 128.0
            codes[e, GROUPS + half * 16 : GROUPS + half * 16 + 16, :] = weight.astype(jnp.int32).astype(jnp.int16)
        codes[e, 2 * GROUPS : 2 * GROUPS + 16, :] = jnp.concatenate([power, power], axis=0).astype(jnp.int16)
        return carry

    lax.fori_loop(0, PAIR_DEV, encode, 0)

    def slot_pair(k, j):
        wanted = pair_at(k, 1) * MOST + j
        found = jnp.int32(0)
        for e in range(1, PAIR_DEV):
            found = found + jnp.where(order[e] == wanted, e, 0)
        return found

    for j in range(MOST):
        recv_buf[0, j] = codes[slot_pair(0, j)]

    pl.semaphore_wait(barrier, CHIPS)

    def meta_copy(k):
        return pltpu.make_async_remote_copy(
            src_ref=meta.at[0],
            dst_ref=meta.at[k],
            send_sem=meta_send.at[k],
            recv_sem=meta_recv.at[k],
            device_id=(my_img, pair_at(k, 1)),
            device_id_type=MESH,
        )

    def slot_copy(k):
        return pltpu.make_async_remote_copy(
            src_ref=send_buf.at[k],
            dst_ref=recv_buf.at[k],
            send_sem=send_sem.at[k],
            recv_sem=recv_sem.at[k],
            device_id=(my_img, pair_at(k, 1)),
            device_id_type=MESH,
        )

    def start_meta(k, carry):
        meta_copy(k).start()
        return carry

    def start_slots(k, carry):
        for j in range(MOST):
            send_buf[k, j] = codes[slot_pair(k, j)]
        slot_copy(k).start()
        return carry

    lax.fori_loop(1, OWNERS, start_meta, 0)
    lax.fori_loop(1, OWNERS, start_slots, 0)

    first_load.wait()
    square_one, dot_one = prepare(0, firsts, stage_one, True)

    def depth_of(values):
        return jnp.exp(values.astype(jnp.bfloat16).astype(f32))

    def image_rows(block, v):
        return pl.ds(block * 32 + v, 8, stride=IMG_DEV)

    def block_rows(block):
        return pl.ds(pl.multiple_of(block * 8, 8), 8)

    def first_depth(block, carry):
        for v in range(IMG_DEV):
            depth_ref[v, block_rows(block), :] = depth_of(log_ref[image_rows(block, v), :])
        return carry

    log_load.wait()
    lax.fori_loop(0, BLOCKS, first_depth, 0)
    for copy in state_loads:
        copy.wait()

    own = [[image_pose[i, my_pair * IMG_DEV + min(v, IMG_DEV - 1)] for v in range(8)] for i in range(7)]
    own_cols = [column(own[i]) for i in range(7)]
    own_rot = rotation(*own_cols[:4])
    for i in range(3):
        tau_ref[i] = sum(own_rot[l][i] * own_cols[4 + l] for l in range(3))

    for k in range(1, OWNERS):
        meta_copy(k).wait_recv()
    known = meta[0]
    for k in range(1, OWNERS):
        known = known + meta[k]
    code_row = jnp.broadcast_to(known[0:1], (8, 128))
    local_row = jnp.broadcast_to(known[1:2], (8, 128))
    from_pair = lane // PAIR_DEV
    step_of = ((my_y - from_pair // ZS + YS) % YS) * ZS + (my_z - from_pair % ZS + ZS) % ZS
    slot_of = jnp.where(code_row // MOST == my_pair, step_of * MOST + code_row % MOST, -1)
    local_first = jnp.zeros((8, 128), jnp.int32)
    for e in range(PAIR_DEV):
        local_first = jnp.where(sub == e, first_local[e], local_first)
    own_mask = jnp.where(lane == my_pair * PAIR_DEV + sub, 1.0, 0.0)
    mask_ref[0:8, :] = own_mask
    for v in range(IMG_DEV):
        hot_ref[v, 0:8, :] = jnp.where(local_first == v, 1.0, 0.0)
    for group in range(SLOTS // 8):
        rows = pl.ds(8 + group * 8, 8)
        held = slot_of == sub + group * 8
        mask_ref[rows, :] = jnp.where(held, 1.0, 0.0)
        for v in range(IMG_DEV):
            found = jnp.where(held & (local_row == v), 1.0, 0.0)
            hot_ref[v, rows, :] = jnp.broadcast_to(jnp.sum(found, axis=1, keepdims=True), (8, 128))

    image_row = jnp.zeros((8, 128), jnp.int32)
    for group in range(VIEWS // 8):
        if group == 0:
            image_col = local_first
        else:
            held = (slot_of == sub + (group - 1) * 8).astype(jnp.int32)
            image_col = jnp.sum(held * (local_row - IMG_DEV), axis=1, keepdims=True) + IMG_DEV
        found = jnp.where(lane == sub + group * 8, image_col, 0)
        image_row = image_row + jnp.broadcast_to(jnp.sum(found, axis=0, keepdims=True), (8, 128))
    order_row = jnp.zeros((8, 128), jnp.int32)
    listed = lane < VIEWS
    for group in range(VIEWS // 8):
        view = sub + group * 8
        found = jnp.where(lane == view, image_row, 0)
        image_col = jnp.sum(found, axis=1, keepdims=True)
        before = listed & ((image_row < image_col) | ((image_row == image_col) & (lane < view)))
        place = jnp.sum(before.astype(jnp.int32), axis=1, keepdims=True)
        found = jnp.where(lane == place, view, 0)
        order_row = order_row + jnp.broadcast_to(jnp.sum(found, axis=0, keepdims=True), (8, 128))
    end_row = jnp.zeros((8, 128), jnp.int32)
    for v in range(IMG_DEV):
        upto = (listed & (image_row <= v)).astype(jnp.int32)
        end_row = jnp.where(lane == v, jnp.sum(upto, axis=1, keepdims=True), end_row)
    image_row = jnp.minimum(image_row, IMG_DEV - 1)
    table_ref[...] = jnp.where(sub == 0, image_row, jnp.where(sub == 1, order_row, end_row))
    table_copy = pltpu.make_async_copy(table_ref, table, table_sem)
    table_copy.start()

    def first_copy(e, carry):
        for block in range(BLOCKS):
            cu_ref[e, block * 8 : block * 8 + 8, :] = stage_one[pl.ds(block * 64 + e, 8, stride=8), :]
        return carry

    lax.fori_loop(0, PAIR_DEV, first_copy, 0)
    table_copy.wait()

    def dot_view(r, carry):
        v = table[0, r]
        totals = [jnp.zeros((8, 128), f32) for n in range(PART)]
        for block in range(BLOCKS):
            rows = slice(block * 8, block * 8 + 8)
            totals[block % PART] = totals[block % PART] + cu_ref[r, rows, :] * depth_ref[v, rows, :]
        total = (totals[0] + totals[1]) + (totals[2] + totals[3])
        inner_ref[pl.ds(r, 1), :] = jnp.sum(total, axis=0, keepdims=True)
        return carry

    lax.fori_loop(0, PAIR_DEV, dot_view, 0)

    def first_sums(block, carry):
        sums = [jnp.zeros((8, 128), f32) for v in range(IMG_DEV)]
        for e in range(PAIR_DEV):
            weight = conf_f[pl.ds(e * 2 * GROUPS + block * 16, 8, stride=2), :]
            for v in range(IMG_DEV):
                sums[v] = sums[v] + weight * hot_ref[v, e : e + 1, :]
        for v in range(IMG_DEV):
            weight_sum[v, block_rows(block), :] = sums[v]
        return carry

    lax.fori_loop(0, BLOCKS, first_sums, 0)

    def take(k, carry):
        @pl.when(k > 0)
        def _():
            slot_copy(k).wait_recv()

        units, hots, images = [], [], []
        for j in range(MOST):
            power = recv_buf[k, j, 2 * GROUPS : 2 * GROUPS + 16, :].astype(jnp.int32).astype(f32)
            unit = jnp.exp(power * (0.6931471805599453 / SCALE_STEPS)) * (1.0 / (LEVELS * 128.0))
            units.append(unit)
            slot = PAIR_DEV + k * MOST + j
            hots.append([hot_ref[v, pl.ds(slot, 1), :] * (1.0 / 128.0) for v in range(IMG_DEV)])
            images.append(table[0, slot])

        def part(half, totals):
            totals = list(totals)
            rows = pl.ds(pl.multiple_of(half * 16, 16), 16)
            weight_rows = pl.ds(pl.multiple_of(GROUPS + half * 16, 16), 16)
            sums = [weight_sum[v, rows, :] for v in range(IMG_DEV)]
            for j in range(MOST):
                value = recv_buf[k, j, rows, :].astype(jnp.int32).astype(f32)
                weight = recv_buf[k, j, weight_rows, :].astype(jnp.int32).astype(f32)
                cu = value * units[j] * weight
                cu_ref[PAIR_DEV + k * MOST + j, rows, :] = cu
                totals[j] = totals[j] + cu * depth_ref[images[j], rows, :]
                for v in range(IMG_DEV):
                    sums[v] = sums[v] + weight * hots[j][v]
            for v in range(IMG_DEV):
                weight_sum[v, rows, :] = sums[v]
            return tuple(totals)

        totals = lax.fori_loop(0, BLOCKS // 2, part, tuple(jnp.zeros((16, 128), f32) for j in range(MOST)))
        for j in range(MOST):
            inner_ref[pl.ds(PAIR_DEV + k * MOST + j, 1), :] = jnp.sum(totals[j], axis=0, keepdims=True)
        return carry

    lax.fori_loop(0, OWNERS, take, 0)

    def pair_row(col):
        return jnp.sum(jnp.sum(col, axis=1, keepdims=True) * own_mask, axis=0, keepdims=True)

    fixed_row = pair_row(dot_one + dot_two)
    square_row = pair_row(square_one + square_two)

    def core_copy(t):
        return pltpu.make_async_remote_copy(
            src_ref=core_buf.at[t, 0],
            dst_ref=core_buf.at[t, 1],
            send_sem=core_send.at[t],
            recv_sem=core_recv.at[t],
            device_id=(my_img + 1 - 2 * my_core, my_pair),
            device_id_type=MESH,
        )

    def chip_copy(t, n, arrival):
        a, b, c = offsets[n]
        pair = ys[b] * ZS + zs[c]
        place = xs[a] * OWNERS + pair if arrival else my_chip
        return pltpu.make_async_remote_copy(
            src_ref=chip_buf.at[t, place],
            dst_ref=chip_buf.at[t, place],
            send_sem=chip_send.at[t, n],
            recv_sem=chip_recv.at[t, place],
            device_id=(xs[a] * 2 + my_core, pair),
            device_id_type=MESH,
        )

    def sum_all(t, tile):
        core_buf[t, 0] = tile
        core_copy(t).start()
        core_copy(t).wait_recv()
        chip_buf[t, my_chip] = tile + core_buf[t, 1]
        for n in range(CHIPS - 1):
            chip_copy(t, n, False).start()
        for n in reversed(range(CHIPS - 1)):
            chip_copy(t, n, True).wait_recv()
        parts = [chip_buf[t, n] for n in range(CHIPS)]
        while len(parts) > 1:
            parts = [parts[n] + parts[n + 1] for n in range(0, len(parts), 2)]
        return parts[0]

    def stores(tile_id):
        rows = pl.ds(pl.multiple_of(tile_id * TILE * 32, 8), TILE * 32)
        pairs = [(log_ref, log_out), (one_ref, one_out), (two_ref, two_out)]
        return [
            pltpu.make_async_copy(a.at[rows], b.at[rows], store_sem.at[tile_id, n])
            for n, (a, b) in enumerate(pairs)
        ]

    scale_store = pltpu.make_async_copy(scale_ref, scale_out, load_sem.at[0])
    denominator = None
    for sweep in range(ITERS):
        row = jnp.zeros((8, 128), f32)
        for group in range(VIEWS // 8):
            rows = slice(group * 8, group * 8 + 8)
            row = row + jnp.sum(inner_ref[rows, :], axis=1, keepdims=True) * mask_ref[rows, :]
        row = jnp.sum(row, axis=0, keepdims=True) + fixed_row
        two = lax.broadcasted_iota(jnp.int32, (2, 128), 0)
        total = sum_all(sweep, jnp.where(two == 0, row, square_row))
        if sweep == 0:
            denominator = total[1:2]
        scales = jnp.broadcast_to(total[0:1] / denominator, (8, 128))
        for group in range(VIEWS // 8):
            rows = slice(group * 8, group * 8 + 8)
            held = jnp.sum(scales * mask_ref[rows, :], axis=1, keepdims=True)
            if group == 0 and sweep == ITERS - 1:
                own_row = jnp.sum(jnp.where(lane == sub, held, 0.0), axis=0, keepdims=True)
                scale_ref[...] = own_row[:, 0:PAIR_DEV]
                scale_store.start()
            weight_ref[rows, :] = jnp.broadcast_to(held, (8, 128))

        steps = START + sweep + 1
        bias_one = 1 - beta_one**steps
        bias_two = 1 - beta_two**steps
        last = sweep == ITERS - 1

        def update(tile_id, carry):
            start = tile_id * TILE

            def gather(step, sums):
                sums = list(sums)
                for n in range(UNROLL):
                    q = step * UNROLL + n
                    r = table[1, q]
                    weight = weight_ref[pl.ds(r, 1), :]
                    for m in range(TILE):
                        sums[m] = sums[m] + cu_ref[r, block_rows(start + m), :] * weight
                        prefix_ref[q + 1, m * 8 : m * 8 + 8, :] = sums[m]
                return tuple(sums)

            zero = jnp.zeros((8, 128), f32)
            for m in range(TILE):
                prefix_ref[0, m * 8 : m * 8 + 8, :] = zero
            lax.fori_loop(0, VIEWS // UNROLL, gather, (zero,) * TILE)
            def step_adam(n, carry):
                block = start + n
                here = pl.ds(pl.multiple_of(n * 8, 8), 8)
                down = (block * 2 + sub // 4).astype(f32) + first_row
                rays_y = (down + 0.5 - ROWS / 2) / COLS
                rays_x = (((sub % 4) * 128 + lane).astype(f32) + 0.5 - COLS / 2) / COLS
                length = rays_x * rays_x + rays_y * rays_y + 1.0
                for v in range(IMG_DEV):
                    depth = depth_ref[v, block_rows(block), :]
                    lever = rays_x * tau_ref[0, v : v + 1, :] + rays_y * tau_ref[1, v : v + 1, :] + tau_ref[2, v : v + 1, :]
                    gathered = prefix_ref[table[2, v], here, :]
                    if v > 0:
                        gathered = gathered - prefix_ref[table[2, v - 1], here, :]
                    pull = (depth * length + lever) * weight_sum[v, block_rows(block), :] - gathered
                    gradient = 2.0 * depth * pull
                    rows = image_rows(block, v)
                    old_one = one_ref[rows, :]
                    old_two = two_ref[rows, :]
                    old_log = log_ref[rows, :]
                    new_one = beta_one * old_one + (1 - beta_one) * gradient
                    new_two = beta_two * old_two + (1 - beta_two) * gradient * gradient
                    corrected_one = new_one * (1 / bias_one)
                    corrected_two = new_two * (1 / bias_two)
                    new_log = old_log - learn_rate * corrected_one / (jnp.sqrt(corrected_two) + adam_eps)
                    one_ref[rows, :] = new_one
                    two_ref[rows, :] = new_two
                    log_ref[rows, :] = new_log
                    if not last:
                        depth_ref[v, block_rows(block), :] = depth_of(new_log)
                return carry

            lax.fori_loop(0, TILE, step_adam, 0)
            if last:
                for copy in stores(tile_id):
                    copy.start()
            return carry

        lax.fori_loop(0, BLOCKS // TILE, update, 0)
        if not last:
            lax.fori_loop(0, VIEWS, dot_view, 0)

    scale_store.wait()
    for tile_id in range(BLOCKS // TILE):
        for copy in stores(tile_id):
            copy.wait()

    def finish(k, carry):
        meta_copy(k).wait_send()
        slot_copy(k).wait_send()
        return carry

    lax.fori_loop(1, OWNERS, finish, 0)
    for t in range(ITERS):
        core_copy(t).wait_send()
        for n in range(CHIPS - 1):
            chip_copy(t, n, False).wait_send()


def store(log_ref, one_ref, two_ref, scale_ref, log_out, one_out, two_out, scale_out, sem):
    copies = [
        pltpu.make_async_copy(log_ref, log_out, sem.at[0]),
        pltpu.make_async_copy(one_ref, one_out, sem.at[1]),
        pltpu.make_async_copy(two_ref, two_out, sem.at[2]),
        pltpu.make_async_copy(scale_ref, scale_out, sem.at[3]),
    ]
    for copy in copies:
        copy.start()
    for copy in copies:
        copy.wait()


def shards(
    log_depth,
    moment_one,
    moment_two,
    image_pose,
    pair_points,
    confidence,
    pair_pose,
    first_local,
    second_owner,
    second_local,
):
    def fold(a):
        return a.reshape(IMG_DEV, GROUPS, 128).transpose(1, 0, 2).reshape(GROUPS * IMG_DEV, 128)

    def unfold(a):
        return a.reshape(GROUPS, IMG_DEV, 128).transpose(1, 0, 2).reshape(IMG_DEV, BAND)

    points = pair_points.transpose(1, 0, 2)
    conf = confidence.reshape(PAIR_DEV, 2, GROUPS, 128).transpose(0, 2, 1, 3).reshape(PAIR_DEV * GROUPS * 2, 128)
    hbm = pl.BlockSpec(memory_space=pltpu.HBM)
    band = jax.ShapeDtypeStruct((GROUPS * IMG_DEV, 128), f32)
    dma = pltpu.SemaphoreType.DMA
    out = pl.pallas_call(
        kernel,
        out_shape=(band, band, band, jax.ShapeDtypeStruct((1, PAIR_DEV), f32)),
        in_specs=[hbm] * 10,
        out_specs=(hbm,) * 4,
        scratch_shapes=[
            pltpu.VMEM((1, PAIR_DEV), f32),
            pltpu.VMEM((GROUPS * IMG_DEV, 128), f32),
            pltpu.VMEM((GROUPS * IMG_DEV, 128), f32),
            pltpu.VMEM((GROUPS * IMG_DEV, 128), f32),
            pltpu.VMEM((6, PAIR_DEV, BAND), jnp.bfloat16),
            pltpu.VMEM((PAIR_DEV * GROUPS * 2, 128), jnp.bfloat16),
            pltpu.SMEM((7, IMG_DEV * OWNERS), f32),
            pltpu.SMEM((7, PAIR_DEV), f32),
            pltpu.SMEM((PAIR_DEV,), jnp.int32),
            pltpu.SMEM((PAIR_DEV,), jnp.int32),
            pltpu.SMEM((PAIR_DEV,), jnp.int32),
            pltpu.VMEM((PAIR_DEV * GROUPS * 2, 128), f32),
            pltpu.VMEM((PAIR_DEV * GROUPS, 128), f32),
            pltpu.VMEM((PAIR_DEV * GROUPS, 128), f32),
            pltpu.VMEM((PAIR_DEV, CODE_ROWS, 128), jnp.int16),
            pltpu.VMEM((OWNERS, MOST, CODE_ROWS, 128), jnp.int16),
            pltpu.VMEM((OWNERS, MOST, CODE_ROWS, 128), jnp.int16),
            pltpu.VMEM((OWNERS, 8, 128), jnp.int32),
            pltpu.VMEM((VIEWS, GROUPS, 128), f32),
            pltpu.VMEM((VIEWS + 1, TILE * 8, 128), f32),
            pltpu.VMEM((IMG_DEV, GROUPS, 128), f32),
            pltpu.VMEM((IMG_DEV, GROUPS, 128), f32),
            pltpu.VMEM((3, 8, 128), f32),
            pltpu.VMEM((IMG_DEV, VIEWS, 128), f32),
            pltpu.VMEM((VIEWS, 128), f32),
            pltpu.VMEM((VIEWS, 128), f32),
            pltpu.VMEM((VIEWS, 128), f32),
            pltpu.VMEM((ITERS, 2, 2, 128), f32),
            pltpu.VMEM((ITERS, CHIPS, 2, 128), f32),
            pltpu.VMEM((8, 128), jnp.int32),
            pltpu.SMEM((8, 128), jnp.int32),
            dma((11,)),
            dma((BLOCKS // TILE, 3)),
            dma,
            dma((OWNERS,)),
            dma((OWNERS,)),
            dma((OWNERS,)),
            dma((OWNERS,)),
            dma((ITERS,)),
            dma((ITERS,)),
            dma((ITERS, CHIPS)),
            dma((ITERS, CHIPS)),
        ],
        compiler_params=pltpu.CompilerParams(
            collective_id=0, has_side_effects=True, vmem_limit_bytes=60 * 2**20
        ),
        name="align",
    )(
        fold(log_depth),
        fold(moment_one),
        fold(moment_two),
        points,
        conf,
        image_pose,
        pair_pose,
        first_local,
        second_owner.reshape(PAIR_DEV),
        second_local,
    )
    out = pl.pallas_call(
        store,
        out_shape=(band, band, band, jax.ShapeDtypeStruct((1, PAIR_DEV), f32)),
        in_specs=[hbm] * 4,
        out_specs=(hbm,) * 4,
        scratch_shapes=[dma((4,))],
        compiler_params=pltpu.CompilerParams(vmem_limit_bytes=60 * 2**20),
        name="store",
    )(*out)
    return (unfold(out[0]), unfold(out[1]), unfold(out[2]), out[3].reshape(PAIR_DEV))


def solution(mesh):
    return jax.shard_map(
        shards,
        mesh=mesh,
        in_specs=(
            P("pair", "img"),
            P("pair", "img"),
            P("pair", "img"),
            P(),
            P("pair", None, "img"),
            P("pair", None, "img"),
            P(None, "pair"),
            P("pair"),
            P("pair", None),
            P("pair"),
        ),
        out_specs=(P("pair", "img"), P("pair", "img"), P("pair", "img"), P("pair")),
        check_vma=False,
    )
```

```python
import jax
import jax.numpy as jnp
from jax import lax
from jax.experimental import pallas as pl
from jax.experimental.pallas import tpu as pltpu
from jax.sharding import PartitionSpec as P

ROWS = 384
COLS = 512
ITERS = 3
START = 100
IMG_DEV = 4
PAIR_DEV = 8
MOST = 2
IMGS = 8
OWNERS = 16
XS = 4
YS = 4
ZS = 4
CHIPS = XS * YS * ZS
BAND = ROWS * COLS // IMGS
GROUPS = BAND // 128
BLOCKS = GROUPS // 8
BAND_ROWS = ROWS // IMGS
SLOTS = OWNERS * MOST
VIEWS = PAIR_DEV + SLOTS
CODE_ROWS = 2 * GROUPS + 16
TILE = 12
PART = 4
UNROLL = 4
LEVELS = 32700.0
SCALE_STEPS = 64.0

beta_one = 0.9
beta_two = 0.999
learn_rate = 0.01
adam_eps = 1e-08
f32 = jnp.float32
MESH = pl.DeviceIdType.MESH


def rotation(scalar_q, vec_a, vec_b, vec_c):
    magnitude = jnp.sqrt(scalar_q * scalar_q + vec_a * vec_a + vec_b * vec_b + vec_c * vec_c)
    unit_s = scalar_q / magnitude
    unit_a = vec_a / magnitude
    unit_b = vec_b / magnitude
    unit_c = vec_c / magnitude
    return (
        (
            1 - 2 * (unit_b * unit_b + unit_c * unit_c),
            2 * (unit_a * unit_b - unit_s * unit_c),
            2 * (unit_a * unit_c + unit_s * unit_b),
        ),
        (
            2 * (unit_a * unit_b + unit_s * unit_c),
            1 - 2 * (unit_a * unit_a + unit_c * unit_c),
            2 * (unit_b * unit_c - unit_s * unit_a),
        ),
        (
            2 * (unit_a * unit_c - unit_s * unit_b),
            2 * (unit_b * unit_c + unit_s * unit_a),
            1 - 2 * (unit_a * unit_a + unit_b * unit_b),
        ),
    )


def kernel(
    log_hbm,
    one_hbm,
    two_hbm,
    points_hbm,
    conf_hbm,
    image_pose_hbm,
    pair_pose_hbm,
    first_local_hbm,
    second_owner_hbm,
    second_local_hbm,
    log_out,
    one_out,
    two_out,
    scale_out,
    scale_ref,
    log_ref,
    one_ref,
    two_ref,
    points_ref,
    conf_ref,
    image_pose,
    pair_pose,
    first_local,
    second_owner,
    second_local,
    conf_f,
    stage_one,
    stage_two,
    codes,
    send_buf,
    recv_buf,
    meta,
    cu_ref,
    prefix_ref,
    weight_sum,
    depth_ref,
    tau_ref,
    hot_ref,
    mask_ref,
    weight_ref,
    inner_ref,
    core_buf,
    chip_buf,
    table_ref,
    table,
    load_sem,
    store_sem,
    table_sem,
    send_sem,
    recv_sem,
    meta_send,
    meta_recv,
    core_send,
    core_recv,
    chip_send,
    chip_recv,
):
    def load(n, src, dst):
        copy = pltpu.make_async_copy(src, dst, load_sem.at[n])
        copy.start()
        return copy

    small = [
        load(0, second_owner_hbm, second_owner),
        load(1, second_local_hbm, second_local),
        load(2, first_local_hbm, first_local),
        load(3, pair_pose_hbm, pair_pose),
        load(4, image_pose_hbm, image_pose),
    ]
    conf_load = load(5, conf_hbm, conf_ref)
    second_load = load(6, points_hbm.at[pl.ds(3, 3)], points_ref.at[pl.ds(3, 3)])
    first_load = load(7, points_hbm.at[pl.ds(0, 3)], points_ref.at[pl.ds(0, 3)])
    log_load = load(8, log_hbm, log_ref)
    state_loads = [load(9, one_hbm, one_ref), load(10, two_hbm, two_ref)]

    my_img = lax.axis_index("img")
    my_pair = lax.axis_index("pair")
    my_y = my_pair // ZS
    my_z = my_pair % ZS

    def pair_at(k, sign):
        return ((my_y + sign * (k // ZS) + YS) % YS) * ZS + (my_z + sign * (k % ZS) + ZS) % ZS

    barrier = pltpu.get_barrier_semaphore()

    my_x = my_img // 2
    my_core = my_img % 2
    my_chip = my_x * OWNERS + my_pair
    xs = [(my_x + d) % XS for d in range(XS)]
    ys = [(my_y + d) % YS for d in range(YS)]
    zs = [(my_z + d) % ZS for d in range(ZS)]
    offsets = [(a, b, c) for a in range(XS) for b in range(YS) for c in range(ZS) if (a, b, c) != (0, 0, 0)]
    offsets.sort(key=lambda o: -sum(min(d, 4 - d) for d in o))

    def greet_chip(k, carry):
        x = (my_x + k // OWNERS) % XS
        y = (my_y + k // ZS) % YS
        z = (my_z + k) % ZS
        pl.semaphore_signal(barrier, 1, device_id=(x * 2 + my_core, y * ZS + z), device_id_type=MESH)
        return carry

    pl.semaphore_signal(barrier, 1, device_id=(my_img + 1 - 2 * my_core, my_pair), device_id_type=MESH)
    lax.fori_loop(1, CHIPS, greet_chip, 0)

    sub = lax.broadcasted_iota(jnp.int32, (8, 128), 0)
    lane = lax.broadcasted_iota(jnp.int32, (8, 128), 1)

    for copy in small:
        copy.wait()

    owners = [second_owner[e] for e in range(PAIR_DEV)]
    order = []
    for e in range(PAIR_DEV):
        rank = jnp.int32(0)
        for other in range(e):
            rank = rank + jnp.where(owners[other] == owners[e], 1, 0)
        order.append(owners[e] * MOST + rank)
    row = jnp.zeros((8, 128), jnp.int32)
    for e in range(PAIR_DEV):
        here = lane == my_pair * PAIR_DEV + e
        row = jnp.where(here & (sub == 0), order[e], row)
        row = jnp.where(here & (sub == 1), second_local[e], row)
    meta[0] = row

    def column(values):
        out = jnp.zeros((8, 128), f32)
        for e in range(PAIR_DEV):
            out = jnp.where(sub == e, values[e], out)
        return out

    pair_cols = [column([pair_pose[i, e] for e in range(PAIR_DEV)]) for i in range(7)]
    pair_rot = rotation(*pair_cols[:4])
    shift = pair_cols[4:]
    firsts = [my_pair * IMG_DEV + first_local[e] for e in range(PAIR_DEV)]
    seconds = [owners[e] * IMG_DEV + second_local[e] for e in range(PAIR_DEV)]
    lean = [2.0 * sum(pair_rot[i][j] * shift[i] for i in range(3)) for j in range(3)]
    shift_sq = sum(shift[i] * shift[i] for i in range(3))
    first_row = (my_img * BAND_ROWS).astype(f32)
    ray_y0 = (first_row + 0.5 - ROWS / 2) / COLS
    ray_x = [((lane + 128 * part).astype(f32) + 0.5 - COLS / 2) / COLS for part in range(4)]

    def widen(step, carry):
        rows = pl.ds(pl.multiple_of(step * 64, 64), 64)
        conf_f[rows, :] = conf_ref[rows, :].astype(f32)
        return carry

    conf_load.wait()
    lax.fori_loop(0, PAIR_DEV * 2 * GROUPS // 64, widen, 0)
    second_load.wait()

    def prepare(view, images, stage, scaled):
        cols = [column([image_pose[i, images[e]] for e in range(PAIR_DEV)]) for i in range(7)]
        rot = rotation(*cols[:4])
        trans = cols[4:]
        both = [[sum(rot[l][i] * pair_rot[l][j] for l in range(3)) for j in range(3)] for i in range(3)]
        moved = [sum(rot[l][i] * shift[l] for l in range(3)) for i in range(3)]
        full = [[both[i][0], both[i][1], both[i][2], moved[i]] for i in range(3)]
        base = [[ray_x[part] * full[0][j] + (full[2][j] + ray_y0 * full[1][j]) for part in range(4)] for j in range(4)]
        slope = [full[1][j] * (1.0 / COLS) for j in range(4)]
        toward = [sum(trans[l] * pair_rot[l][j] for l in range(3)) for j in range(3)]
        offset = sum(trans[l] * shift[l] for l in range(3))

        def body(r, carry):
            total_sq, total_dot, total_conf = carry
            down = r.astype(f32)
            tilt = [slope[j] * down for j in range(4)]
            for part in range(4):
                at = pl.ds(pl.multiple_of(r * COLS + part * 128, 128), 128)
                x = [points_ref[3 * view + j, :, at].astype(f32) for j in range(3)]
                weight = conf_f[pl.ds((r * 4 + part) * 2 + view, 8, stride=2 * GROUPS), :]
                value = base[3][part] + tilt[3]
                for j in range(3):
                    value = value + (base[j][part] + tilt[j]) * x[j]
                if scaled:
                    value = value * weight
                stage[pl.ds(pl.multiple_of((r * 4 + part) * 8, 8), 8), :] = value
                square = x[0] * (x[0] + lean[0]) + x[1] * (x[1] + lean[1]) + x[2] * (x[2] + lean[2])
                dot = x[0] * toward[0] + x[1] * toward[1] + x[2] * toward[2]
                total_sq = total_sq + weight * square
                total_dot = total_dot + weight * dot
                total_conf = total_conf + weight
            return (total_sq, total_dot, total_conf)

        zero = jnp.zeros((8, 128), f32)
        total_sq, total_dot, total_conf = lax.fori_loop(0, BAND_ROWS, body, (zero, zero, zero))
        return (total_sq + total_conf * shift_sq, total_dot + total_conf * offset)

    square_two, dot_two = prepare(1, seconds, stage_two, False)

    def encode(e, carry):
        largest = jnp.full((8, 128), 1e-30, f32)
        for block in range(BLOCKS):
            largest = jnp.maximum(largest, jnp.abs(stage_two[pl.ds(block * 64 + e, 8, stride=8), :]))
        power = jnp.ceil(jnp.log(largest) * (SCALE_STEPS / 0.6931471805599453)).astype(jnp.int32)
        inverse = LEVELS / jnp.exp(power.astype(f32) * (0.6931471805599453 / SCALE_STEPS))
        inverse = jnp.concatenate([inverse, inverse], axis=0)
        for half in range(BLOCKS // 2):
            value = stage_two[pl.ds(half * 128 + e, 16, stride=8), :] * inverse
            value = jnp.floor(value + 0.5).astype(jnp.int32).astype(jnp.int16)
            codes[e, half * 16 : half * 16 + 16, :] = value
            weight = conf_f[pl.ds(e * 2 * GROUPS + half * 32 + 1, 16, stride=2), :] * 128.0
            codes[e, GROUPS + half * 16 : GROUPS + half * 16 + 16, :] = weight.astype(jnp.int32).astype(jnp.int16)
        codes[e, 2 * GROUPS : 2 * GROUPS + 16, :] = jnp.concatenate([power, power], axis=0).astype(jnp.int16)
        return carry

    lax.fori_loop(0, PAIR_DEV, encode, 0)

    def slot_pair(k, j):
        wanted = pair_at(k, 1) * MOST + j
        found = jnp.int32(0)
        for e in range(1, PAIR_DEV):
            found = found + jnp.where(order[e] == wanted, e, 0)
        return found

    for j in range(MOST):
        recv_buf[0, j] = codes[slot_pair(0, j)]

    pl.semaphore_wait(barrier, CHIPS)

    def meta_copy(k):
        return pltpu.make_async_remote_copy(
            src_ref=meta.at[0],
            dst_ref=meta.at[k],
            send_sem=meta_send.at[k],
            recv_sem=meta_recv.at[k],
            device_id=(my_img, pair_at(k, 1)),
            device_id_type=MESH,
        )

    def slot_copy(k):
        return pltpu.make_async_remote_copy(
            src_ref=send_buf.at[k],
            dst_ref=recv_buf.at[k],
            send_sem=send_sem.at[k],
            recv_sem=recv_sem.at[k],
            device_id=(my_img, pair_at(k, 1)),
            device_id_type=MESH,
        )

    def start_meta(k, carry):
        meta_copy(k).start()
        return carry

    def start_slots(k, carry):
        for j in range(MOST):
            send_buf[k, j] = codes[slot_pair(k, j)]
        slot_copy(k).start()
        return carry

    lax.fori_loop(1, OWNERS, start_meta, 0)
    lax.fori_loop(1, OWNERS, start_slots, 0)

    first_load.wait()
    square_one, dot_one = prepare(0, firsts, stage_one, True)

    def depth_of(values):
        return jnp.exp(values.astype(jnp.bfloat16).astype(f32))

    def image_rows(block, v):
        return pl.ds(block * 32 + v, 8, stride=IMG_DEV)

    def block_rows(block):
        return pl.ds(pl.multiple_of(block * 8, 8), 8)

    def first_depth(block, carry):
        for v in range(IMG_DEV):
            depth_ref[v, block_rows(block), :] = depth_of(log_ref[image_rows(block, v), :])
        return carry

    log_load.wait()
    lax.fori_loop(0, BLOCKS, first_depth, 0)
    for copy in state_loads:
        copy.wait()

    own = [[image_pose[i, my_pair * IMG_DEV + min(v, IMG_DEV - 1)] for v in range(8)] for i in range(7)]
    own_cols = [column(own[i]) for i in range(7)]
    own_rot = rotation(*own_cols[:4])
    for i in range(3):
        tau_ref[i] = sum(own_rot[l][i] * own_cols[4 + l] for l in range(3))

    for k in range(1, OWNERS):
        meta_copy(k).wait_recv()
    known = meta[0]
    for k in range(1, OWNERS):
        known = known + meta[k]
    code_row = jnp.broadcast_to(known[0:1], (8, 128))
    local_row = jnp.broadcast_to(known[1:2], (8, 128))
    from_pair = lane // PAIR_DEV
    step_of = ((my_y - from_pair // ZS + YS) % YS) * ZS + (my_z - from_pair % ZS + ZS) % ZS
    slot_of = jnp.where(code_row // MOST == my_pair, step_of * MOST + code_row % MOST, -1)
    local_first = jnp.zeros((8, 128), jnp.int32)
    for e in range(PAIR_DEV):
        local_first = jnp.where(sub == e, first_local[e], local_first)
    own_mask = jnp.where(lane == my_pair * PAIR_DEV + sub, 1.0, 0.0)
    mask_ref[0:8, :] = own_mask
    for v in range(IMG_DEV):
        hot_ref[v, 0:8, :] = jnp.where(local_first == v, 1.0, 0.0)
    for group in range(SLOTS // 8):
        rows = pl.ds(8 + group * 8, 8)
        held = slot_of == sub + group * 8
        mask_ref[rows, :] = jnp.where(held, 1.0, 0.0)
        for v in range(IMG_DEV):
            found = jnp.where(held & (local_row == v), 1.0, 0.0)
            hot_ref[v, rows, :] = jnp.broadcast_to(jnp.sum(found, axis=1, keepdims=True), (8, 128))

    image_row = jnp.zeros((8, 128), jnp.int32)
    for group in range(VIEWS // 8):
        if group == 0:
            image_col = local_first
        else:
            held = (slot_of == sub + (group - 1) * 8).astype(jnp.int32)
            image_col = jnp.sum(held * (local_row - IMG_DEV), axis=1, keepdims=True) + IMG_DEV
        found = jnp.where(lane == sub + group * 8, image_col, 0)
        image_row = image_row + jnp.broadcast_to(jnp.sum(found, axis=0, keepdims=True), (8, 128))
    order_row = jnp.zeros((8, 128), jnp.int32)
    listed = lane < VIEWS
    for group in range(VIEWS // 8):
        view = sub + group * 8
        found = jnp.where(lane == view, image_row, 0)
        image_col = jnp.sum(found, axis=1, keepdims=True)
        before = listed & ((image_row < image_col) | ((image_row == image_col) & (lane < view)))
        place = jnp.sum(before.astype(jnp.int32), axis=1, keepdims=True)
        found = jnp.where(lane == place, view, 0)
        order_row = order_row + jnp.broadcast_to(jnp.sum(found, axis=0, keepdims=True), (8, 128))
    end_row = jnp.zeros((8, 128), jnp.int32)
    for v in range(IMG_DEV):
        upto = (listed & (image_row <= v)).astype(jnp.int32)
        end_row = jnp.where(lane == v, jnp.sum(upto, axis=1, keepdims=True), end_row)
    image_row = jnp.minimum(image_row, IMG_DEV - 1)
    table_ref[...] = jnp.where(sub == 0, image_row, jnp.where(sub == 1, order_row, end_row))
    table_copy = pltpu.make_async_copy(table_ref, table, table_sem)
    table_copy.start()

    def first_copy(e, carry):
        for block in range(BLOCKS):
            cu_ref[e, block * 8 : block * 8 + 8, :] = stage_one[pl.ds(block * 64 + e, 8, stride=8), :]
        return carry

    lax.fori_loop(0, PAIR_DEV, first_copy, 0)
    table_copy.wait()

    def dot_view(r, carry):
        v = table[0, r]
        totals = [jnp.zeros((8, 128), f32) for n in range(PART)]
        for block in range(BLOCKS):
            rows = slice(block * 8, block * 8 + 8)
            totals[block % PART] = totals[block % PART] + cu_ref[r, rows, :] * depth_ref[v, rows, :]
        total = (totals[0] + totals[1]) + (totals[2] + totals[3])
        inner_ref[pl.ds(r, 1), :] = jnp.sum(total, axis=0, keepdims=True)
        return carry

    lax.fori_loop(0, PAIR_DEV, dot_view, 0)

    def first_sums(block, carry):
        sums = [jnp.zeros((8, 128), f32) for v in range(IMG_DEV)]
        for e in range(PAIR_DEV):
            weight = conf_f[pl.ds(e * 2 * GROUPS + block * 16, 8, stride=2), :]
            for v in range(IMG_DEV):
                sums[v] = sums[v] + weight * hot_ref[v, e : e + 1, :]
        for v in range(IMG_DEV):
            weight_sum[v, block_rows(block), :] = sums[v]
        return carry

    lax.fori_loop(0, BLOCKS, first_sums, 0)

    def take(k, carry):
        @pl.when(k > 0)
        def _():
            slot_copy(k).wait_recv()

        units, hots, images = [], [], []
        for j in range(MOST):
            power = recv_buf[k, j, 2 * GROUPS : 2 * GROUPS + 16, :].astype(jnp.int32).astype(f32)
            unit = jnp.exp(power * (0.6931471805599453 / SCALE_STEPS)) * (1.0 / (LEVELS * 128.0))
            units.append(unit)
            slot = PAIR_DEV + k * MOST + j
            hots.append([hot_ref[v, pl.ds(slot, 1), :] * (1.0 / 128.0) for v in range(IMG_DEV)])
            images.append(table[0, slot])

        def part(half, totals):
            totals = list(totals)
            rows = pl.ds(pl.multiple_of(half * 16, 16), 16)
            weight_rows = pl.ds(pl.multiple_of(GROUPS + half * 16, 16), 16)
            sums = [weight_sum[v, rows, :] for v in range(IMG_DEV)]
            for j in range(MOST):
                value = recv_buf[k, j, rows, :].astype(jnp.int32).astype(f32)
                weight = recv_buf[k, j, weight_rows, :].astype(jnp.int32).astype(f32)
                cu = value * units[j] * weight
                cu_ref[PAIR_DEV + k * MOST + j, rows, :] = cu
                totals[j] = totals[j] + cu * depth_ref[images[j], rows, :]
                for v in range(IMG_DEV):
                    sums[v] = sums[v] + weight * hots[j][v]
            for v in range(IMG_DEV):
                weight_sum[v, rows, :] = sums[v]
            return tuple(totals)

        totals = lax.fori_loop(0, BLOCKS // 2, part, tuple(jnp.zeros((16, 128), f32) for j in range(MOST)))
        for j in range(MOST):
            inner_ref[pl.ds(PAIR_DEV + k * MOST + j, 1), :] = jnp.sum(totals[j], axis=0, keepdims=True)
        return carry

    lax.fori_loop(0, OWNERS, take, 0)

    def pair_row(col):
        return jnp.sum(jnp.sum(col, axis=1, keepdims=True) * own_mask, axis=0, keepdims=True)

    fixed_row = pair_row(dot_one + dot_two)
    square_row = pair_row(square_one + square_two)

    def core_copy(t):
        return pltpu.make_async_remote_copy(
            src_ref=core_buf.at[t, 0],
            dst_ref=core_buf.at[t, 1],
            send_sem=core_send.at[t],
            recv_sem=core_recv.at[t],
            device_id=(my_img + 1 - 2 * my_core, my_pair),
            device_id_type=MESH,
        )

    def chip_copy(t, n, arrival):
        a, b, c = offsets[n]
        pair = ys[b] * ZS + zs[c]
        place = xs[a] * OWNERS + pair if arrival else my_chip
        return pltpu.make_async_remote_copy(
            src_ref=chip_buf.at[t, place],
            dst_ref=chip_buf.at[t, place],
            send_sem=chip_send.at[t, n],
            recv_sem=chip_recv.at[t, place],
            device_id=(xs[a] * 2 + my_core, pair),
            device_id_type=MESH,
        )

    def sum_all(t, tile):
        core_buf[t, 0] = tile
        core_copy(t).start()
        core_copy(t).wait_recv()
        chip_buf[t, my_chip] = tile + core_buf[t, 1]
        for n in range(CHIPS - 1):
            chip_copy(t, n, False).start()
        for n in reversed(range(CHIPS - 1)):
            chip_copy(t, n, True).wait_recv()
        parts = [chip_buf[t, n] for n in range(CHIPS)]
        while len(parts) > 1:
            parts = [parts[n] + parts[n + 1] for n in range(0, len(parts), 2)]
        return parts[0]

    def stores(tile_id):
        rows = pl.ds(pl.multiple_of(tile_id * TILE * 32, 8), TILE * 32)
        pairs = [(log_ref, log_out), (one_ref, one_out), (two_ref, two_out)]
        return [
            pltpu.make_async_copy(a.at[rows], b.at[rows], store_sem.at[tile_id, n])
            for n, (a, b) in enumerate(pairs)
        ]

    scale_store = pltpu.make_async_copy(scale_ref, scale_out, load_sem.at[0])
    denominator = None
    for sweep in range(ITERS):
        row = jnp.zeros((8, 128), f32)
        for group in range(VIEWS // 8):
            rows = slice(group * 8, group * 8 + 8)
            row = row + jnp.sum(inner_ref[rows, :], axis=1, keepdims=True) * mask_ref[rows, :]
        row = jnp.sum(row, axis=0, keepdims=True) + fixed_row
        two = lax.broadcasted_iota(jnp.int32, (2, 128), 0)
        total = sum_all(sweep, jnp.where(two == 0, row, square_row))
        if sweep == 0:
            denominator = total[1:2]
        scales = jnp.broadcast_to(total[0:1] / denominator, (8, 128))
        for group in range(VIEWS // 8):
            rows = slice(group * 8, group * 8 + 8)
            held = jnp.sum(scales * mask_ref[rows, :], axis=1, keepdims=True)
            if group == 0 and sweep == ITERS - 1:
                own_row = jnp.sum(jnp.where(lane == sub, held, 0.0), axis=0, keepdims=True)
                scale_ref[...] = own_row[:, 0:PAIR_DEV]
                scale_store.start()
            weight_ref[rows, :] = jnp.broadcast_to(held, (8, 128))

        steps = START + sweep + 1
        bias_one = 1 - beta_one**steps
        bias_two = 1 - beta_two**steps
        last = sweep == ITERS - 1

        def update(tile_id, carry):
            start = tile_id * TILE

            def gather(step, sums):
                sums = list(sums)
                for n in range(UNROLL):
                    q = step * UNROLL + n
                    r = table[1, q]
                    weight = weight_ref[pl.ds(r, 1), :]
                    for m in range(TILE):
                        sums[m] = sums[m] + cu_ref[r, block_rows(start + m), :] * weight
                        prefix_ref[q + 1, m * 8 : m * 8 + 8, :] = sums[m]
                return tuple(sums)

            zero = jnp.zeros((8, 128), f32)
            for m in range(TILE):
                prefix_ref[0, m * 8 : m * 8 + 8, :] = zero
            lax.fori_loop(0, VIEWS // UNROLL, gather, (zero,) * TILE)
            def step_adam(n, carry):
                block = start + n
                here = pl.ds(pl.multiple_of(n * 8, 8), 8)
                down = (block * 2 + sub // 4).astype(f32) + first_row
                rays_y = (down + 0.5 - ROWS / 2) / COLS
                rays_x = (((sub % 4) * 128 + lane).astype(f32) + 0.5 - COLS / 2) / COLS
                length = rays_x * rays_x + rays_y * rays_y + 1.0
                for v in range(IMG_DEV):
                    depth = depth_ref[v, block_rows(block), :]
                    lever = rays_x * tau_ref[0, v : v + 1, :] + rays_y * tau_ref[1, v : v + 1, :] + tau_ref[2, v : v + 1, :]
                    gathered = prefix_ref[table[2, v], here, :]
                    if v > 0:
                        gathered = gathered - prefix_ref[table[2, v - 1], here, :]
                    pull = (depth * length + lever) * weight_sum[v, block_rows(block), :] - gathered
                    gradient = 2.0 * depth * pull
                    rows = image_rows(block, v)
                    old_one = one_ref[rows, :]
                    old_two = two_ref[rows, :]
                    old_log = log_ref[rows, :]
                    new_one = beta_one * old_one + (1 - beta_one) * gradient
                    new_two = beta_two * old_two + (1 - beta_two) * gradient * gradient
                    corrected_one = new_one * (1 / bias_one)
                    corrected_two = new_two * (1 / bias_two)
                    new_log = old_log - learn_rate * corrected_one / (jnp.sqrt(corrected_two) + adam_eps)
                    one_ref[rows, :] = new_one
                    two_ref[rows, :] = new_two
                    log_ref[rows, :] = new_log
                    if not last:
                        depth_ref[v, block_rows(block), :] = depth_of(new_log)
                return carry

            lax.fori_loop(0, TILE, step_adam, 0)
            if last:
                for copy in stores(tile_id):
                    copy.start()
            return carry

        lax.fori_loop(0, BLOCKS // TILE, update, 0)
        if not last:
            lax.fori_loop(0, VIEWS, dot_view, 0)

    scale_store.wait()
    for tile_id in range(BLOCKS // TILE):
        for copy in stores(tile_id):
            copy.wait()

    def finish(k, carry):
        meta_copy(k).wait_send()
        slot_copy(k).wait_send()
        return carry

    lax.fori_loop(1, OWNERS, finish, 0)
    for t in range(ITERS):
        core_copy(t).wait_send()
        for n in range(CHIPS - 1):
            chip_copy(t, n, False).wait_send()


def store(log_in, one_in, two_in, scale_in, log_out, one_out, two_out, scale_out, bands, scale, in_sem, out_sem):
    half = GROUPS * IMG_DEV // 2
    moves = [(scale_in, scale, scale_out)]
    for part in range(2):
        rows = pl.ds(part * half, half)
        for n, (a, b) in enumerate([(log_in, log_out), (one_in, one_out), (two_in, two_out)]):
            moves.append((a.at[rows], bands.at[n, rows], b.at[rows]))
    loads = [pltpu.make_async_copy(a, m, in_sem.at[n]) for n, (a, m, b) in enumerate(moves)]
    stores = [pltpu.make_async_copy(m, b, out_sem.at[n]) for n, (a, m, b) in enumerate(moves)]
    for copy in loads:
        copy.start()
    for arrived, copy in zip(loads, stores):
        arrived.wait()
        copy.start()
    for copy in stores:
        copy.wait()


def shards(
    log_depth,
    moment_one,
    moment_two,
    image_pose,
    pair_points,
    confidence,
    pair_pose,
    first_local,
    second_owner,
    second_local,
):
    def fold(a):
        return a.reshape(IMG_DEV, GROUPS, 128).transpose(1, 0, 2).reshape(GROUPS * IMG_DEV, 128)

    def unfold(a):
        return a.reshape(GROUPS, IMG_DEV, 128).transpose(1, 0, 2).reshape(IMG_DEV, BAND)

    points = pair_points.transpose(1, 0, 2)
    conf = confidence.reshape(PAIR_DEV, 2, GROUPS, 128).transpose(0, 2, 1, 3).reshape(PAIR_DEV * GROUPS * 2, 128)
    hbm = pl.BlockSpec(memory_space=pltpu.HBM)
    band = jax.ShapeDtypeStruct((GROUPS * IMG_DEV, 128), f32)
    dma = pltpu.SemaphoreType.DMA
    out = pl.pallas_call(
        kernel,
        out_shape=(band, band, band, jax.ShapeDtypeStruct((1, PAIR_DEV), f32)),
        in_specs=[hbm] * 10,
        out_specs=(hbm,) * 4,
        scratch_shapes=[
            pltpu.VMEM((1, PAIR_DEV), f32),
            pltpu.VMEM((GROUPS * IMG_DEV, 128), f32),
            pltpu.VMEM((GROUPS * IMG_DEV, 128), f32),
            pltpu.VMEM((GROUPS * IMG_DEV, 128), f32),
            pltpu.VMEM((6, PAIR_DEV, BAND), jnp.bfloat16),
            pltpu.VMEM((PAIR_DEV * GROUPS * 2, 128), jnp.bfloat16),
            pltpu.SMEM((7, IMG_DEV * OWNERS), f32),
            pltpu.SMEM((7, PAIR_DEV), f32),
            pltpu.SMEM((PAIR_DEV,), jnp.int32),
            pltpu.SMEM((PAIR_DEV,), jnp.int32),
            pltpu.SMEM((PAIR_DEV,), jnp.int32),
            pltpu.VMEM((PAIR_DEV * GROUPS * 2, 128), f32),
            pltpu.VMEM((PAIR_DEV * GROUPS, 128), f32),
            pltpu.VMEM((PAIR_DEV * GROUPS, 128), f32),
            pltpu.VMEM((PAIR_DEV, CODE_ROWS, 128), jnp.int16),
            pltpu.VMEM((OWNERS, MOST, CODE_ROWS, 128), jnp.int16),
            pltpu.VMEM((OWNERS, MOST, CODE_ROWS, 128), jnp.int16),
            pltpu.VMEM((OWNERS, 8, 128), jnp.int32),
            pltpu.VMEM((VIEWS, GROUPS, 128), f32),
            pltpu.VMEM((VIEWS + 1, TILE * 8, 128), f32),
            pltpu.VMEM((IMG_DEV, GROUPS, 128), f32),
            pltpu.VMEM((IMG_DEV, GROUPS, 128), f32),
            pltpu.VMEM((3, 8, 128), f32),
            pltpu.VMEM((IMG_DEV, VIEWS, 128), f32),
            pltpu.VMEM((VIEWS, 128), f32),
            pltpu.VMEM((VIEWS, 128), f32),
            pltpu.VMEM((VIEWS, 128), f32),
            pltpu.VMEM((ITERS, 2, 2, 128), f32),
            pltpu.VMEM((ITERS, CHIPS, 2, 128), f32),
            pltpu.VMEM((8, 128), jnp.int32),
            pltpu.SMEM((8, 128), jnp.int32),
            dma((11,)),
            dma((BLOCKS // TILE, 3)),
            dma,
            dma((OWNERS,)),
            dma((OWNERS,)),
            dma((OWNERS,)),
            dma((OWNERS,)),
            dma((ITERS,)),
            dma((ITERS,)),
            dma((ITERS, CHIPS)),
            dma((ITERS, CHIPS)),
        ],
        compiler_params=pltpu.CompilerParams(
            collective_id=0, has_side_effects=True, vmem_limit_bytes=60 * 2**20
        ),
        name="align",
    )(
        fold(log_depth),
        fold(moment_one),
        fold(moment_two),
        points,
        conf,
        image_pose,
        pair_pose,
        first_local,
        second_owner.reshape(PAIR_DEV),
        second_local,
    )
    out = pl.pallas_call(
        store,
        out_shape=(band, band, band, jax.ShapeDtypeStruct((1, PAIR_DEV), f32)),
        in_specs=[hbm] * 4,
        out_specs=(hbm,) * 4,
        scratch_shapes=[
            pltpu.VMEM((3, GROUPS * IMG_DEV, 128), f32),
            pltpu.VMEM((1, PAIR_DEV), f32),
            dma((7,)),
            dma((7,)),
        ],
        compiler_params=pltpu.CompilerParams(vmem_limit_bytes=60 * 2**20),
        name="store",
    )(*out)
    return (unfold(out[0]), unfold(out[1]), unfold(out[2]), out[3].reshape(PAIR_DEV))


def solution(mesh):
    return jax.shard_map(
        shards,
        mesh=mesh,
        in_specs=(
            P("pair", "img"),
            P("pair", "img"),
            P("pair", "img"),
            P(),
            P("pair", None, "img"),
            P("pair", None, "img"),
            P(None, "pair"),
            P("pair"),
            P("pair", None),
            P("pair"),
        ),
        out_specs=(P("pair", "img"), P("pair", "img"), P("pair", "img"), P("pair")),
        check_vma=False,
    )
```

```python
import jax
import jax.numpy as jnp
from jax import lax
from jax.experimental import pallas as pl
from jax.experimental.pallas import tpu as pltpu
from jax.sharding import PartitionSpec as P

ROWS = 384
COLS = 512
ITERS = 3
START = 100
IMG_DEV = 4
PAIR_DEV = 8
MOST = 2
IMGS = 8
OWNERS = 16
XS = 4
YS = 4
ZS = 4
CHIPS = XS * YS * ZS
BAND = ROWS * COLS // IMGS
GROUPS = BAND // 128
BLOCKS = GROUPS // 8
BAND_ROWS = ROWS // IMGS
SLOTS = OWNERS * MOST
VIEWS = PAIR_DEV + SLOTS
HALF = GROUPS // 2
OWN_STEPS = 4
STEPS = (2, 1, 3)
TILE = 12
PART = 4
UNROLL = 4
LEVELS = 32700.0

beta_one = 0.9
beta_two = 0.999
learn_rate = 0.01
adam_eps = 1e-08
f32 = jnp.float32
MESH = pl.DeviceIdType.MESH


def rotation(scalar_q, vec_a, vec_b, vec_c):
    magnitude = jnp.sqrt(scalar_q * scalar_q + vec_a * vec_a + vec_b * vec_b + vec_c * vec_c)
    unit_s = scalar_q / magnitude
    unit_a = vec_a / magnitude
    unit_b = vec_b / magnitude
    unit_c = vec_c / magnitude
    return (
        (
            1 - 2 * (unit_b * unit_b + unit_c * unit_c),
            2 * (unit_a * unit_b - unit_s * unit_c),
            2 * (unit_a * unit_c + unit_s * unit_b),
        ),
        (
            2 * (unit_a * unit_b + unit_s * unit_c),
            1 - 2 * (unit_a * unit_a + unit_c * unit_c),
            2 * (unit_b * unit_c - unit_s * unit_a),
        ),
        (
            2 * (unit_a * unit_c - unit_s * unit_b),
            2 * (unit_b * unit_c + unit_s * unit_a),
            1 - 2 * (unit_a * unit_a + unit_b * unit_b),
        ),
    )


def kernel(
    log_hbm,
    one_hbm,
    two_hbm,
    points_hbm,
    conf_hbm,
    image_pose_hbm,
    pair_pose_hbm,
    first_local_hbm,
    second_owner_hbm,
    second_local_hbm,
    log_out,
    one_out,
    two_out,
    scale_out,
    scale_ref,
    log_ref,
    one_ref,
    two_ref,
    points_ref,
    conf_ref,
    image_pose,
    pair_pose,
    first_local,
    second_owner,
    second_local,
    conf_f,
    stage_one,
    stage_two,
    code_one_a,
    code_one_b,
    unit_one_a,
    unit_one_b,
    inverse_ref,
    code_two,
    unit_two,
    pass_hot,
    meta,
    cu_ref,
    prefix_ref,
    weight_sum,
    depth_ref,
    tau_ref,
    hot_ref,
    mask_ref,
    weight_ref,
    inner_ref,
    core_buf,
    chip_buf,
    table_ref,
    table,
    load_sem,
    store_sem,
    table_sem,
    send_sem,
    recv_sem,
    meta_send,
    meta_recv,
    core_send,
    core_recv,
    chip_send,
    chip_recv,
):
    def load(n, src, dst):
        copy = pltpu.make_async_copy(src, dst, load_sem.at[n])
        copy.start()
        return copy

    small = [
        load(0, second_owner_hbm, second_owner),
        load(1, second_local_hbm, second_local),
        load(2, first_local_hbm, first_local),
        load(3, pair_pose_hbm, pair_pose),
        load(4, image_pose_hbm, image_pose),
    ]
    conf_load = load(5, conf_hbm, conf_ref)
    second_load = load(6, points_hbm.at[pl.ds(3, 3)], points_ref.at[pl.ds(3, 3)])
    first_load = load(7, points_hbm.at[pl.ds(0, 3)], points_ref.at[pl.ds(0, 3)])
    log_load = load(8, log_hbm, log_ref)
    state_loads = [load(9, one_hbm, one_ref), load(10, two_hbm, two_ref)]

    my_img = lax.axis_index("img")
    my_pair = lax.axis_index("pair")
    my_y = my_pair // ZS
    my_z = my_pair % ZS

    def pair_at(k, sign):
        return ((my_y + sign * (k // ZS) + YS) % YS) * ZS + (my_z + sign * (k % ZS) + ZS) % ZS

    barrier = pltpu.get_barrier_semaphore()

    my_x = my_img // 2
    my_core = my_img % 2
    my_chip = my_x * OWNERS + my_pair
    xs = [(my_x + d) % XS for d in range(XS)]
    ys = [(my_y + d) % YS for d in range(YS)]
    zs = [(my_z + d) % ZS for d in range(ZS)]
    offsets = [(a, b, c) for a in range(XS) for b in range(YS) for c in range(ZS) if (a, b, c) != (0, 0, 0)]
    offsets.sort(key=lambda o: -sum(min(d, 4 - d) for d in o))

    def greet_chip(k, carry):
        x = (my_x + k // OWNERS) % XS
        y = (my_y + k // ZS) % YS
        z = (my_z + k) % ZS
        pl.semaphore_signal(barrier, 1, device_id=(x * 2 + my_core, y * ZS + z), device_id_type=MESH)
        return carry

    pl.semaphore_signal(barrier, 1, device_id=(my_img + 1 - 2 * my_core, my_pair), device_id_type=MESH)
    lax.fori_loop(1, CHIPS, greet_chip, 0)

    sub = lax.broadcasted_iota(jnp.int32, (8, 128), 0)
    lane = lax.broadcasted_iota(jnp.int32, (8, 128), 1)

    for copy in small:
        copy.wait()

    owners = [second_owner[e] for e in range(PAIR_DEV)]
    order = []
    for e in range(PAIR_DEV):
        rank = jnp.int32(0)
        for other in range(e):
            rank = rank + jnp.where(owners[other] == owners[e], 1, 0)
        order.append(owners[e] * MOST + rank)
    row = jnp.zeros((8, 128), jnp.int32)
    for e in range(PAIR_DEV):
        here = lane == my_pair * PAIR_DEV + e
        row = jnp.where(here & (sub == 0), order[e], row)
        row = jnp.where(here & (sub == 1), second_local[e], row)
    meta[0] = row

    def column(values):
        out = jnp.zeros((8, 128), f32)
        for e in range(PAIR_DEV):
            out = jnp.where(sub == e, values[e], out)
        return out

    pair_cols = [column([pair_pose[i, e] for e in range(PAIR_DEV)]) for i in range(7)]
    pair_rot = rotation(*pair_cols[:4])
    shift = pair_cols[4:]
    firsts = [my_pair * IMG_DEV + first_local[e] for e in range(PAIR_DEV)]
    seconds = [owners[e] * IMG_DEV + second_local[e] for e in range(PAIR_DEV)]
    lean = [2.0 * sum(pair_rot[i][j] * shift[i] for i in range(3)) for j in range(3)]
    shift_sq = sum(shift[i] * shift[i] for i in range(3))
    first_row = (my_img * BAND_ROWS).astype(f32)
    ray_y0 = (first_row + 0.5 - ROWS / 2) / COLS
    ray_x = [((lane + 128 * part).astype(f32) + 0.5 - COLS / 2) / COLS for part in range(4)]

    def widen(step, carry):
        rows = pl.ds(pl.multiple_of(step * 64, 64), 64)
        conf_f[rows, :] = conf_ref[rows, :].astype(f32)
        return carry

    conf_load.wait()
    lax.fori_loop(0, PAIR_DEV * 2 * GROUPS // 64, widen, 0)
    second_load.wait()

    def prepare(view, images, stage):
        cols = [column([image_pose[i, images[e]] for e in range(PAIR_DEV)]) for i in range(7)]
        rot = rotation(*cols[:4])
        trans = cols[4:]
        both = [[sum(rot[l][i] * pair_rot[l][j] for l in range(3)) for j in range(3)] for i in range(3)]
        moved = [sum(rot[l][i] * shift[l] for l in range(3)) for i in range(3)]
        full = [[both[i][0], both[i][1], both[i][2], moved[i]] for i in range(3)]
        base = [[ray_x[part] * full[0][j] + (full[2][j] + ray_y0 * full[1][j]) for part in range(4)] for j in range(4)]
        slope = [full[1][j] * (1.0 / COLS) for j in range(4)]
        toward = [sum(trans[l] * pair_rot[l][j] for l in range(3)) for j in range(3)]
        offset = sum(trans[l] * shift[l] for l in range(3))

        def body(r, carry):
            total_sq, total_dot, total_conf, largest = carry
            down = r.astype(f32)
            tilt = [slope[j] * down for j in range(4)]
            for part in range(4):
                at = pl.ds(pl.multiple_of(r * COLS + part * 128, 128), 128)
                x = [points_ref[3 * view + j, :, at].astype(f32) for j in range(3)]
                weight = conf_f[pl.ds((r * 4 + part) * 2 + view, 8, stride=2 * GROUPS), :]
                value = base[3][part] + tilt[3]
                for j in range(3):
                    value = value + (base[j][part] + tilt[j]) * x[j]
                value = value * weight
                largest = jnp.maximum(largest, jnp.abs(value))
                stage[pl.ds(pl.multiple_of((r * 4 + part) * 8, 8), 8), :] = value
                square = x[0] * (x[0] + lean[0]) + x[1] * (x[1] + lean[1]) + x[2] * (x[2] + lean[2])
                dot = x[0] * toward[0] + x[1] * toward[1] + x[2] * toward[2]
                total_sq = total_sq + weight * square
                total_dot = total_dot + weight * dot
                total_conf = total_conf + weight
            return (total_sq, total_dot, total_conf, largest)

        def run(half, sums):
            tiny = jnp.full((8, 128), 1e-30, f32)
            start = half * (BAND_ROWS // 2)
            out = lax.fori_loop(start, start + BAND_ROWS // 2, body, (*sums, tiny))
            return out[:3], out[3]

        def close(sums):
            return (sums[0] + sums[2] * shift_sq, sums[1] + sums[2] * offset)

        return run, close

    empty = (jnp.zeros((8, 128), f32),) * 3
    code_one = (code_one_a, code_one_b)
    unit_one = (unit_one_a, unit_one_b)
    run_two, close_two = prepare(1, seconds, stage_two)

    def encode(half, largest):
        unit_one[half][0] = largest * (1.0 / LEVELS)
        inverse_ref[...] = LEVELS / largest

        def body(e, carry):
            inverse = inverse_ref[pl.ds(e, 1), :]
            for step in range(HALF // 16):
                place = half * (HALF // 16) + step
                rows = slice(step * 16, step * 16 + 16)
                value = stage_two[pl.ds(place * 128 + e, 16, stride=8), :] * inverse
                code_one[half][0, e, rows, :] = jnp.floor(value + 0.5).astype(jnp.int32).astype(jnp.int16)
                weight = conf_f[pl.ds(e * 2 * GROUPS + place * 32 + 1, 16, stride=2), :] * 128.0
                rows = slice(HALF + step * 16, HALF + step * 16 + 16)
                code_one[half][0, e, rows, :] = weight.astype(jnp.int32).astype(jnp.int16)
            return carry

        lax.fori_loop(0, PAIR_DEV, body, 0)

    def ahead(axis, d):
        if axis == 0:
            return (my_img, ys[d] * ZS + my_z)
        return (my_img, my_y * ZS + zs[d])

    def bulk_copies(phase, half, d):
        if phase == 0:
            refs = (code_one[half], unit_one[half])
        else:
            refs = (code_two.at[half], unit_two.at[half])
        axis = half if phase == 0 else 1 - half
        source = 0 if phase == 0 else d
        landing = d if phase == 0 else OWN_STEPS + d
        sems = (phase * 2 + half) * 4 + d
        return [
            pltpu.make_async_remote_copy(
                src_ref=ref.at[source],
                dst_ref=ref.at[landing],
                send_sem=send_sem.at[n, sems],
                recv_sem=recv_sem.at[n, sems],
                device_id=ahead(axis, d),
                device_id_type=MESH,
            )
            for n, ref in enumerate(refs)
        ]

    sums, largest = run_two(0, empty)
    encode(0, largest)
    pl.semaphore_wait(barrier, CHIPS)
    for d in STEPS:
        for copy in bulk_copies(0, 0, d):
            copy.start()

    def meta_copy(k):
        return pltpu.make_async_remote_copy(
            src_ref=meta.at[0],
            dst_ref=meta.at[k],
            send_sem=meta_send.at[k],
            recv_sem=meta_recv.at[k],
            device_id=(my_img, pair_at(k, 1)),
            device_id_type=MESH,
        )

    def start_meta(k, carry):
        meta_copy(k).start()
        return carry

    lax.fori_loop(1, OWNERS, start_meta, 0)
    sums, largest = run_two(1, sums)
    encode(1, largest)
    for d in STEPS:
        for copy in bulk_copies(0, 1, d):
            copy.start()
    square_two, dot_two = close_two(sums)
    first_load.wait()
    run_one, close_one = prepare(0, firsts, stage_one)
    sums, largest = run_one(0, empty)
    sums, largest = run_one(1, sums)
    square_one, dot_one = close_one(sums)

    def depth_of(values):
        return jnp.exp(values.astype(jnp.bfloat16).astype(f32))

    def image_rows(block, v):
        return pl.ds(block * 32 + v, 8, stride=IMG_DEV)

    def block_rows(block):
        return pl.ds(pl.multiple_of(block * 8, 8), 8)

    def first_depth(block, carry):
        for v in range(IMG_DEV):
            depth_ref[v, block_rows(block), :] = depth_of(log_ref[image_rows(block, v), :])
        return carry

    log_load.wait()
    lax.fori_loop(0, BLOCKS, first_depth, 0)
    for copy in state_loads:
        copy.wait()

    own = [[image_pose[i, my_pair * IMG_DEV + min(v, IMG_DEV - 1)] for v in range(8)] for i in range(7)]
    own_cols = [column(own[i]) for i in range(7)]
    own_rot = rotation(*own_cols[:4])
    for i in range(3):
        tau_ref[i] = sum(own_rot[l][i] * own_cols[4 + l] for l in range(3))

    for k in range(1, OWNERS):
        meta_copy(k).wait_recv()
    known = meta[0]
    for k in range(1, OWNERS):
        known = known + meta[k]
    code_row = jnp.broadcast_to(known[0:1], (8, 128))
    local_row = jnp.broadcast_to(known[1:2], (8, 128))
    from_pair = lane // PAIR_DEV
    step_of = ((my_y - from_pair // ZS + YS) % YS) * ZS + (my_z - from_pair % ZS + ZS) % ZS
    slot_of = jnp.where(code_row // MOST == my_pair, step_of * MOST + code_row % MOST, -1)
    local_first = jnp.zeros((8, 128), jnp.int32)
    for e in range(PAIR_DEV):
        local_first = jnp.where(sub == e, first_local[e], local_first)
    own_mask = jnp.where(lane == my_pair * PAIR_DEV + sub, 1.0, 0.0)
    mask_ref[0:8, :] = own_mask
    for v in range(IMG_DEV):
        hot_ref[v, 0:8, :] = jnp.where(local_first == v, 1.0, 0.0)
    for group in range(SLOTS // 8):
        rows = pl.ds(8 + group * 8, 8)
        held = slot_of == sub + group * 8
        mask_ref[rows, :] = jnp.where(held, 1.0, 0.0)
        for v in range(IMG_DEV):
            found = jnp.where(held & (local_row == v), 1.0, 0.0)
            hot_ref[v, rows, :] = jnp.broadcast_to(jnp.sum(found, axis=1, keepdims=True), (8, 128))

    image_row = jnp.zeros((8, 128), jnp.int32)
    for group in range(VIEWS // 8):
        if group == 0:
            image_col = local_first
        else:
            held = (slot_of == sub + (group - 1) * 8).astype(jnp.int32)
            image_col = jnp.sum(held * (local_row - IMG_DEV), axis=1, keepdims=True) + IMG_DEV
        found = jnp.where(lane == sub + group * 8, image_col, 0)
        image_row = image_row + jnp.broadcast_to(jnp.sum(found, axis=0, keepdims=True), (8, 128))
    order_row = jnp.zeros((8, 128), jnp.int32)
    listed = lane < VIEWS
    for group in range(VIEWS // 8):
        view = sub + group * 8
        found = jnp.where(lane == view, image_row, 0)
        image_col = jnp.sum(found, axis=1, keepdims=True)
        before = listed & ((image_row < image_col) | ((image_row == image_col) & (lane < view)))
        place = jnp.sum(before.astype(jnp.int32), axis=1, keepdims=True)
        found = jnp.where(lane == place, view, 0)
        order_row = order_row + jnp.broadcast_to(jnp.sum(found, axis=0, keepdims=True), (8, 128))
    end_row = jnp.zeros((8, 128), jnp.int32)
    for v in range(IMG_DEV):
        upto = (listed & (image_row <= v)).astype(jnp.int32)
        end_row = jnp.where(lane == v, jnp.sum(upto, axis=1, keepdims=True), end_row)
    image_row = jnp.minimum(image_row, IMG_DEV - 1)

    pass_row = jnp.zeros((8, 128), jnp.int32)
    for half in range(2):
        for d in range(4):
            if half == 0:
                goal = my_y * ZS + zs[d]
                source = ((my_y - sub // MOST + YS) % YS) * ZS + my_z
            else:
                goal = ys[d] * ZS + my_z
                source = my_y * ZS + (my_z - sub // MOST + ZS) % ZS
            match = (from_pair == source) & (code_row == goal * MOST + sub % MOST)
            chosen = jnp.sum(jnp.where(match, lane % PAIR_DEV, 0), axis=1, keepdims=True)
            found = jnp.where(lane == sub + (half * 4 + d) * 8, chosen, 0)
            pass_row = pass_row + jnp.broadcast_to(jnp.sum(found, axis=0, keepdims=True), (8, 128))
            for v in range(IMG_DEV):
                hot = jnp.where(match & (local_row == v), 1.0, 0.0)
                pass_hot[half * 4 + d, v] = jnp.broadcast_to(jnp.sum(hot, axis=1, keepdims=True), (8, 128))
    table_ref[...] = jnp.where(sub == 0, image_row, jnp.where(sub == 1, order_row, jnp.where(sub == 2, end_row, pass_row)))
    table_copy = pltpu.make_async_copy(table_ref, table, table_sem)
    table_copy.start()

    def first_copy(e, carry):
        for block in range(BLOCKS):
            cu_ref[e, block * 8 : block * 8 + 8, :] = stage_one[pl.ds(block * 64 + e, 8, stride=8), :]
        return carry

    lax.fori_loop(0, PAIR_DEV, first_copy, 0)
    table_copy.wait()

    def dot_view(r, carry):
        v = table[0, r]
        totals = [jnp.zeros((8, 128), f32) for n in range(PART)]
        for block in range(BLOCKS):
            rows = slice(block * 8, block * 8 + 8)
            totals[block % PART] = totals[block % PART] + cu_ref[r, rows, :] * depth_ref[v, rows, :]
        total = (totals[0] + totals[1]) + (totals[2] + totals[3])
        inner_ref[pl.ds(r, 1), :] = jnp.sum(total, axis=0, keepdims=True)
        return carry

    lax.fori_loop(0, PAIR_DEV, dot_view, 0)

    def first_sums(block, carry):
        sums = [jnp.zeros((8, 128), f32) for v in range(IMG_DEV)]
        for e in range(PAIR_DEV):
            weight = conf_f[pl.ds(e * 2 * GROUPS + block * 16, 8, stride=2), :]
            for v in range(IMG_DEV):
                sums[v] = sums[v] + weight * hot_ref[v, e : e + 1, :]
        for v in range(IMG_DEV):
            weight_sum[v, block_rows(block), :] = sums[v]
        return carry

    lax.fori_loop(0, BLOCKS, first_sums, 0)

    def pass_on(half, d):
        place = d if d > 0 else OWN_STEPS
        index = half * 4 + d
        sources = [table[3, index * 8 + n] for n in range(8)]
        hots = [[pass_hot[index, v, n : n + 1, :] for v in range(IMG_DEV)] for n in range(8)]
        for n in range(8):
            unit_two[half, place, n : n + 1, :] = unit_one[half][n // MOST, pl.ds(sources[n], 1), :]

        def body(step, carry):
            rows = pl.ds(pl.multiple_of(step * 16, 16), 16)
            weight_rows = pl.ds(pl.multiple_of(HALF + step * 16, 16), 16)
            totals = [jnp.zeros((16, 128), f32) for v in range(IMG_DEV)]
            for n in range(8):
                code_two[half, place, n, rows, :] = code_one[half][n // MOST, sources[n], rows, :]
                weight = code_one[half][n // MOST, sources[n], weight_rows, :].astype(jnp.int32).astype(f32)
                for v in range(IMG_DEV):
                    totals[v] = totals[v] + weight * hots[n][v]
            for v in range(IMG_DEV):
                code_two[half, place, 8 + v, rows, :] = totals[v].astype(jnp.int32).astype(jnp.int16)
            return carry

        lax.fori_loop(0, HALF // 16, body, 0)

    def take(half, d):
        place = OWN_STEPS + d
        slots = []
        for n in range(8):
            step = n // MOST * 4 + d if half == 0 else d * 4 + n // MOST
            slots.append(PAIR_DEV + step * MOST + n % MOST)
        units = [unit_two[half, place, n : n + 1, :] for n in range(8)]
        images = [table[0, slot] for slot in slots]

        def body(step, totals):
            totals = list(totals)
            rows = pl.ds(pl.multiple_of(step * 16, 16), 16)
            full = pl.ds(pl.multiple_of(half * HALF + step * 16, 16), 16)
            for n in range(8):
                cu = code_two[half, place, n, rows, :].astype(jnp.int32).astype(f32) * units[n]
                cu_ref[slots[n], full, :] = cu
                cu = cu * depth_ref[images[n], full, :]
                totals[n] = totals[n] + (cu[0:8] + cu[8:16])
            for v in range(IMG_DEV):
                weight = code_two[half, place, 8 + v, rows, :].astype(jnp.int32).astype(f32)
                weight_sum[v, full, :] = weight_sum[v, full, :] + weight * (1.0 / 128.0)
            return tuple(totals)

        totals = lax.fori_loop(0, HALF // 16, body, (jnp.zeros((8, 128), f32),) * 8)
        for n in range(8):
            total = jnp.sum(totals[n], axis=0, keepdims=True)
            row = slice(slots[n], slots[n] + 1)
            inner_ref[row, :] = inner_ref[row, :] + total

    inner_ref[PAIR_DEV:VIEWS, :] = jnp.zeros((SLOTS, 128), f32)
    for half in range(2):
        for d in STEPS:
            for copy in bulk_copies(0, half, d):
                copy.wait_recv()
        for d in STEPS:
            pass_on(half, d)
            for copy in bulk_copies(1, half, d):
                copy.start()
        pass_on(half, 0)
        take(half, 0)
    for half in range(2):
        for d in STEPS:
            for copy in bulk_copies(1, half, d):
                copy.wait_recv()
            take(half, d)

    def pair_row(col):
        return jnp.sum(jnp.sum(col, axis=1, keepdims=True) * own_mask, axis=0, keepdims=True)

    fixed_row = pair_row(dot_one + dot_two)
    square_row = pair_row(square_one + square_two)

    def core_copy(t):
        return pltpu.make_async_remote_copy(
            src_ref=core_buf.at[t, 0],
            dst_ref=core_buf.at[t, 1],
            send_sem=core_send.at[t],
            recv_sem=core_recv.at[t],
            device_id=(my_img + 1 - 2 * my_core, my_pair),
            device_id_type=MESH,
        )

    def chip_copy(t, n, arrival):
        a, b, c = offsets[n]
        pair = ys[b] * ZS + zs[c]
        place = xs[a] * OWNERS + pair if arrival else my_chip
        return pltpu.make_async_remote_copy(
            src_ref=chip_buf.at[t, place],
            dst_ref=chip_buf.at[t, place],
            send_sem=chip_send.at[t, n],
            recv_sem=chip_recv.at[t, place],
            device_id=(xs[a] * 2 + my_core, pair),
            device_id_type=MESH,
        )

    def sum_all(t, tile):
        core_buf[t, 0] = tile
        core_copy(t).start()
        core_copy(t).wait_recv()
        chip_buf[t, my_chip] = tile + core_buf[t, 1]
        for n in range(CHIPS - 1):
            chip_copy(t, n, False).start()
        for n in reversed(range(CHIPS - 1)):
            chip_copy(t, n, True).wait_recv()
        parts = [chip_buf[t, n] for n in range(CHIPS)]
        while len(parts) > 1:
            parts = [parts[n] + parts[n + 1] for n in range(0, len(parts), 2)]
        return parts[0]

    def stores(tile_id):
        rows = pl.ds(pl.multiple_of(tile_id * TILE * 32, 8), TILE * 32)
        pairs = [(log_ref, log_out), (one_ref, one_out), (two_ref, two_out)]
        return [
            pltpu.make_async_copy(a.at[rows], b.at[rows], store_sem.at[tile_id, n])
            for n, (a, b) in enumerate(pairs)
        ]

    scale_store = pltpu.make_async_copy(scale_ref, scale_out, load_sem.at[0])
    denominator = None
    for sweep in range(ITERS):
        row = jnp.zeros((8, 128), f32)
        for group in range(VIEWS // 8):
            rows = slice(group * 8, group * 8 + 8)
            row = row + jnp.sum(inner_ref[rows, :], axis=1, keepdims=True) * mask_ref[rows, :]
        row = jnp.sum(row, axis=0, keepdims=True) + fixed_row
        two = lax.broadcasted_iota(jnp.int32, (2, 128), 0)
        total = sum_all(sweep, jnp.where(two == 0, row, square_row))
        if sweep == 0:
            denominator = total[1:2]
        scales = jnp.broadcast_to(total[0:1] / denominator, (8, 128))
        for group in range(VIEWS // 8):
            rows = slice(group * 8, group * 8 + 8)
            held = jnp.sum(scales * mask_ref[rows, :], axis=1, keepdims=True)
            if group == 0 and sweep == ITERS - 1:
                own_row = jnp.sum(jnp.where(lane == sub, held, 0.0), axis=0, keepdims=True)
                scale_ref[...] = own_row[:, 0:PAIR_DEV]
                scale_store.start()
            weight_ref[rows, :] = jnp.broadcast_to(held, (8, 128))

        steps = START + sweep + 1
        bias_one = 1 - beta_one**steps
        bias_two = 1 - beta_two**steps
        last = sweep == ITERS - 1

        def update(tile_id, carry):
            start = tile_id * TILE

            def gather(step, sums):
                sums = list(sums)
                for n in range(UNROLL):
                    q = step * UNROLL + n
                    r = table[1, q]
                    weight = weight_ref[pl.ds(r, 1), :]
                    for m in range(TILE):
                        sums[m] = sums[m] + cu_ref[r, block_rows(start + m), :] * weight
                        prefix_ref[q + 1, m * 8 : m * 8 + 8, :] = sums[m]
                return tuple(sums)

            zero = jnp.zeros((8, 128), f32)
            for m in range(TILE):
                prefix_ref[0, m * 8 : m * 8 + 8, :] = zero
            lax.fori_loop(0, VIEWS // UNROLL, gather, (zero,) * TILE)
            def step_adam(n, carry):
                block = start + n
                here = pl.ds(pl.multiple_of(n * 8, 8), 8)
                down = (block * 2 + sub // 4).astype(f32) + first_row
                rays_y = (down + 0.5 - ROWS / 2) / COLS
                rays_x = (((sub % 4) * 128 + lane).astype(f32) + 0.5 - COLS / 2) / COLS
                length = rays_x * rays_x + rays_y * rays_y + 1.0
                for v in range(IMG_DEV):
                    depth = depth_ref[v, block_rows(block), :]
                    lever = rays_x * tau_ref[0, v : v + 1, :] + rays_y * tau_ref[1, v : v + 1, :] + tau_ref[2, v : v + 1, :]
                    gathered = prefix_ref[table[2, v], here, :]
                    if v > 0:
                        gathered = gathered - prefix_ref[table[2, v - 1], here, :]
                    pull = (depth * length + lever) * weight_sum[v, block_rows(block), :] - gathered
                    gradient = 2.0 * depth * pull
                    rows = image_rows(block, v)
                    old_one = one_ref[rows, :]
                    old_two = two_ref[rows, :]
                    old_log = log_ref[rows, :]
                    new_one = beta_one * old_one + (1 - beta_one) * gradient
                    new_two = beta_two * old_two + (1 - beta_two) * gradient * gradient
                    corrected_one = new_one * (1 / bias_one)
                    corrected_two = new_two * (1 / bias_two)
                    new_log = old_log - learn_rate * corrected_one / (jnp.sqrt(corrected_two) + adam_eps)
                    one_ref[rows, :] = new_one
                    two_ref[rows, :] = new_two
                    log_ref[rows, :] = new_log
                    if not last:
                        depth_ref[v, block_rows(block), :] = depth_of(new_log)
                return carry

            lax.fori_loop(0, TILE, step_adam, 0)
            if last:
                for copy in stores(tile_id):
                    copy.start()
            return carry

        lax.fori_loop(0, BLOCKS // TILE, update, 0)
        if not last:
            lax.fori_loop(0, VIEWS, dot_view, 0)

    scale_store.wait()
    for tile_id in range(BLOCKS // TILE):
        for copy in stores(tile_id):
            copy.wait()

    def finish(k, carry):
        meta_copy(k).wait_send()
        return carry

    lax.fori_loop(1, OWNERS, finish, 0)
    for phase in range(2):
        for half in range(2):
            for d in STEPS:
                for copy in bulk_copies(phase, half, d):
                    copy.wait_send()
    for t in range(ITERS):
        core_copy(t).wait_send()
        for n in range(CHIPS - 1):
            chip_copy(t, n, False).wait_send()


def store(log_in, one_in, two_in, scale_in, log_out, one_out, two_out, scale_out, bands, scale, in_sem, out_sem):
    half = GROUPS * IMG_DEV // 2
    moves = [(scale_in, scale, scale_out)]
    for part in range(2):
        rows = pl.ds(part * half, half)
        for n, (a, b) in enumerate([(log_in, log_out), (one_in, one_out), (two_in, two_out)]):
            moves.append((a.at[rows], bands.at[n, rows], b.at[rows]))
    loads = [pltpu.make_async_copy(a, m, in_sem.at[n]) for n, (a, m, b) in enumerate(moves)]
    stores = [pltpu.make_async_copy(m, b, out_sem.at[n]) for n, (a, m, b) in enumerate(moves)]
    for copy in loads:
        copy.start()
    for arrived, copy in zip(loads, stores):
        arrived.wait()
        copy.start()
    for copy in stores:
        copy.wait()


def shards(
    log_depth,
    moment_one,
    moment_two,
    image_pose,
    pair_points,
    confidence,
    pair_pose,
    first_local,
    second_owner,
    second_local,
):
    def fold(a):
        return a.reshape(IMG_DEV, GROUPS, 128).transpose(1, 0, 2).reshape(GROUPS * IMG_DEV, 128)

    def unfold(a):
        return a.reshape(GROUPS, IMG_DEV, 128).transpose(1, 0, 2).reshape(IMG_DEV, BAND)

    points = pair_points.transpose(1, 0, 2)
    conf = confidence.reshape(PAIR_DEV, 2, GROUPS, 128).transpose(0, 2, 1, 3).reshape(PAIR_DEV * GROUPS * 2, 128)
    hbm = pl.BlockSpec(memory_space=pltpu.HBM)
    band = jax.ShapeDtypeStruct((GROUPS * IMG_DEV, 128), f32)
    dma = pltpu.SemaphoreType.DMA
    out = pl.pallas_call(
        kernel,
        out_shape=(band, band, band, jax.ShapeDtypeStruct((1, PAIR_DEV), f32)),
        in_specs=[hbm] * 10,
        out_specs=(hbm,) * 4,
        scratch_shapes=[
            pltpu.VMEM((1, PAIR_DEV), f32),
            pltpu.VMEM((GROUPS * IMG_DEV, 128), f32),
            pltpu.VMEM((GROUPS * IMG_DEV, 128), f32),
            pltpu.VMEM((GROUPS * IMG_DEV, 128), f32),
            pltpu.VMEM((6, PAIR_DEV, BAND), jnp.bfloat16),
            pltpu.VMEM((PAIR_DEV * GROUPS * 2, 128), jnp.bfloat16),
            pltpu.SMEM((7, IMG_DEV * OWNERS), f32),
            pltpu.SMEM((7, PAIR_DEV), f32),
            pltpu.SMEM((PAIR_DEV,), jnp.int32),
            pltpu.SMEM((PAIR_DEV,), jnp.int32),
            pltpu.SMEM((PAIR_DEV,), jnp.int32),
            pltpu.VMEM((PAIR_DEV * GROUPS * 2, 128), f32),
            pltpu.VMEM((PAIR_DEV * GROUPS, 128), f32),
            pltpu.VMEM((PAIR_DEV * GROUPS, 128), f32),
            pltpu.VMEM((4, PAIR_DEV, 2 * HALF, 128), jnp.int16),
            pltpu.VMEM((4, PAIR_DEV, 2 * HALF, 128), jnp.int16),
            pltpu.VMEM((4, PAIR_DEV, 128), f32),
            pltpu.VMEM((4, PAIR_DEV, 128), f32),
            pltpu.VMEM((PAIR_DEV, 128), f32),
            pltpu.VMEM((2, 2 * OWN_STEPS, 8 + IMG_DEV, HALF, 128), jnp.int16),
            pltpu.VMEM((2, 2 * OWN_STEPS, 8, 128), f32),
            pltpu.VMEM((8, IMG_DEV, 8, 128), f32),
            pltpu.VMEM((OWNERS, 8, 128), jnp.int32),
            pltpu.VMEM((VIEWS, GROUPS, 128), f32),
            pltpu.VMEM((VIEWS + 1, TILE * 8, 128), f32),
            pltpu.VMEM((IMG_DEV, GROUPS, 128), f32),
            pltpu.VMEM((IMG_DEV, GROUPS, 128), f32),
            pltpu.VMEM((3, 8, 128), f32),
            pltpu.VMEM((IMG_DEV, VIEWS, 128), f32),
            pltpu.VMEM((VIEWS, 128), f32),
            pltpu.VMEM((VIEWS, 128), f32),
            pltpu.VMEM((VIEWS, 128), f32),
            pltpu.VMEM((ITERS, 2, 2, 128), f32),
            pltpu.VMEM((ITERS, CHIPS, 2, 128), f32),
            pltpu.VMEM((8, 128), jnp.int32),
            pltpu.SMEM((8, 128), jnp.int32),
            dma((11,)),
            dma((BLOCKS // TILE, 3)),
            dma,
            dma((2, 16)),
            dma((2, 16)),
            dma((OWNERS,)),
            dma((OWNERS,)),
            dma((ITERS,)),
            dma((ITERS,)),
            dma((ITERS, CHIPS)),
            dma((ITERS, CHIPS)),
        ],
        compiler_params=pltpu.CompilerParams(
            collective_id=0, has_side_effects=True, vmem_limit_bytes=60 * 2**20
        ),
        name="align",
    )(
        fold(log_depth),
        fold(moment_one),
        fold(moment_two),
        points,
        conf,
        image_pose,
        pair_pose,
        first_local,
        second_owner.reshape(PAIR_DEV),
        second_local,
    )
    out = pl.pallas_call(
        store,
        out_shape=(band, band, band, jax.ShapeDtypeStruct((1, PAIR_DEV), f32)),
        in_specs=[hbm] * 4,
        out_specs=(hbm,) * 4,
        scratch_shapes=[
            pltpu.VMEM((3, GROUPS * IMG_DEV, 128), f32),
            pltpu.VMEM((1, PAIR_DEV), f32),
            dma((7,)),
            dma((7,)),
        ],
        compiler_params=pltpu.CompilerParams(vmem_limit_bytes=60 * 2**20),
        name="store",
    )(*out)
    return (unfold(out[0]), unfold(out[1]), unfold(out[2]), out[3].reshape(PAIR_DEV))


def solution(mesh):
    return jax.shard_map(
        shards,
        mesh=mesh,
        in_specs=(
            P("pair", "img"),
            P("pair", "img"),
            P("pair", "img"),
            P(),
            P("pair", None, "img"),
            P("pair", None, "img"),
            P(None, "pair"),
            P("pair"),
            P("pair", None),
            P("pair"),
        ),
        out_specs=(P("pair", "img"), P("pair", "img"), P("pair", "img"), P("pair")),
        check_vma=False,
    )
```

```python
import jax
import jax.numpy as jnp
from jax import lax
from jax.experimental import pallas as pl
from jax.experimental.pallas import tpu as pltpu
from jax.sharding import PartitionSpec as P

ROWS = 384
COLS = 512
ITERS = 3
START = 100
IMG_DEV = 4
PAIR_DEV = 8
MOST = 2
IMGS = 8
OWNERS = 16
XS = 4
YS = 4
ZS = 4
CHIPS = XS * YS * ZS
BAND = ROWS * COLS // IMGS
GROUPS = BAND // 128
BLOCKS = GROUPS // 8
BAND_ROWS = ROWS // IMGS
SLOTS = OWNERS * MOST
VIEWS = PAIR_DEV + SLOTS
HALF = GROUPS // 2
OWN_STEPS = 4
STEPS = (2, 1, 3)
TILE = 12
PART = 4
ADAM = 6
UNROLL = 4
LEVELS = 32700.0

beta_one = 0.9
beta_two = 0.999
learn_rate = 0.01
adam_eps = 1e-08
f32 = jnp.float32
MESH = pl.DeviceIdType.MESH


def rotation(scalar_q, vec_a, vec_b, vec_c):
    magnitude = jnp.sqrt(scalar_q * scalar_q + vec_a * vec_a + vec_b * vec_b + vec_c * vec_c)
    unit_s = scalar_q / magnitude
    unit_a = vec_a / magnitude
    unit_b = vec_b / magnitude
    unit_c = vec_c / magnitude
    return (
        (
            1 - 2 * (unit_b * unit_b + unit_c * unit_c),
            2 * (unit_a * unit_b - unit_s * unit_c),
            2 * (unit_a * unit_c + unit_s * unit_b),
        ),
        (
            2 * (unit_a * unit_b + unit_s * unit_c),
            1 - 2 * (unit_a * unit_a + unit_c * unit_c),
            2 * (unit_b * unit_c - unit_s * unit_a),
        ),
        (
            2 * (unit_a * unit_c - unit_s * unit_b),
            2 * (unit_b * unit_c + unit_s * unit_a),
            1 - 2 * (unit_a * unit_a + unit_b * unit_b),
        ),
    )


def kernel(
    log_hbm,
    one_hbm,
    two_hbm,
    points_hbm,
    conf_hbm,
    image_pose_hbm,
    pair_pose_hbm,
    first_local_hbm,
    second_owner_hbm,
    second_local_hbm,
    log_out,
    one_out,
    two_out,
    scale_out,
    scale_ref,
    log_ref,
    one_ref,
    two_ref,
    points_ref,
    conf_ref,
    image_pose,
    pair_pose,
    first_local,
    second_owner,
    second_local,
    conf_f,
    stage_one,
    stage_two,
    code_one_a,
    code_one_b,
    unit_one_a,
    unit_one_b,
    inverse_ref,
    code_two,
    unit_two,
    pass_hot,
    meta,
    cu_ref,
    prefix_ref,
    state_ref,
    weight_sum,
    lever_sum,
    depth_ref,
    tau_ref,
    hot_ref,
    mask_ref,
    weight_ref,
    inner_ref,
    core_buf,
    chip_buf,
    table_ref,
    table,
    load_sem,
    store_sem,
    table_sem,
    send_sem,
    recv_sem,
    meta_send,
    meta_recv,
    core_send,
    core_recv,
    chip_send,
    chip_recv,
):
    def load(n, src, dst):
        copy = pltpu.make_async_copy(src, dst, load_sem.at[n])
        copy.start()
        return copy

    small = [
        load(0, second_owner_hbm, second_owner),
        load(1, second_local_hbm, second_local),
        load(2, first_local_hbm, first_local),
        load(3, pair_pose_hbm, pair_pose),
        load(4, image_pose_hbm, image_pose),
    ]
    conf_load = load(5, conf_hbm, conf_ref)
    second_load = load(6, points_hbm.at[pl.ds(3, 3)], points_ref.at[pl.ds(3, 3)])
    first_load = load(7, points_hbm.at[pl.ds(0, 3)], points_ref.at[pl.ds(0, 3)])
    log_load = load(8, log_hbm, log_ref)
    state_loads = [load(9, one_hbm, one_ref), load(10, two_hbm, two_ref)]

    my_img = lax.axis_index("img")
    my_pair = lax.axis_index("pair")
    my_y = my_pair // ZS
    my_z = my_pair % ZS

    def pair_at(k, sign):
        return ((my_y + sign * (k // ZS) + YS) % YS) * ZS + (my_z + sign * (k % ZS) + ZS) % ZS

    barrier = pltpu.get_barrier_semaphore()

    my_x = my_img // 2
    my_core = my_img % 2
    my_chip = my_x * OWNERS + my_pair
    xs = [(my_x + d) % XS for d in range(XS)]
    ys = [(my_y + d) % YS for d in range(YS)]
    zs = [(my_z + d) % ZS for d in range(ZS)]
    offsets = [(a, b, c) for a in range(XS) for b in range(YS) for c in range(ZS) if (a, b, c) != (0, 0, 0)]
    offsets.sort(key=lambda o: -sum(min(d, 4 - d) for d in o))

    def greet_chip(k, carry):
        x = (my_x + k // OWNERS) % XS
        y = (my_y + k // ZS) % YS
        z = (my_z + k) % ZS
        pl.semaphore_signal(barrier, 1, device_id=(x * 2 + my_core, y * ZS + z), device_id_type=MESH)
        return carry

    pl.semaphore_signal(barrier, 1, device_id=(my_img + 1 - 2 * my_core, my_pair), device_id_type=MESH)
    lax.fori_loop(1, CHIPS, greet_chip, 0)

    sub = lax.broadcasted_iota(jnp.int32, (8, 128), 0)
    lane = lax.broadcasted_iota(jnp.int32, (8, 128), 1)

    for copy in small:
        copy.wait()

    owners = [second_owner[e] for e in range(PAIR_DEV)]
    order = []
    for e in range(PAIR_DEV):
        rank = jnp.int32(0)
        for other in range(e):
            rank = rank + jnp.where(owners[other] == owners[e], 1, 0)
        order.append(owners[e] * MOST + rank)
    row = jnp.zeros((8, 128), jnp.int32)
    for e in range(PAIR_DEV):
        here = lane == my_pair * PAIR_DEV + e
        row = jnp.where(here & (sub == 0), order[e], row)
        row = jnp.where(here & (sub == 1), second_local[e], row)
    meta[0] = row

    def column(values):
        out = jnp.zeros((8, 128), f32)
        for e in range(PAIR_DEV):
            out = jnp.where(sub == e, values[e], out)
        return out

    pair_cols = [column([pair_pose[i, e] for e in range(PAIR_DEV)]) for i in range(7)]
    pair_rot = rotation(*pair_cols[:4])
    shift = pair_cols[4:]
    firsts = [my_pair * IMG_DEV + first_local[e] for e in range(PAIR_DEV)]
    seconds = [owners[e] * IMG_DEV + second_local[e] for e in range(PAIR_DEV)]
    lean = [2.0 * sum(pair_rot[i][j] * shift[i] for i in range(3)) for j in range(3)]
    shift_sq = sum(shift[i] * shift[i] for i in range(3))
    first_row = (my_img * BAND_ROWS).astype(f32)
    ray_y0 = (first_row + 0.5 - ROWS / 2) / COLS
    ray_x = [((lane + 128 * part).astype(f32) + 0.5 - COLS / 2) / COLS for part in range(4)]

    def widen(step, carry):
        rows = pl.ds(pl.multiple_of(step * 64, 64), 64)
        conf_f[rows, :] = conf_ref[rows, :].astype(f32)
        return carry

    conf_load.wait()
    lax.fori_loop(0, PAIR_DEV * 2 * GROUPS // 64, widen, 0)
    second_load.wait()

    def prepare(view, images, stage):
        cols = [column([image_pose[i, images[e]] for e in range(PAIR_DEV)]) for i in range(7)]
        rot = rotation(*cols[:4])
        trans = cols[4:]
        both = [[sum(rot[l][i] * pair_rot[l][j] for l in range(3)) for j in range(3)] for i in range(3)]
        moved = [sum(rot[l][i] * shift[l] for l in range(3)) for i in range(3)]
        full = [[both[i][0], both[i][1], both[i][2], moved[i]] for i in range(3)]
        base = [[ray_x[part] * full[0][j] + (full[2][j] + ray_y0 * full[1][j]) for part in range(4)] for j in range(4)]
        slope = [full[1][j] * (1.0 / COLS) for j in range(4)]
        toward = [sum(trans[l] * pair_rot[l][j] for l in range(3)) for j in range(3)]
        offset = sum(trans[l] * shift[l] for l in range(3))

        def body(r, carry):
            total_sq, total_dot, total_conf, largest = carry
            down = r.astype(f32)
            tilt = [slope[j] * down for j in range(4)]
            for part in range(4):
                at = pl.ds(pl.multiple_of(r * COLS + part * 128, 128), 128)
                x = [points_ref[3 * view + j, :, at].astype(f32) for j in range(3)]
                weight = conf_f[pl.ds((r * 4 + part) * 2 + view, 8, stride=2 * GROUPS), :]
                value = base[3][part] + tilt[3]
                for j in range(3):
                    value = value + (base[j][part] + tilt[j]) * x[j]
                value = value * weight
                largest = jnp.maximum(largest, jnp.abs(value))
                stage[pl.ds(pl.multiple_of((r * 4 + part) * 8, 8), 8), :] = value
                square = x[0] * (x[0] + lean[0]) + x[1] * (x[1] + lean[1]) + x[2] * (x[2] + lean[2])
                dot = x[0] * toward[0] + x[1] * toward[1] + x[2] * toward[2]
                total_sq = total_sq + weight * square
                total_dot = total_dot + weight * dot
                total_conf = total_conf + weight
            return (total_sq, total_dot, total_conf, largest)

        def run(half, sums):
            tiny = jnp.full((8, 128), 1e-30, f32)
            start = half * (BAND_ROWS // 2)
            out = lax.fori_loop(start, start + BAND_ROWS // 2, body, (*sums, tiny))
            return out[:3], out[3]

        def close(sums):
            return (sums[0] + sums[2] * shift_sq, sums[1] + sums[2] * offset)

        return run, close

    empty = (jnp.zeros((8, 128), f32),) * 3
    code_one = (code_one_a, code_one_b)
    unit_one = (unit_one_a, unit_one_b)
    run_two, close_two = prepare(1, seconds, stage_two)

    def encode(half, largest):
        unit_one[half][0] = largest * (1.0 / LEVELS)
        inverse_ref[...] = LEVELS / largest

        def body(e, carry):
            inverse = inverse_ref[pl.ds(e, 1), :]
            for step in range(HALF // 16):
                place = half * (HALF // 16) + step
                rows = slice(step * 16, step * 16 + 16)
                value = stage_two[pl.ds(place * 128 + e, 16, stride=8), :] * inverse
                code_one[half][0, e, rows, :] = jnp.floor(value + 0.5).astype(jnp.int32).astype(jnp.int16)
                weight = conf_f[pl.ds(e * 2 * GROUPS + place * 32 + 1, 16, stride=2), :] * 128.0
                rows = slice(HALF + step * 16, HALF + step * 16 + 16)
                code_one[half][0, e, rows, :] = weight.astype(jnp.int32).astype(jnp.int16)
            return carry

        lax.fori_loop(0, PAIR_DEV, body, 0)

    def ahead(axis, d):
        if axis == 0:
            return (my_img, ys[d] * ZS + my_z)
        return (my_img, my_y * ZS + zs[d])

    def bulk_copies(phase, half, d):
        if phase == 0:
            refs = (code_one[half], unit_one[half])
        else:
            refs = (code_two.at[half], unit_two.at[half])
        axis = half if phase == 0 else 1 - half
        source = 0 if phase == 0 else d
        landing = d if phase == 0 else OWN_STEPS + d
        sems = (phase * 2 + half) * 4 + d
        return [
            pltpu.make_async_remote_copy(
                src_ref=ref.at[source],
                dst_ref=ref.at[landing],
                send_sem=send_sem.at[n, sems],
                recv_sem=recv_sem.at[n, sems],
                device_id=ahead(axis, d),
                device_id_type=MESH,
            )
            for n, ref in enumerate(refs)
        ]

    sums, largest = run_two(0, empty)
    encode(0, largest)
    pl.semaphore_wait(barrier, CHIPS)
    for d in STEPS:
        for copy in bulk_copies(0, 0, d):
            copy.start()

    def meta_copy(k):
        return pltpu.make_async_remote_copy(
            src_ref=meta.at[0],
            dst_ref=meta.at[k],
            send_sem=meta_send.at[k],
            recv_sem=meta_recv.at[k],
            device_id=(my_img, pair_at(k, 1)),
            device_id_type=MESH,
        )

    def start_meta(k, carry):
        meta_copy(k).start()
        return carry

    lax.fori_loop(1, OWNERS, start_meta, 0)
    sums, largest = run_two(1, sums)
    encode(1, largest)
    for d in STEPS:
        for copy in bulk_copies(0, 1, d):
            copy.start()
    square_two, dot_two = close_two(sums)
    first_load.wait()
    run_one, close_one = prepare(0, firsts, stage_one)
    sums, largest = run_one(0, empty)
    sums, largest = run_one(1, sums)
    square_one, dot_one = close_one(sums)

    def depth_of(values):
        return jnp.exp(values.astype(jnp.bfloat16).astype(f32))

    def image_rows(block, v):
        return pl.ds(block * 32 + v, 8, stride=IMG_DEV)

    def block_rows(block):
        return pl.ds(pl.multiple_of(block * 8, 8), 8)

    def first_depth(block, carry):
        for v in range(IMG_DEV):
            value = log_ref[image_rows(block, v), :]
            state_ref[0, v, block_rows(block), :] = value
            depth_ref[v, block_rows(block), :] = depth_of(value)
        return carry

    log_load.wait()
    lax.fori_loop(0, BLOCKS, first_depth, 0)
    for copy in state_loads:
        copy.wait()

    def fold_moments(block, carry):
        for v in range(IMG_DEV):
            state_ref[1, v, block_rows(block), :] = one_ref[image_rows(block, v), :]
            state_ref[2, v, block_rows(block), :] = two_ref[image_rows(block, v), :]
        return carry

    lax.fori_loop(0, BLOCKS, fold_moments, 0)

    own = [[image_pose[i, my_pair * IMG_DEV + min(v, IMG_DEV - 1)] for v in range(8)] for i in range(7)]
    own_cols = [column(own[i]) for i in range(7)]
    own_rot = rotation(*own_cols[:4])
    for i in range(3):
        tau_ref[i] = sum(own_rot[l][i] * own_cols[4 + l] for l in range(3))

    for k in range(1, OWNERS):
        meta_copy(k).wait_recv()
    known = meta[0]
    for k in range(1, OWNERS):
        known = known + meta[k]
    code_row = jnp.broadcast_to(known[0:1], (8, 128))
    local_row = jnp.broadcast_to(known[1:2], (8, 128))
    from_pair = lane // PAIR_DEV
    step_of = ((my_y - from_pair // ZS + YS) % YS) * ZS + (my_z - from_pair % ZS + ZS) % ZS
    slot_of = jnp.where(code_row // MOST == my_pair, step_of * MOST + code_row % MOST, -1)
    local_first = jnp.zeros((8, 128), jnp.int32)
    for e in range(PAIR_DEV):
        local_first = jnp.where(sub == e, first_local[e], local_first)
    own_mask = jnp.where(lane == my_pair * PAIR_DEV + sub, 1.0, 0.0)
    mask_ref[0:8, :] = own_mask
    for v in range(IMG_DEV):
        hot_ref[v, 0:8, :] = jnp.where(local_first == v, 1.0, 0.0)
    for group in range(SLOTS // 8):
        rows = pl.ds(8 + group * 8, 8)
        held = slot_of == sub + group * 8
        mask_ref[rows, :] = jnp.where(held, 1.0, 0.0)
        for v in range(IMG_DEV):
            found = jnp.where(held & (local_row == v), 1.0, 0.0)
            hot_ref[v, rows, :] = jnp.broadcast_to(jnp.sum(found, axis=1, keepdims=True), (8, 128))

    image_row = jnp.zeros((8, 128), jnp.int32)
    for group in range(VIEWS // 8):
        if group == 0:
            image_col = local_first
        else:
            held = (slot_of == sub + (group - 1) * 8).astype(jnp.int32)
            image_col = jnp.sum(held * (local_row - IMG_DEV), axis=1, keepdims=True) + IMG_DEV
        found = jnp.where(lane == sub + group * 8, image_col, 0)
        image_row = image_row + jnp.broadcast_to(jnp.sum(found, axis=0, keepdims=True), (8, 128))
    order_row = jnp.zeros((8, 128), jnp.int32)
    listed = lane < VIEWS
    for group in range(VIEWS // 8):
        view = sub + group * 8
        found = jnp.where(lane == view, image_row, 0)
        image_col = jnp.sum(found, axis=1, keepdims=True)
        before = listed & ((image_row < image_col) | ((image_row == image_col) & (lane < view)))
        place = jnp.sum(before.astype(jnp.int32), axis=1, keepdims=True)
        found = jnp.where(lane == place, view, 0)
        order_row = order_row + jnp.broadcast_to(jnp.sum(found, axis=0, keepdims=True), (8, 128))
    end_row = jnp.zeros((8, 128), jnp.int32)
    for v in range(IMG_DEV):
        upto = (listed & (image_row <= v)).astype(jnp.int32)
        end_row = jnp.where(lane == v, jnp.sum(upto, axis=1, keepdims=True), end_row)
    image_row = jnp.minimum(image_row, IMG_DEV - 1)

    pass_row = jnp.zeros((8, 128), jnp.int32)
    for half in range(2):
        for d in range(4):
            if half == 0:
                goal = my_y * ZS + zs[d]
                source = ((my_y - sub // MOST + YS) % YS) * ZS + my_z
            else:
                goal = ys[d] * ZS + my_z
                source = my_y * ZS + (my_z - sub // MOST + ZS) % ZS
            match = (from_pair == source) & (code_row == goal * MOST + sub % MOST)
            chosen = jnp.sum(jnp.where(match, lane % PAIR_DEV, 0), axis=1, keepdims=True)
            found = jnp.where(lane == sub + (half * 4 + d) * 8, chosen, 0)
            pass_row = pass_row + jnp.broadcast_to(jnp.sum(found, axis=0, keepdims=True), (8, 128))
            for v in range(IMG_DEV):
                hot = jnp.where(match & (local_row == v), 1.0, 0.0)
                pass_hot[half * 4 + d, v] = jnp.broadcast_to(jnp.sum(hot, axis=1, keepdims=True), (8, 128))
    table_ref[...] = jnp.where(sub == 0, image_row, jnp.where(sub == 1, order_row, jnp.where(sub == 2, end_row, pass_row)))
    table_copy = pltpu.make_async_copy(table_ref, table, table_sem)
    table_copy.start()

    def first_copy(e, carry):
        for block in range(BLOCKS):
            cu_ref[e, block * 8 : block * 8 + 8, :] = stage_one[pl.ds(block * 64 + e, 8, stride=8), :]
        return carry

    lax.fori_loop(0, PAIR_DEV, first_copy, 0)
    table_copy.wait()

    def dot_view(r, carry):
        v = table[0, r]
        totals = [jnp.zeros((8, 128), f32) for n in range(PART)]
        for block in range(BLOCKS):
            rows = slice(block * 8, block * 8 + 8)
            totals[block % PART] = totals[block % PART] + cu_ref[r, rows, :] * depth_ref[v, rows, :]
        total = (totals[0] + totals[1]) + (totals[2] + totals[3])
        inner_ref[pl.ds(r, 1), :] = jnp.sum(total, axis=0, keepdims=True)
        return carry

    lax.fori_loop(0, PAIR_DEV, dot_view, 0)

    def first_sums(block, carry):
        sums = [jnp.zeros((8, 128), f32) for v in range(IMG_DEV)]
        for e in range(PAIR_DEV):
            weight = conf_f[pl.ds(e * 2 * GROUPS + block * 16, 8, stride=2), :]
            for v in range(IMG_DEV):
                sums[v] = sums[v] + weight * hot_ref[v, e : e + 1, :]
        for v in range(IMG_DEV):
            weight_sum[v, block_rows(block), :] = sums[v]
        return carry

    lax.fori_loop(0, BLOCKS, first_sums, 0)

    def pass_on(half, d):
        place = d if d > 0 else OWN_STEPS
        index = half * 4 + d
        sources = [table[3, index * 8 + n] for n in range(8)]
        hots = [[pass_hot[index, v, n : n + 1, :] for v in range(IMG_DEV)] for n in range(8)]
        for n in range(8):
            unit_two[half, place, n : n + 1, :] = unit_one[half][n // MOST, pl.ds(sources[n], 1), :]

        def body(step, carry):
            rows = pl.ds(pl.multiple_of(step * 16, 16), 16)
            weight_rows = pl.ds(pl.multiple_of(HALF + step * 16, 16), 16)
            totals = [jnp.zeros((16, 128), f32) for v in range(IMG_DEV)]
            for n in range(8):
                code_two[half, place, n, rows, :] = code_one[half][n // MOST, sources[n], rows, :]
                weight = code_one[half][n // MOST, sources[n], weight_rows, :].astype(jnp.int32).astype(f32)
                for v in range(IMG_DEV):
                    totals[v] = totals[v] + weight * hots[n][v]
            for v in range(IMG_DEV):
                code_two[half, place, 8 + v, rows, :] = totals[v].astype(jnp.int32).astype(jnp.int16)
            return carry

        lax.fori_loop(0, HALF // 16, body, 0)

    def take(half, d):
        place = OWN_STEPS + d
        slots = []
        for n in range(8):
            step = n // MOST * 4 + d if half == 0 else d * 4 + n // MOST
            slots.append(PAIR_DEV + step * MOST + n % MOST)
        units = [unit_two[half, place, n : n + 1, :] for n in range(8)]
        images = [table[0, slot] for slot in slots]

        def body(step, totals):
            totals = list(totals)
            rows = pl.ds(pl.multiple_of(step * 16, 16), 16)
            full = pl.ds(pl.multiple_of(half * HALF + step * 16, 16), 16)
            for n in range(8):
                cu = code_two[half, place, n, rows, :].astype(jnp.int32).astype(f32) * units[n]
                cu_ref[slots[n], full, :] = cu
                cu = cu * depth_ref[images[n], full, :]
                totals[n] = totals[n] + (cu[0:8] + cu[8:16])
            for v in range(IMG_DEV):
                weight = code_two[half, place, 8 + v, rows, :].astype(jnp.int32).astype(f32)
                weight_sum[v, full, :] = weight_sum[v, full, :] + weight * (1.0 / 128.0)
            return tuple(totals)

        totals = lax.fori_loop(0, HALF // 16, body, (jnp.zeros((8, 128), f32),) * 8)
        for n in range(8):
            total = jnp.sum(totals[n], axis=0, keepdims=True)
            row = slice(slots[n], slots[n] + 1)
            inner_ref[row, :] = inner_ref[row, :] + total

    inner_ref[PAIR_DEV:VIEWS, :] = jnp.zeros((SLOTS, 128), f32)
    for half in range(2):
        for d in STEPS:
            for copy in bulk_copies(0, half, d):
                copy.wait_recv()
        for d in STEPS:
            pass_on(half, d)
            for copy in bulk_copies(1, half, d):
                copy.start()
        pass_on(half, 0)
        take(half, 0)
    for half in range(2):
        for d in STEPS:
            for copy in bulk_copies(1, half, d):
                copy.wait_recv()
            take(half, d)

    def pair_row(col):
        return jnp.sum(jnp.sum(col, axis=1, keepdims=True) * own_mask, axis=0, keepdims=True)

    fixed_row = pair_row(dot_one + dot_two)
    square_row = pair_row(square_one + square_two)

    def core_copy(t):
        return pltpu.make_async_remote_copy(
            src_ref=core_buf.at[t, 0],
            dst_ref=core_buf.at[t, 1],
            send_sem=core_send.at[t],
            recv_sem=core_recv.at[t],
            device_id=(my_img + 1 - 2 * my_core, my_pair),
            device_id_type=MESH,
        )

    def chip_copy(t, n, arrival):
        a, b, c = offsets[n]
        pair = ys[b] * ZS + zs[c]
        place = xs[a] * OWNERS + pair if arrival else my_chip
        return pltpu.make_async_remote_copy(
            src_ref=chip_buf.at[t, place],
            dst_ref=chip_buf.at[t, place],
            send_sem=chip_send.at[t, n],
            recv_sem=chip_recv.at[t, place],
            device_id=(xs[a] * 2 + my_core, pair),
            device_id_type=MESH,
        )

    def sum_all(t, tile, beside):
        core_buf[t, 0] = tile
        core_copy(t).start()
        core_copy(t).wait_recv()
        chip_buf[t, my_chip] = tile + core_buf[t, 1]
        for n in range(CHIPS - 1):
            chip_copy(t, n, False).start()
        beside()
        for n in reversed(range(CHIPS - 1)):
            chip_copy(t, n, True).wait_recv()
        parts = [chip_buf[t, n] for n in range(CHIPS)]
        while len(parts) > 1:
            parts = [parts[n] + parts[n + 1] for n in range(0, len(parts), 2)]
        return parts[0]

    def stores(tile_id):
        rows = pl.ds(pl.multiple_of(tile_id * TILE * 32, 8), TILE * 32)
        pairs = [(log_ref, log_out), (one_ref, one_out), (two_ref, two_out)]
        return [
            pltpu.make_async_copy(a.at[rows], b.at[rows], store_sem.at[tile_id, n])
            for n, (a, b) in enumerate(pairs)
        ]

    scale_store = pltpu.make_async_copy(scale_ref, scale_out, load_sem.at[0])
    def ray_sums():
        def body(block, carry):
            down = (block * 2 + sub // 4).astype(f32) + first_row
            rays_y = (down + 0.5 - ROWS / 2) / COLS
            rays_x = (((sub % 4) * 128 + lane).astype(f32) + 0.5 - COLS / 2) / COLS
            length = rays_x * rays_x + rays_y * rays_y + 1.0
            rows = block_rows(block)
            for v in range(IMG_DEV):
                lever = rays_x * tau_ref[0, v : v + 1, :] + rays_y * tau_ref[1, v : v + 1, :] + tau_ref[2, v : v + 1, :]
                weight = weight_sum[v, rows, :]
                lever_sum[v, rows, :] = lever * weight
                weight_sum[v, rows, :] = length * weight
            return carry

        lax.fori_loop(0, BLOCKS, body, 0)

    denominator = None
    for sweep in range(ITERS):
        row = jnp.zeros((8, 128), f32)
        for group in range(VIEWS // 8):
            rows = slice(group * 8, group * 8 + 8)
            row = row + jnp.sum(inner_ref[rows, :], axis=1, keepdims=True) * mask_ref[rows, :]
        row = jnp.sum(row, axis=0, keepdims=True) + fixed_row
        two = lax.broadcasted_iota(jnp.int32, (2, 128), 0)
        total = sum_all(sweep, jnp.where(two == 0, row, square_row), ray_sums if sweep == 0 else lambda: None)
        if sweep == 0:
            denominator = total[1:2]
        scales = jnp.broadcast_to(total[0:1] / denominator, (8, 128))
        for group in range(VIEWS // 8):
            rows = slice(group * 8, group * 8 + 8)
            held = jnp.sum(scales * mask_ref[rows, :], axis=1, keepdims=True)
            if group == 0 and sweep == ITERS - 1:
                own_row = jnp.sum(jnp.where(lane == sub, held, 0.0), axis=0, keepdims=True)
                scale_ref[...] = own_row[:, 0:PAIR_DEV]
                scale_store.start()
            weight_ref[rows, :] = jnp.broadcast_to(held, (8, 128))

        steps = START + sweep + 1
        bias_one = 1 - beta_one**steps
        bias_two = 1 - beta_two**steps
        last = sweep == ITERS - 1

        def update(tile_id, carry):
            start = tile_id * TILE

            def gather(step, sums):
                sums = list(sums)
                for n in range(UNROLL):
                    q = step * UNROLL + n
                    r = table[1, q]
                    weight = weight_ref[pl.ds(r, 1), :]
                    for m in range(TILE):
                        sums[m] = sums[m] + cu_ref[r, block_rows(start + m), :] * weight
                        prefix_ref[q + 1, m * 8 : m * 8 + 8, :] = sums[m]
                return tuple(sums)

            zero = jnp.zeros((8, 128), f32)
            for m in range(TILE):
                prefix_ref[0, m * 8 : m * 8 + 8, :] = zero
            lax.fori_loop(0, VIEWS // UNROLL, gather, (zero,) * TILE)
            def step_adam(step, carry):
                for m in range(ADAM):
                    n = step * ADAM + m
                    block = start + n
                    here = pl.ds(pl.multiple_of(n * 8, 8), 8)
                    for v in range(IMG_DEV):
                        depth = depth_ref[v, block_rows(block), :]
                        gathered = prefix_ref[table[2, v], here, :]
                        if v > 0:
                            gathered = gathered - prefix_ref[table[2, v - 1], here, :]
                        pull = depth * weight_sum[v, block_rows(block), :] + lever_sum[v, block_rows(block), :] - gathered
                        half_gradient = depth * pull
                        rows = block_rows(block)
                        old_log, old_one, old_two = (state_ref[n, v, rows, :] for n in range(3))
                        new_one = beta_one * old_one + (2 * (1 - beta_one)) * half_gradient
                        new_two = beta_two * old_two + (4 * (1 - beta_two)) * (half_gradient * half_gradient)
                        corrected_two = new_two * (1 / bias_two)
                        root = corrected_two * lax.rsqrt(corrected_two) + adam_eps
                        inverse = pl.reciprocal(root, approx=True)
                        inverse = inverse * (2.0 - root * inverse)
                        new_log = old_log - (learn_rate / bias_one) * (new_one * inverse)
                        if last:
                            rows = image_rows(block, v)
                            log_ref[rows, :] = new_log
                            one_ref[rows, :] = new_one
                            two_ref[rows, :] = new_two
                        else:
                            state_ref[0, v, rows, :] = new_log
                            state_ref[1, v, rows, :] = new_one
                            state_ref[2, v, rows, :] = new_two
                            depth_ref[v, rows, :] = depth_of(new_log)
                return carry

            lax.fori_loop(0, TILE // ADAM, step_adam, 0)
            if last:
                for copy in stores(tile_id):
                    copy.start()
            return carry

        lax.fori_loop(0, BLOCKS // TILE, update, 0)
        if not last:
            lax.fori_loop(0, VIEWS, dot_view, 0)

    scale_store.wait()
    for tile_id in range(BLOCKS // TILE):
        for copy in stores(tile_id):
            copy.wait()

    def finish(k, carry):
        meta_copy(k).wait_send()
        return carry

    lax.fori_loop(1, OWNERS, finish, 0)
    for phase in range(2):
        for half in range(2):
            for d in STEPS:
                for copy in bulk_copies(phase, half, d):
                    copy.wait_send()
    for t in range(ITERS):
        core_copy(t).wait_send()
        for n in range(CHIPS - 1):
            chip_copy(t, n, False).wait_send()


def store(log_in, one_in, two_in, scale_in, log_out, one_out, two_out, scale_out, bands, scale, in_sem, out_sem):
    half = GROUPS * IMG_DEV // 2
    moves = [(scale_in, scale, scale_out)]
    for part in range(2):
        rows = pl.ds(part * half, half)
        for n, (a, b) in enumerate([(log_in, log_out), (one_in, one_out), (two_in, two_out)]):
            moves.append((a.at[rows], bands.at[n, rows], b.at[rows]))
    loads = [pltpu.make_async_copy(a, m, in_sem.at[n]) for n, (a, m, b) in enumerate(moves)]
    stores = [pltpu.make_async_copy(m, b, out_sem.at[n]) for n, (a, m, b) in enumerate(moves)]
    for copy in loads:
        copy.start()
    for arrived, copy in zip(loads, stores):
        arrived.wait()
        copy.start()
    for copy in stores:
        copy.wait()


def shards(
    log_depth,
    moment_one,
    moment_two,
    image_pose,
    pair_points,
    confidence,
    pair_pose,
    first_local,
    second_owner,
    second_local,
):
    def fold(a):
        return a.reshape(IMG_DEV, GROUPS, 128).transpose(1, 0, 2).reshape(GROUPS * IMG_DEV, 128)

    def unfold(a):
        return a.reshape(GROUPS, IMG_DEV, 128).transpose(1, 0, 2).reshape(IMG_DEV, BAND)

    points = pair_points.transpose(1, 0, 2)
    conf = confidence.reshape(PAIR_DEV, 2, GROUPS, 128).transpose(0, 2, 1, 3).reshape(PAIR_DEV * GROUPS * 2, 128)
    hbm = pl.BlockSpec(memory_space=pltpu.HBM)
    band = jax.ShapeDtypeStruct((GROUPS * IMG_DEV, 128), f32)
    dma = pltpu.SemaphoreType.DMA
    out = pl.pallas_call(
        kernel,
        out_shape=(band, band, band, jax.ShapeDtypeStruct((1, PAIR_DEV), f32)),
        in_specs=[hbm] * 10,
        out_specs=(hbm,) * 4,
        scratch_shapes=[
            pltpu.VMEM((1, PAIR_DEV), f32),
            pltpu.VMEM((GROUPS * IMG_DEV, 128), f32),
            pltpu.VMEM((GROUPS * IMG_DEV, 128), f32),
            pltpu.VMEM((GROUPS * IMG_DEV, 128), f32),
            pltpu.VMEM((6, PAIR_DEV, BAND), jnp.bfloat16),
            pltpu.VMEM((PAIR_DEV * GROUPS * 2, 128), jnp.bfloat16),
            pltpu.SMEM((7, IMG_DEV * OWNERS), f32),
            pltpu.SMEM((7, PAIR_DEV), f32),
            pltpu.SMEM((PAIR_DEV,), jnp.int32),
            pltpu.SMEM((PAIR_DEV,), jnp.int32),
            pltpu.SMEM((PAIR_DEV,), jnp.int32),
            pltpu.VMEM((PAIR_DEV * GROUPS * 2, 128), f32),
            pltpu.VMEM((PAIR_DEV * GROUPS, 128), f32),
            pltpu.VMEM((PAIR_DEV * GROUPS, 128), f32),
            pltpu.VMEM((4, PAIR_DEV, 2 * HALF, 128), jnp.int16),
            pltpu.VMEM((4, PAIR_DEV, 2 * HALF, 128), jnp.int16),
            pltpu.VMEM((4, PAIR_DEV, 128), f32),
            pltpu.VMEM((4, PAIR_DEV, 128), f32),
            pltpu.VMEM((PAIR_DEV, 128), f32),
            pltpu.VMEM((2, 2 * OWN_STEPS, 8 + IMG_DEV, HALF, 128), jnp.int16),
            pltpu.VMEM((2, 2 * OWN_STEPS, 8, 128), f32),
            pltpu.VMEM((8, IMG_DEV, 8, 128), f32),
            pltpu.VMEM((OWNERS, 8, 128), jnp.int32),
            pltpu.VMEM((VIEWS, GROUPS, 128), f32),
            pltpu.VMEM((VIEWS + 1, TILE * 8, 128), f32),
            pltpu.VMEM((3, IMG_DEV, GROUPS, 128), f32),
            pltpu.VMEM((IMG_DEV, GROUPS, 128), f32),
            pltpu.VMEM((IMG_DEV, GROUPS, 128), f32),
            pltpu.VMEM((IMG_DEV, GROUPS, 128), f32),
            pltpu.VMEM((3, 8, 128), f32),
            pltpu.VMEM((IMG_DEV, VIEWS, 128), f32),
            pltpu.VMEM((VIEWS, 128), f32),
            pltpu.VMEM((VIEWS, 128), f32),
            pltpu.VMEM((VIEWS, 128), f32),
            pltpu.VMEM((ITERS, 2, 2, 128), f32),
            pltpu.VMEM((ITERS, CHIPS, 2, 128), f32),
            pltpu.VMEM((8, 128), jnp.int32),
            pltpu.SMEM((8, 128), jnp.int32),
            dma((11,)),
            dma((BLOCKS // TILE, 3)),
            dma,
            dma((2, 16)),
            dma((2, 16)),
            dma((OWNERS,)),
            dma((OWNERS,)),
            dma((ITERS,)),
            dma((ITERS,)),
            dma((ITERS, CHIPS)),
            dma((ITERS, CHIPS)),
        ],
        compiler_params=pltpu.CompilerParams(
            collective_id=0, has_side_effects=True, vmem_limit_bytes=60 * 2**20
        ),
        name="align",
    )(
        fold(log_depth),
        fold(moment_one),
        fold(moment_two),
        points,
        conf,
        image_pose,
        pair_pose,
        first_local,
        second_owner.reshape(PAIR_DEV),
        second_local,
    )
    out = pl.pallas_call(
        store,
        out_shape=(band, band, band, jax.ShapeDtypeStruct((1, PAIR_DEV), f32)),
        in_specs=[hbm] * 4,
        out_specs=(hbm,) * 4,
        scratch_shapes=[
            pltpu.VMEM((3, GROUPS * IMG_DEV, 128), f32),
            pltpu.VMEM((1, PAIR_DEV), f32),
            dma((7,)),
            dma((7,)),
        ],
        compiler_params=pltpu.CompilerParams(vmem_limit_bytes=60 * 2**20),
        name="store",
    )(*out)
    return (unfold(out[0]), unfold(out[1]), unfold(out[2]), out[3].reshape(PAIR_DEV))


def solution(mesh):
    return jax.shard_map(
        shards,
        mesh=mesh,
        in_specs=(
            P("pair", "img"),
            P("pair", "img"),
            P("pair", "img"),
            P(),
            P("pair", None, "img"),
            P("pair", None, "img"),
            P(None, "pair"),
            P("pair"),
            P("pair", None),
            P("pair"),
        ),
        out_specs=(P("pair", "img"), P("pair", "img"), P("pair", "img"), P("pair")),
        check_vma=False,
    )
```

```python
import jax
import jax.numpy as jnp
from jax import lax
from jax.experimental import pallas as pl
from jax.experimental.pallas import tpu as pltpu
from jax.sharding import PartitionSpec as P

ROWS = 384
COLS = 512
ITERS = 3
START = 100
IMG_DEV = 4
PAIR_DEV = 8
MOST = 2
IMGS = 8
OWNERS = 16
XS = 4
YS = 4
ZS = 4
CHIPS = XS * YS * ZS
BAND = ROWS * COLS // IMGS
GROUPS = BAND // 128
BLOCKS = GROUPS // 8
BAND_ROWS = ROWS // IMGS
SLOTS = OWNERS * MOST
VIEWS = PAIR_DEV + SLOTS
UNITS = 4
CHUNK = GROUPS // UNITS
UNIT_ROWS = BAND_ROWS // UNITS
OWN_STEPS = 4
STEPS = (2, 1, 3)
TILE = 12
PART = 4
ADAM = 6
UNROLL = 4
LEVELS = 32700.0

beta_one = 0.9
beta_two = 0.999
learn_rate = 0.01
adam_eps = 1e-08
f32 = jnp.float32
MESH = pl.DeviceIdType.MESH


def rotation(scalar_q, vec_a, vec_b, vec_c):
    magnitude = jnp.sqrt(scalar_q * scalar_q + vec_a * vec_a + vec_b * vec_b + vec_c * vec_c)
    unit_s = scalar_q / magnitude
    unit_a = vec_a / magnitude
    unit_b = vec_b / magnitude
    unit_c = vec_c / magnitude
    return (
        (
            1 - 2 * (unit_b * unit_b + unit_c * unit_c),
            2 * (unit_a * unit_b - unit_s * unit_c),
            2 * (unit_a * unit_c + unit_s * unit_b),
        ),
        (
            2 * (unit_a * unit_b + unit_s * unit_c),
            1 - 2 * (unit_a * unit_a + unit_c * unit_c),
            2 * (unit_b * unit_c - unit_s * unit_a),
        ),
        (
            2 * (unit_a * unit_c - unit_s * unit_b),
            2 * (unit_b * unit_c + unit_s * unit_a),
            1 - 2 * (unit_a * unit_a + unit_b * unit_b),
        ),
    )


def kernel(
    log_hbm,
    one_hbm,
    two_hbm,
    points_hbm,
    conf_hbm,
    image_pose_hbm,
    pair_pose_hbm,
    first_local_hbm,
    second_owner_hbm,
    second_local_hbm,
    log_out,
    one_out,
    two_out,
    scale_out,
    scale_ref,
    log_ref,
    one_ref,
    two_ref,
    points_ref,
    conf_ref,
    image_pose,
    pair_pose,
    first_local,
    second_owner,
    second_local,
    conf_f,
    stage_one,
    stage_two,
    code_one_a,
    code_one_b,
    code_one_c,
    code_one_d,
    unit_one_a,
    unit_one_b,
    unit_one_c,
    unit_one_d,
    inverse_ref,
    code_two,
    unit_two,
    part_ref,
    pass_hot,
    meta,
    cu_ref,
    prefix_ref,
    state_ref,
    weight_sum,
    lever_sum,
    depth_ref,
    tau_ref,
    hot_ref,
    mask_ref,
    weight_ref,
    inner_ref,
    core_buf,
    chip_buf,
    table_ref,
    table,
    load_sem,
    store_sem,
    table_sem,
    one_send,
    one_recv,
    scale_send,
    scale_recv,
    two_send,
    two_recv,
    pass_send,
    pass_recv,
    meta_send,
    meta_recv,
    core_send,
    core_recv,
    chip_send,
    chip_recv,
):
    def load(n, src, dst):
        copy = pltpu.make_async_copy(src, dst, load_sem.at[n])
        copy.start()
        return copy

    small = [
        load(0, second_owner_hbm, second_owner),
        load(1, second_local_hbm, second_local),
        load(2, first_local_hbm, first_local),
        load(3, pair_pose_hbm, pair_pose),
        load(4, image_pose_hbm, image_pose),
    ]
    conf_load = load(5, conf_hbm, conf_ref)
    second_load = load(6, points_hbm.at[pl.ds(3, 3)], points_ref.at[pl.ds(3, 3)])
    first_load = load(7, points_hbm.at[pl.ds(0, 3)], points_ref.at[pl.ds(0, 3)])
    log_load = load(8, log_hbm, log_ref)
    state_loads = [load(9, one_hbm, one_ref), load(10, two_hbm, two_ref)]

    my_img = lax.axis_index("img")
    my_pair = lax.axis_index("pair")
    my_y = my_pair // ZS
    my_z = my_pair % ZS

    def pair_at(k, sign):
        return ((my_y + sign * (k // ZS) + YS) % YS) * ZS + (my_z + sign * (k % ZS) + ZS) % ZS

    barrier = pltpu.get_barrier_semaphore()

    my_x = my_img // 2
    my_core = my_img % 2
    my_chip = my_x * OWNERS + my_pair
    xs = [(my_x + d) % XS for d in range(XS)]
    ys = [(my_y + d) % YS for d in range(YS)]
    zs = [(my_z + d) % ZS for d in range(ZS)]
    offsets = [(a, b, c) for a in range(XS) for b in range(YS) for c in range(ZS) if (a, b, c) != (0, 0, 0)]
    offsets.sort(key=lambda o: -sum(min(d, 4 - d) for d in o))

    def greet_chip(k, carry):
        x = (my_x + k // OWNERS) % XS
        y = (my_y + k // ZS) % YS
        z = (my_z + k) % ZS
        pl.semaphore_signal(barrier, 1, device_id=(x * 2 + my_core, y * ZS + z), device_id_type=MESH)
        return carry

    pl.semaphore_signal(barrier, 1, device_id=(my_img + 1 - 2 * my_core, my_pair), device_id_type=MESH)
    lax.fori_loop(1, CHIPS, greet_chip, 0)

    sub = lax.broadcasted_iota(jnp.int32, (8, 128), 0)
    lane = lax.broadcasted_iota(jnp.int32, (8, 128), 1)

    for copy in small:
        copy.wait()

    owners = [second_owner[e] for e in range(PAIR_DEV)]
    order = []
    for e in range(PAIR_DEV):
        rank = jnp.int32(0)
        for other in range(e):
            rank = rank + jnp.where(owners[other] == owners[e], 1, 0)
        order.append(owners[e] * MOST + rank)
    row = jnp.zeros((8, 128), jnp.int32)
    for e in range(PAIR_DEV):
        here = lane == my_pair * PAIR_DEV + e
        row = jnp.where(here & (sub == 0), order[e], row)
        row = jnp.where(here & (sub == 1), second_local[e], row)
    meta[0] = row

    def column(values):
        out = jnp.zeros((8, 128), f32)
        for e in range(PAIR_DEV):
            out = jnp.where(sub == e, values[e], out)
        return out

    pair_cols = [column([pair_pose[i, e] for e in range(PAIR_DEV)]) for i in range(7)]
    pair_rot = rotation(*pair_cols[:4])
    shift = pair_cols[4:]
    firsts = [my_pair * IMG_DEV + first_local[e] for e in range(PAIR_DEV)]
    seconds = [owners[e] * IMG_DEV + second_local[e] for e in range(PAIR_DEV)]
    lean = [2.0 * sum(pair_rot[i][j] * shift[i] for i in range(3)) for j in range(3)]
    shift_sq = sum(shift[i] * shift[i] for i in range(3))
    first_row = (my_img * BAND_ROWS).astype(f32)
    ray_y0 = (first_row + 0.5 - ROWS / 2) / COLS
    ray_x = [((lane + 128 * part).astype(f32) + 0.5 - COLS / 2) / COLS for part in range(4)]

    def widen(step, carry):
        rows = pl.ds(pl.multiple_of(step * 64, 64), 64)
        conf_f[rows, :] = conf_ref[rows, :].astype(f32)
        return carry

    conf_load.wait()
    lax.fori_loop(0, PAIR_DEV * 2 * GROUPS // 64, widen, 0)
    second_load.wait()

    def prepare(view, images, stage):
        cols = [column([image_pose[i, images[e]] for e in range(PAIR_DEV)]) for i in range(7)]
        rot = rotation(*cols[:4])
        trans = cols[4:]
        both = [[sum(rot[l][i] * pair_rot[l][j] for l in range(3)) for j in range(3)] for i in range(3)]
        moved = [sum(rot[l][i] * shift[l] for l in range(3)) for i in range(3)]
        full = [[both[i][0], both[i][1], both[i][2], moved[i]] for i in range(3)]
        base = [[ray_x[part] * full[0][j] + (full[2][j] + ray_y0 * full[1][j]) for part in range(4)] for j in range(4)]
        slope = [full[1][j] * (1.0 / COLS) for j in range(4)]
        toward = [sum(trans[l] * pair_rot[l][j] for l in range(3)) for j in range(3)]
        offset = sum(trans[l] * shift[l] for l in range(3))

        def body(r, carry):
            total_sq, total_dot, total_conf, largest = carry
            down = r.astype(f32)
            tilt = [slope[j] * down for j in range(4)]
            for part in range(4):
                at = pl.ds(pl.multiple_of(r * COLS + part * 128, 128), 128)
                x = [points_ref[3 * view + j, :, at].astype(f32) for j in range(3)]
                weight = conf_f[pl.ds((r * 4 + part) * 2 + view, 8, stride=2 * GROUPS), :]
                value = base[3][part] + tilt[3]
                for j in range(3):
                    value = value + (base[j][part] + tilt[j]) * x[j]
                value = value * weight
                largest = jnp.maximum(largest, jnp.abs(value))
                stage[pl.ds(pl.multiple_of((r * 4 + part) * 8, 8), 8), :] = value
                square = x[0] * (x[0] + lean[0]) + x[1] * (x[1] + lean[1]) + x[2] * (x[2] + lean[2])
                dot = x[0] * toward[0] + x[1] * toward[1] + x[2] * toward[2]
                total_sq = total_sq + weight * square
                total_dot = total_dot + weight * dot
                total_conf = total_conf + weight
            return (total_sq, total_dot, total_conf, largest)

        def run(unit, sums):
            tiny = jnp.full((8, 128), 1e-30, f32)
            start = unit * UNIT_ROWS
            out = lax.fori_loop(start, start + UNIT_ROWS, body, (*sums, tiny))
            return out[:3], out[3]

        def close(sums):
            return (sums[0] + sums[2] * shift_sq, sums[1] + sums[2] * offset)

        return run, close

    empty = (jnp.zeros((8, 128), f32),) * 3
    code_one = (code_one_a, code_one_b, code_one_c, code_one_d)
    unit_one = (unit_one_a, unit_one_b, unit_one_c, unit_one_d)
    run_two, close_two = prepare(1, seconds, stage_two)

    def encode(unit, largest):
        unit_one[unit][0] = largest * (1.0 / LEVELS)
        inverse_ref[...] = LEVELS / largest

        def body(e, carry):
            inverse = inverse_ref[pl.ds(e, 1), :]
            for step in range(CHUNK // 16):
                place = unit * (CHUNK // 16) + step
                rows = slice(step * 16, step * 16 + 16)
                value = stage_two[pl.ds(place * 128 + e, 16, stride=8), :] * inverse
                code_one[unit][0, e, rows, :] = jnp.floor(value + 0.5).astype(jnp.int32).astype(jnp.int16)
                weight = conf_f[pl.ds(e * 2 * GROUPS + place * 32 + 1, 16, stride=2), :] * 128.0
                rows = slice(CHUNK + step * 16, CHUNK + step * 16 + 16)
                code_one[unit][0, e, rows, :] = weight.astype(jnp.int32).astype(jnp.int16)
            return carry

        lax.fori_loop(0, PAIR_DEV, body, 0)

    def ahead(axis, d):
        if axis == 0:
            return (my_img, ys[d] * ZS + my_z)
        return (my_img, my_y * ZS + zs[d])

    def remote(src, dst, sems, place, device):
        return pltpu.make_async_remote_copy(
            src_ref=src,
            dst_ref=dst,
            send_sem=sems[0].at[place],
            recv_sem=sems[1].at[place],
            device_id=device,
            device_id_type=MESH,
        )

    def near_copies(unit):
        return [
            remote(code_one[unit].at[0], code_one[unit].at[d], (one_send, one_recv), unit * 4 + d, ahead(unit % 2, d))
            for d in (1, 3)
        ]

    def far_copies(unit):
        half = PAIR_DEV // 2
        return [
            remote(
                code_one[unit].at[d, part], code_one[unit].at[2, part], (one_send, one_recv), unit * 4 + n, ahead(unit % 2, d)
            )
            for d, n, part in ((1, 0, pl.ds(0, half)), (3, 2, pl.ds(half, half)))
        ]

    def scale_copies(unit):
        return [
            remote(unit_one[unit].at[0], unit_one[unit].at[d], (scale_send, scale_recv), unit * 4 + d, ahead(unit % 2, d))
            for d in STEPS
        ]

    def slot_copies(unit, d):
        place = unit * 4 + d
        to = ahead(1 - unit % 2, d)
        return [
            remote(code_two.at[unit, d], code_two.at[unit, OWN_STEPS + d], (two_send, two_recv), place, to),
            remote(unit_two.at[unit, d], unit_two.at[unit, OWN_STEPS + d], (pass_send, pass_recv), place, to),
        ]

    def send(unit, sums):
        sums, largest = run_two(unit, sums)
        encode(unit, largest)
        if unit == 0:
            pl.semaphore_wait(barrier, CHIPS)
        for copy in near_copies(unit) + scale_copies(unit):
            copy.start()
        return sums

    def hand_on(unit):
        for arrived, copy in zip(near_copies(unit), far_copies(unit)):
            arrived.wait_recv()
            copy.start()

    sums = send(0, empty)

    def meta_copy(k):
        return pltpu.make_async_remote_copy(
            src_ref=meta.at[0],
            dst_ref=meta.at[k],
            send_sem=meta_send.at[k],
            recv_sem=meta_recv.at[k],
            device_id=(my_img, pair_at(k, 1)),
            device_id_type=MESH,
        )

    def start_meta(k, carry):
        meta_copy(k).start()
        return carry

    lax.fori_loop(1, OWNERS, start_meta, 0)
    for unit in range(1, UNITS):
        sums = send(unit, sums)
    square_two, dot_two = close_two(sums)
    first_load.wait()
    run_one, close_one = prepare(0, firsts, stage_one)
    sums = empty
    for unit in range(UNITS):
        sums, largest = run_one(unit, sums)
    square_one, dot_one = close_one(sums)

    def depth_of(values):
        return jnp.exp(values.astype(jnp.bfloat16).astype(f32))

    def image_rows(block, v):
        return pl.ds(block * 32 + v, 8, stride=IMG_DEV)

    def block_rows(block):
        return pl.ds(pl.multiple_of(block * 8, 8), 8)

    def first_depth(block, carry):
        for v in range(IMG_DEV):
            value = log_ref[image_rows(block, v), :]
            state_ref[0, v, block_rows(block), :] = value
            depth_ref[v, block_rows(block), :] = depth_of(value)
        return carry

    log_load.wait()
    lax.fori_loop(0, BLOCKS, first_depth, 0)
    for copy in state_loads:
        copy.wait()

    def fold_moments(block, carry):
        for v in range(IMG_DEV):
            state_ref[1, v, block_rows(block), :] = one_ref[image_rows(block, v), :]
            state_ref[2, v, block_rows(block), :] = two_ref[image_rows(block, v), :]
        return carry

    lax.fori_loop(0, BLOCKS, fold_moments, 0)

    for unit in range(min(2, UNITS)):
        hand_on(unit)

    own = [[image_pose[i, my_pair * IMG_DEV + min(v, IMG_DEV - 1)] for v in range(8)] for i in range(7)]
    own_cols = [column(own[i]) for i in range(7)]
    own_rot = rotation(*own_cols[:4])
    for i in range(3):
        tau_ref[i] = sum(own_rot[l][i] * own_cols[4 + l] for l in range(3))

    for k in range(1, OWNERS):
        meta_copy(k).wait_recv()
    known = meta[0]
    for k in range(1, OWNERS):
        known = known + meta[k]
    code_row = jnp.broadcast_to(known[0:1], (8, 128))
    local_row = jnp.broadcast_to(known[1:2], (8, 128))
    from_pair = lane // PAIR_DEV
    step_of = ((my_y - from_pair // ZS + YS) % YS) * ZS + (my_z - from_pair % ZS + ZS) % ZS
    slot_of = jnp.where(code_row // MOST == my_pair, step_of * MOST + code_row % MOST, -1)
    local_first = jnp.zeros((8, 128), jnp.int32)
    for e in range(PAIR_DEV):
        local_first = jnp.where(sub == e, first_local[e], local_first)
    own_mask = jnp.where(lane == my_pair * PAIR_DEV + sub, 1.0, 0.0)
    mask_ref[0:8, :] = own_mask
    for v in range(IMG_DEV):
        hot_ref[v, 0:8, :] = jnp.where(local_first == v, 1.0, 0.0)
    for group in range(SLOTS // 8):
        rows = pl.ds(8 + group * 8, 8)
        held = slot_of == sub + group * 8
        mask_ref[rows, :] = jnp.where(held, 1.0, 0.0)
        for v in range(IMG_DEV):
            found = jnp.where(held & (local_row == v), 1.0, 0.0)
            hot_ref[v, rows, :] = jnp.broadcast_to(jnp.sum(found, axis=1, keepdims=True), (8, 128))

    image_row = jnp.zeros((8, 128), jnp.int32)
    for group in range(VIEWS // 8):
        if group == 0:
            image_col = local_first
        else:
            held = (slot_of == sub + (group - 1) * 8).astype(jnp.int32)
            image_col = jnp.sum(held * (local_row - IMG_DEV), axis=1, keepdims=True) + IMG_DEV
        found = jnp.where(lane == sub + group * 8, image_col, 0)
        image_row = image_row + jnp.broadcast_to(jnp.sum(found, axis=0, keepdims=True), (8, 128))
    order_row = jnp.zeros((8, 128), jnp.int32)
    listed = lane < VIEWS
    for group in range(VIEWS // 8):
        view = sub + group * 8
        found = jnp.where(lane == view, image_row, 0)
        image_col = jnp.sum(found, axis=1, keepdims=True)
        before = listed & ((image_row < image_col) | ((image_row == image_col) & (lane < view)))
        place = jnp.sum(before.astype(jnp.int32), axis=1, keepdims=True)
        found = jnp.where(lane == place, view, 0)
        order_row = order_row + jnp.broadcast_to(jnp.sum(found, axis=0, keepdims=True), (8, 128))
    end_row = jnp.zeros((8, 128), jnp.int32)
    for v in range(IMG_DEV):
        upto = (listed & (image_row <= v)).astype(jnp.int32)
        end_row = jnp.where(lane == v, jnp.sum(upto, axis=1, keepdims=True), end_row)
    image_row = jnp.minimum(image_row, IMG_DEV - 1)

    pass_row = jnp.zeros((8, 128), jnp.int32)
    for half in range(2):
        for d in range(4):
            if half == 0:
                goal = my_y * ZS + zs[d]
                source = ((my_y - sub // MOST + YS) % YS) * ZS + my_z
            else:
                goal = ys[d] * ZS + my_z
                source = my_y * ZS + (my_z - sub // MOST + ZS) % ZS
            match = (from_pair == source) & (code_row == goal * MOST + sub % MOST)
            chosen = jnp.sum(jnp.where(match, lane % PAIR_DEV, 0), axis=1, keepdims=True)
            found = jnp.where(lane == sub + (half * 4 + d) * 8, chosen, 0)
            pass_row = pass_row + jnp.broadcast_to(jnp.sum(found, axis=0, keepdims=True), (8, 128))
            for v in range(IMG_DEV):
                hot = jnp.where(match & (local_row == v), 1.0, 0.0)
                pass_hot[half * 4 + d, v] = jnp.broadcast_to(jnp.sum(hot, axis=1, keepdims=True), (8, 128))
    table_ref[...] = jnp.where(sub == 0, image_row, jnp.where(sub == 1, order_row, jnp.where(sub == 2, end_row, pass_row)))
    table_copy = pltpu.make_async_copy(table_ref, table, table_sem)
    table_copy.start()

    def first_copy(e, carry):
        for block in range(BLOCKS):
            cu_ref[e, block * 8 : block * 8 + 8, :] = stage_one[pl.ds(block * 64 + e, 8, stride=8), :]
        return carry

    lax.fori_loop(0, PAIR_DEV, first_copy, 0)
    table_copy.wait()

    def dot_view(r, carry):
        v = table[0, r]
        totals = [jnp.zeros((8, 128), f32) for n in range(PART)]
        for block in range(BLOCKS):
            rows = slice(block * 8, block * 8 + 8)
            totals[block % PART] = totals[block % PART] + cu_ref[r, rows, :] * depth_ref[v, rows, :]
        total = (totals[0] + totals[1]) + (totals[2] + totals[3])
        inner_ref[pl.ds(r, 1), :] = jnp.sum(total, axis=0, keepdims=True)
        return carry

    lax.fori_loop(0, PAIR_DEV, dot_view, 0)

    def first_sums(block, carry):
        sums = [jnp.zeros((8, 128), f32) for v in range(IMG_DEV)]
        for e in range(PAIR_DEV):
            weight = conf_f[pl.ds(e * 2 * GROUPS + block * 16, 8, stride=2), :]
            for v in range(IMG_DEV):
                sums[v] = sums[v] + weight * hot_ref[v, e : e + 1, :]
        for v in range(IMG_DEV):
            weight_sum[v, block_rows(block), :] = sums[v]
        return carry

    lax.fori_loop(0, BLOCKS, first_sums, 0)

    def pass_on(unit, d):
        place = d if d > 0 else OWN_STEPS
        index = unit % 2 * 4 + d
        sources = [table[3, index * 8 + n] for n in range(8)]
        hots = [[pass_hot[index, v, n : n + 1, :] for v in range(IMG_DEV)] for n in range(8)]
        for n in range(8):
            unit_two[unit, place, n : n + 1, :] = unit_one[unit][n // MOST, pl.ds(sources[n], 1), :]

        def body(step, carry):
            rows = pl.ds(pl.multiple_of(step * 16, 16), 16)
            weight_rows = pl.ds(pl.multiple_of(CHUNK + step * 16, 16), 16)
            totals = [jnp.zeros((16, 128), f32) for v in range(IMG_DEV)]
            for n in range(8):
                code_two[unit, place, n, rows, :] = code_one[unit][n // MOST, sources[n], rows, :]
                weight = code_one[unit][n // MOST, sources[n], weight_rows, :].astype(jnp.int32).astype(f32)
                for v in range(IMG_DEV):
                    totals[v] = totals[v] + weight * hots[n][v]
            for v in range(IMG_DEV):
                code_two[unit, place, 8 + v, rows, :] = totals[v].astype(jnp.int32).astype(jnp.int16)
            return carry

        lax.fori_loop(0, CHUNK // 16, body, 0)

    def take(unit, d):
        place = OWN_STEPS + d
        slots = []
        for n in range(8):
            step = n // MOST * 4 + d if unit % 2 == 0 else d * 4 + n // MOST
            slots.append(PAIR_DEV + step * MOST + n % MOST)
        units = [unit_two[unit, place, n : n + 1, :] for n in range(8)]
        images = [table[0, slot] for slot in slots]

        def body(step, totals):
            totals = list(totals)
            rows = pl.ds(pl.multiple_of(step * 16, 16), 16)
            full = pl.ds(pl.multiple_of(unit * CHUNK + step * 16, 16), 16)
            for n in range(8):
                cu = code_two[unit, place, n, rows, :].astype(jnp.int32).astype(f32) * units[n]
                cu_ref[slots[n], full, :] = cu
                cu = cu * depth_ref[images[n], full, :]
                totals[n] = totals[n] + (cu[0:8] + cu[8:16])
            for v in range(IMG_DEV):
                weight = code_two[unit, place, 8 + v, rows, :].astype(jnp.int32).astype(f32)
                weight_sum[v, full, :] = weight_sum[v, full, :] + weight * (1.0 / 128.0)
            return tuple(totals)

        totals = lax.fori_loop(0, CHUNK // 16, body, (jnp.zeros((8, 128), f32),) * 8)
        for n in range(8):
            row = slice(slots[n] - PAIR_DEV, slots[n] - PAIR_DEV + 1)
            part_ref[unit, row, :] = jnp.sum(totals[n], axis=0, keepdims=True)

    for unit in range(2, UNITS):
        hand_on(unit)
    for unit in range(UNITS):
        for copy in far_copies(unit) + scale_copies(unit):
            copy.wait_recv()
        for d in STEPS:
            pass_on(unit, d)
            for copy in slot_copies(unit, d):
                copy.start()
    for unit in range(UNITS):
        pass_on(unit, 0)
        take(unit, 0)
    for unit in range(UNITS):
        for d in STEPS:
            for copy in slot_copies(unit, d):
                copy.wait_recv()
            take(unit, d)
    inner_ref[PAIR_DEV:VIEWS, :] = sum(part_ref[unit] for unit in range(1, UNITS)) + part_ref[0]

    def pair_row(col):
        return jnp.sum(jnp.sum(col, axis=1, keepdims=True) * own_mask, axis=0, keepdims=True)

    fixed_row = pair_row(dot_one + dot_two)
    square_row = pair_row(square_one + square_two)

    def core_copy(t):
        return pltpu.make_async_remote_copy(
            src_ref=core_buf.at[t, 0],
            dst_ref=core_buf.at[t, 1],
            send_sem=core_send.at[t],
            recv_sem=core_recv.at[t],
            device_id=(my_img + 1 - 2 * my_core, my_pair),
            device_id_type=MESH,
        )

    def chip_copy(t, n, arrival):
        a, b, c = offsets[n]
        pair = ys[b] * ZS + zs[c]
        place = xs[a] * OWNERS + pair if arrival else my_chip
        return pltpu.make_async_remote_copy(
            src_ref=chip_buf.at[t, place],
            dst_ref=chip_buf.at[t, place],
            send_sem=chip_send.at[t, n],
            recv_sem=chip_recv.at[t, place],
            device_id=(xs[a] * 2 + my_core, pair),
            device_id_type=MESH,
        )

    def sum_all(t, tile, beside):
        core_buf[t, 0] = tile
        core_copy(t).start()
        core_copy(t).wait_recv()
        chip_buf[t, my_chip] = tile + core_buf[t, 1]
        for n in range(CHIPS - 1):
            chip_copy(t, n, False).start()
        beside()
        for n in reversed(range(CHIPS - 1)):
            chip_copy(t, n, True).wait_recv()
        parts = [chip_buf[t, n] for n in range(CHIPS)]
        while len(parts) > 1:
            parts = [parts[n] + parts[n + 1] for n in range(0, len(parts), 2)]
        return parts[0]

    def stores(tile_id):
        rows = pl.ds(pl.multiple_of(tile_id * TILE * 32, 8), TILE * 32)
        pairs = [(log_ref, log_out), (one_ref, one_out), (two_ref, two_out)]
        return [
            pltpu.make_async_copy(a.at[rows], b.at[rows], store_sem.at[tile_id, n])
            for n, (a, b) in enumerate(pairs)
        ]

    scale_store = pltpu.make_async_copy(scale_ref, scale_out, load_sem.at[0])
    def ray_sums():
        def body(block, carry):
            down = (block * 2 + sub // 4).astype(f32) + first_row
            rays_y = (down + 0.5 - ROWS / 2) / COLS
            rays_x = (((sub % 4) * 128 + lane).astype(f32) + 0.5 - COLS / 2) / COLS
            length = rays_x * rays_x + rays_y * rays_y + 1.0
            rows = block_rows(block)
            for v in range(IMG_DEV):
                lever = rays_x * tau_ref[0, v : v + 1, :] + rays_y * tau_ref[1, v : v + 1, :] + tau_ref[2, v : v + 1, :]
                weight = weight_sum[v, rows, :]
                lever_sum[v, rows, :] = lever * weight
                weight_sum[v, rows, :] = length * weight
            return carry

        lax.fori_loop(0, BLOCKS, body, 0)

    denominator = None
    for sweep in range(ITERS):
        row = jnp.zeros((8, 128), f32)
        for group in range(VIEWS // 8):
            rows = slice(group * 8, group * 8 + 8)
            row = row + jnp.sum(inner_ref[rows, :], axis=1, keepdims=True) * mask_ref[rows, :]
        row = jnp.sum(row, axis=0, keepdims=True) + fixed_row
        two = lax.broadcasted_iota(jnp.int32, (2, 128), 0)
        total = sum_all(sweep, jnp.where(two == 0, row, square_row), ray_sums if sweep == 0 else lambda: None)
        if sweep == 0:
            denominator = total[1:2]
        scales = jnp.broadcast_to(total[0:1] / denominator, (8, 128))
        for group in range(VIEWS // 8):
            rows = slice(group * 8, group * 8 + 8)
            held = jnp.sum(scales * mask_ref[rows, :], axis=1, keepdims=True)
            if group == 0 and sweep == ITERS - 1:
                own_row = jnp.sum(jnp.where(lane == sub, held, 0.0), axis=0, keepdims=True)
                scale_ref[...] = own_row[:, 0:PAIR_DEV]
                scale_store.start()
            weight_ref[rows, :] = jnp.broadcast_to(held, (8, 128))

        steps = START + sweep + 1
        bias_one = 1 - beta_one**steps
        bias_two = 1 - beta_two**steps
        last = sweep == ITERS - 1

        def update(tile_id, carry):
            start = tile_id * TILE

            def gather(step, sums):
                sums = list(sums)
                for n in range(UNROLL):
                    q = step * UNROLL + n
                    r = table[1, q]
                    weight = weight_ref[pl.ds(r, 1), :]
                    for m in range(TILE):
                        sums[m] = sums[m] + cu_ref[r, block_rows(start + m), :] * weight
                        prefix_ref[q + 1, m * 8 : m * 8 + 8, :] = sums[m]
                return tuple(sums)

            zero = jnp.zeros((8, 128), f32)
            for m in range(TILE):
                prefix_ref[0, m * 8 : m * 8 + 8, :] = zero
            lax.fori_loop(0, VIEWS // UNROLL, gather, (zero,) * TILE)
            def step_adam(step, carry):
                for m in range(ADAM):
                    n = step * ADAM + m
                    block = start + n
                    here = pl.ds(pl.multiple_of(n * 8, 8), 8)
                    for v in range(IMG_DEV):
                        depth = depth_ref[v, block_rows(block), :]
                        gathered = prefix_ref[table[2, v], here, :]
                        if v > 0:
                            gathered = gathered - prefix_ref[table[2, v - 1], here, :]
                        pull = depth * weight_sum[v, block_rows(block), :] + lever_sum[v, block_rows(block), :] - gathered
                        half_gradient = depth * pull
                        rows = block_rows(block)
                        old_log, old_one, old_two = (state_ref[n, v, rows, :] for n in range(3))
                        new_one = beta_one * old_one + (2 * (1 - beta_one)) * half_gradient
                        new_two = beta_two * old_two + (4 * (1 - beta_two)) * (half_gradient * half_gradient)
                        corrected_two = new_two * (1 / bias_two)
                        root = corrected_two * lax.rsqrt(corrected_two) + adam_eps
                        inverse = pl.reciprocal(root, approx=True)
                        inverse = inverse * (2.0 - root * inverse)
                        new_log = old_log - (learn_rate / bias_one) * (new_one * inverse)
                        if last:
                            rows = image_rows(block, v)
                            log_ref[rows, :] = new_log
                            one_ref[rows, :] = new_one
                            two_ref[rows, :] = new_two
                        else:
                            state_ref[0, v, rows, :] = new_log
                            state_ref[1, v, rows, :] = new_one
                            state_ref[2, v, rows, :] = new_two
                            depth_ref[v, rows, :] = depth_of(new_log)
                return carry

            lax.fori_loop(0, TILE // ADAM, step_adam, 0)
            if last:
                for copy in stores(tile_id):
                    copy.start()
            return carry

        lax.fori_loop(0, BLOCKS // TILE, update, 0)
        if not last:
            lax.fori_loop(0, VIEWS, dot_view, 0)

    scale_store.wait()
    for tile_id in range(BLOCKS // TILE):
        for copy in stores(tile_id):
            copy.wait()

    def finish(k, carry):
        meta_copy(k).wait_send()
        return carry

    lax.fori_loop(1, OWNERS, finish, 0)
    for unit in range(UNITS):
        for copy in near_copies(unit) + far_copies(unit) + scale_copies(unit):
            copy.wait_send()
        for d in STEPS:
            for copy in slot_copies(unit, d):
                copy.wait_send()
    for t in range(ITERS):
        core_copy(t).wait_send()
        for n in range(CHIPS - 1):
            chip_copy(t, n, False).wait_send()


def store(log_in, one_in, two_in, scale_in, log_out, one_out, two_out, scale_out, bands, scale, in_sem, out_sem):
    half = GROUPS * IMG_DEV // 2
    moves = [(scale_in, scale, scale_out)]
    for part in range(2):
        rows = pl.ds(part * half, half)
        for n, (a, b) in enumerate([(log_in, log_out), (one_in, one_out), (two_in, two_out)]):
            moves.append((a.at[rows], bands.at[n, rows], b.at[rows]))
    loads = [pltpu.make_async_copy(a, m, in_sem.at[n]) for n, (a, m, b) in enumerate(moves)]
    stores = [pltpu.make_async_copy(m, b, out_sem.at[n]) for n, (a, m, b) in enumerate(moves)]
    for copy in loads:
        copy.start()
    for arrived, copy in zip(loads, stores):
        arrived.wait()
        copy.start()
    for copy in stores:
        copy.wait()


def shards(
    log_depth,
    moment_one,
    moment_two,
    image_pose,
    pair_points,
    confidence,
    pair_pose,
    first_local,
    second_owner,
    second_local,
):
    def fold(a):
        return a.reshape(IMG_DEV, GROUPS, 128).transpose(1, 0, 2).reshape(GROUPS * IMG_DEV, 128)

    def unfold(a):
        return a.reshape(GROUPS, IMG_DEV, 128).transpose(1, 0, 2).reshape(IMG_DEV, BAND)

    points = pair_points.transpose(1, 0, 2)
    conf = confidence.reshape(PAIR_DEV, 2, GROUPS, 128).transpose(0, 2, 1, 3).reshape(PAIR_DEV * GROUPS * 2, 128)
    hbm = pl.BlockSpec(memory_space=pltpu.HBM)
    band = jax.ShapeDtypeStruct((GROUPS * IMG_DEV, 128), f32)
    dma = pltpu.SemaphoreType.DMA
    out = pl.pallas_call(
        kernel,
        out_shape=(band, band, band, jax.ShapeDtypeStruct((1, PAIR_DEV), f32)),
        in_specs=[hbm] * 10,
        out_specs=(hbm,) * 4,
        scratch_shapes=[
            pltpu.VMEM((1, PAIR_DEV), f32),
            pltpu.VMEM((GROUPS * IMG_DEV, 128), f32),
            pltpu.VMEM((GROUPS * IMG_DEV, 128), f32),
            pltpu.VMEM((GROUPS * IMG_DEV, 128), f32),
            pltpu.VMEM((6, PAIR_DEV, BAND), jnp.bfloat16),
            pltpu.VMEM((PAIR_DEV * GROUPS * 2, 128), jnp.bfloat16),
            pltpu.SMEM((7, IMG_DEV * OWNERS), f32),
            pltpu.SMEM((7, PAIR_DEV), f32),
            pltpu.SMEM((PAIR_DEV,), jnp.int32),
            pltpu.SMEM((PAIR_DEV,), jnp.int32),
            pltpu.SMEM((PAIR_DEV,), jnp.int32),
            pltpu.VMEM((PAIR_DEV * GROUPS * 2, 128), f32),
            pltpu.VMEM((PAIR_DEV * GROUPS, 128), f32),
            pltpu.VMEM((PAIR_DEV * GROUPS, 128), f32),
            *(pltpu.VMEM((4, PAIR_DEV, 2 * CHUNK, 128), jnp.int16) for unit in range(4)),
            *(pltpu.VMEM((4, PAIR_DEV, 128), f32) for unit in range(4)),
            pltpu.VMEM((PAIR_DEV, 128), f32),
            pltpu.VMEM((UNITS, 2 * OWN_STEPS, 8 + IMG_DEV, CHUNK, 128), jnp.int16),
            pltpu.VMEM((UNITS, 2 * OWN_STEPS, 8, 128), f32),
            pltpu.VMEM((UNITS, SLOTS, 128), f32),
            pltpu.VMEM((8, IMG_DEV, 8, 128), f32),
            pltpu.VMEM((OWNERS, 8, 128), jnp.int32),
            pltpu.VMEM((VIEWS, GROUPS, 128), f32),
            pltpu.VMEM((VIEWS + 1, TILE * 8, 128), f32),
            pltpu.VMEM((3, IMG_DEV, GROUPS, 128), f32),
            pltpu.VMEM((IMG_DEV, GROUPS, 128), f32),
            pltpu.VMEM((IMG_DEV, GROUPS, 128), f32),
            pltpu.VMEM((IMG_DEV, GROUPS, 128), f32),
            pltpu.VMEM((3, 8, 128), f32),
            pltpu.VMEM((IMG_DEV, VIEWS, 128), f32),
            pltpu.VMEM((VIEWS, 128), f32),
            pltpu.VMEM((VIEWS, 128), f32),
            pltpu.VMEM((VIEWS, 128), f32),
            pltpu.VMEM((ITERS, 2, 2, 128), f32),
            pltpu.VMEM((ITERS, CHIPS, 2, 128), f32),
            pltpu.VMEM((8, 128), jnp.int32),
            pltpu.SMEM((8, 128), jnp.int32),
            dma((11,)),
            dma((BLOCKS // TILE, 3)),
            dma,
            *(dma((UNITS * 4,)) for kind in range(8)),
            dma((OWNERS,)),
            dma((OWNERS,)),
            dma((ITERS,)),
            dma((ITERS,)),
            dma((ITERS, CHIPS)),
            dma((ITERS, CHIPS)),
        ],
        compiler_params=pltpu.CompilerParams(
            collective_id=0, has_side_effects=True, vmem_limit_bytes=60 * 2**20
        ),
        name="align",
    )(
        fold(log_depth),
        fold(moment_one),
        fold(moment_two),
        points,
        conf,
        image_pose,
        pair_pose,
        first_local,
        second_owner.reshape(PAIR_DEV),
        second_local,
    )
    out = pl.pallas_call(
        store,
        out_shape=(band, band, band, jax.ShapeDtypeStruct((1, PAIR_DEV), f32)),
        in_specs=[hbm] * 4,
        out_specs=(hbm,) * 4,
        scratch_shapes=[
            pltpu.VMEM((3, GROUPS * IMG_DEV, 128), f32),
            pltpu.VMEM((1, PAIR_DEV), f32),
            dma((7,)),
            dma((7,)),
        ],
        compiler_params=pltpu.CompilerParams(vmem_limit_bytes=60 * 2**20),
        name="store",
    )(*out)
    return (unfold(out[0]), unfold(out[1]), unfold(out[2]), out[3].reshape(PAIR_DEV))


def solution(mesh):
    return jax.shard_map(
        shards,
        mesh=mesh,
        in_specs=(
            P("pair", "img"),
            P("pair", "img"),
            P("pair", "img"),
            P(),
            P("pair", None, "img"),
            P("pair", None, "img"),
            P(None, "pair"),
            P("pair"),
            P("pair", None),
            P("pair"),
        ),
        out_specs=(P("pair", "img"), P("pair", "img"), P("pair", "img"), P("pair")),
        check_vma=False,
    )
```

```python
import jax
import jax.numpy as jnp
from jax import lax
from jax.experimental import pallas as pl
from jax.experimental.pallas import tpu as pltpu
from jax.sharding import PartitionSpec as P

ROWS = 384
COLS = 512
ITERS = 3
START = 100
IMG_DEV = 4
PAIR_DEV = 8
MOST = 2
IMGS = 8
OWNERS = 16
XS = 4
YS = 4
ZS = 4
CHIPS = XS * YS * ZS
BAND = ROWS * COLS // IMGS
GROUPS = BAND // 128
BLOCKS = GROUPS // 8
BAND_ROWS = ROWS // IMGS
SLOTS = OWNERS * MOST
VIEWS = PAIR_DEV + SLOTS
UNITS = 4
CHUNK = GROUPS // UNITS
UNIT_ROWS = BAND_ROWS // UNITS
OWN_STEPS = 4
STEPS = (2, 1, 3)
TILE = 12
PART = 4
ADAM = 6
UNROLL = 8
LEVELS = 32700.0

beta_one = 0.9
beta_two = 0.999
learn_rate = 0.01
adam_eps = 1e-08
f32 = jnp.float32
MESH = pl.DeviceIdType.MESH


def rotation(scalar_q, vec_a, vec_b, vec_c):
    magnitude = jnp.sqrt(scalar_q * scalar_q + vec_a * vec_a + vec_b * vec_b + vec_c * vec_c)
    unit_s = scalar_q / magnitude
    unit_a = vec_a / magnitude
    unit_b = vec_b / magnitude
    unit_c = vec_c / magnitude
    return (
        (
            1 - 2 * (unit_b * unit_b + unit_c * unit_c),
            2 * (unit_a * unit_b - unit_s * unit_c),
            2 * (unit_a * unit_c + unit_s * unit_b),
        ),
        (
            2 * (unit_a * unit_b + unit_s * unit_c),
            1 - 2 * (unit_a * unit_a + unit_c * unit_c),
            2 * (unit_b * unit_c - unit_s * unit_a),
        ),
        (
            2 * (unit_a * unit_c - unit_s * unit_b),
            2 * (unit_b * unit_c + unit_s * unit_a),
            1 - 2 * (unit_a * unit_a + unit_b * unit_b),
        ),
    )


def kernel(
    log_hbm,
    one_hbm,
    two_hbm,
    points_hbm,
    conf_hbm,
    image_pose_hbm,
    pair_pose_hbm,
    first_local_hbm,
    second_owner_hbm,
    second_local_hbm,
    log_out,
    one_out,
    two_out,
    scale_out,
    scale_ref,
    log_ref,
    one_ref,
    two_ref,
    points_ref,
    conf_ref,
    image_pose,
    pair_pose,
    first_local,
    second_owner,
    second_local,
    conf_f,
    stage_one,
    stage_two,
    inverse_ref,
    code_two,
    unit_two,
    part_ref,
    pass_hot,
    meta,
    cu_ref,
    prefix_ref,
    state_ref,
    weight_sum,
    lever_sum,
    depth_ref,
    tau_ref,
    hot_ref,
    mask_ref,
    weight_ref,
    inner_ref,
    core_buf,
    chip_buf,
    table_ref,
    table,
    load_sem,
    store_sem,
    table_sem,
    one_send,
    one_recv,
    scale_send,
    scale_recv,
    two_send,
    two_recv,
    pass_send,
    pass_recv,
    meta_send,
    meta_recv,
    core_send,
    core_recv,
    chip_send,
    chip_recv,
    *per_unit,
):
    def load(n, src, dst):
        copy = pltpu.make_async_copy(src, dst, load_sem.at[n])
        copy.start()
        return copy

    small = [
        load(0, second_owner_hbm, second_owner),
        load(1, second_local_hbm, second_local),
        load(2, first_local_hbm, first_local),
        load(3, pair_pose_hbm, pair_pose),
        load(4, image_pose_hbm, image_pose),
    ]
    conf_load = load(5, conf_hbm, conf_ref)
    second_load = load(6, points_hbm.at[pl.ds(3, 3)], points_ref.at[pl.ds(3, 3)])
    first_load = load(7, points_hbm.at[pl.ds(0, 3)], points_ref.at[pl.ds(0, 3)])
    log_load = load(8, log_hbm, log_ref)
    state_loads = [load(9, one_hbm, one_ref), load(10, two_hbm, two_ref)]

    my_img = lax.axis_index("img")
    my_pair = lax.axis_index("pair")
    my_y = my_pair // ZS
    my_z = my_pair % ZS

    def pair_at(k, sign):
        return ((my_y + sign * (k // ZS) + YS) % YS) * ZS + (my_z + sign * (k % ZS) + ZS) % ZS

    barrier = pltpu.get_barrier_semaphore()

    my_x = my_img // 2
    my_core = my_img % 2
    my_chip = my_x * OWNERS + my_pair
    xs = [(my_x + d) % XS for d in range(XS)]
    ys = [(my_y + d) % YS for d in range(YS)]
    zs = [(my_z + d) % ZS for d in range(ZS)]
    offsets = [(a, b, c) for a in range(XS) for b in range(YS) for c in range(ZS) if (a, b, c) != (0, 0, 0)]
    offsets.sort(key=lambda o: -sum(min(d, 4 - d) for d in o))

    def greet_chip(k, carry):
        x = (my_x + k // OWNERS) % XS
        y = (my_y + k // ZS) % YS
        z = (my_z + k) % ZS
        pl.semaphore_signal(barrier, 1, device_id=(x * 2 + my_core, y * ZS + z), device_id_type=MESH)
        return carry

    pl.semaphore_signal(barrier, 1, device_id=(my_img + 1 - 2 * my_core, my_pair), device_id_type=MESH)
    lax.fori_loop(1, CHIPS, greet_chip, 0)

    sub = lax.broadcasted_iota(jnp.int32, (8, 128), 0)
    lane = lax.broadcasted_iota(jnp.int32, (8, 128), 1)

    for copy in small:
        copy.wait()

    owners = [second_owner[e] for e in range(PAIR_DEV)]
    order = []
    for e in range(PAIR_DEV):
        rank = jnp.int32(0)
        for other in range(e):
            rank = rank + jnp.where(owners[other] == owners[e], 1, 0)
        order.append(owners[e] * MOST + rank)
    row = jnp.zeros((8, 128), jnp.int32)
    for e in range(PAIR_DEV):
        here = lane == my_pair * PAIR_DEV + e
        row = jnp.where(here & (sub == 0), order[e], row)
        row = jnp.where(here & (sub == 1), second_local[e], row)
    meta[0] = row

    def column(values):
        out = jnp.zeros((8, 128), f32)
        for e in range(PAIR_DEV):
            out = jnp.where(sub == e, values[e], out)
        return out

    pair_cols = [column([pair_pose[i, e] for e in range(PAIR_DEV)]) for i in range(7)]
    pair_rot = rotation(*pair_cols[:4])
    shift = pair_cols[4:]
    firsts = [my_pair * IMG_DEV + first_local[e] for e in range(PAIR_DEV)]
    seconds = [owners[e] * IMG_DEV + second_local[e] for e in range(PAIR_DEV)]
    lean = [2.0 * sum(pair_rot[i][j] * shift[i] for i in range(3)) for j in range(3)]
    shift_sq = sum(shift[i] * shift[i] for i in range(3))
    first_row = (my_img * BAND_ROWS).astype(f32)
    ray_y0 = (first_row + 0.5 - ROWS / 2) / COLS
    ray_x = [((lane + 128 * part).astype(f32) + 0.5 - COLS / 2) / COLS for part in range(4)]

    def widen(step, carry):
        rows = pl.ds(pl.multiple_of(step * 64, 64), 64)
        conf_f[rows, :] = conf_ref[rows, :].astype(f32)
        return carry

    conf_load.wait()
    lax.fori_loop(0, PAIR_DEV * 2 * GROUPS // 64, widen, 0)
    second_load.wait()

    def prepare(view, images, stage):
        cols = [column([image_pose[i, images[e]] for e in range(PAIR_DEV)]) for i in range(7)]
        rot = rotation(*cols[:4])
        trans = cols[4:]
        both = [[sum(rot[l][i] * pair_rot[l][j] for l in range(3)) for j in range(3)] for i in range(3)]
        moved = [sum(rot[l][i] * shift[l] for l in range(3)) for i in range(3)]
        full = [[both[i][0], both[i][1], both[i][2], moved[i]] for i in range(3)]
        base = [[ray_x[part] * full[0][j] + (full[2][j] + ray_y0 * full[1][j]) for part in range(4)] for j in range(4)]
        slope = [full[1][j] * (1.0 / COLS) for j in range(4)]
        toward = [sum(trans[l] * pair_rot[l][j] for l in range(3)) for j in range(3)]
        offset = sum(trans[l] * shift[l] for l in range(3))

        def body(r, carry):
            total_sq, total_dot, total_conf, largest = carry
            down = r.astype(f32)
            tilt = [slope[j] * down for j in range(4)]
            for part in range(4):
                at = pl.ds(pl.multiple_of(r * COLS + part * 128, 128), 128)
                x = [points_ref[3 * view + j, :, at].astype(f32) for j in range(3)]
                weight = conf_f[pl.ds((r * 4 + part) * 2 + view, 8, stride=2 * GROUPS), :]
                value = base[3][part] + tilt[3]
                for j in range(3):
                    value = value + (base[j][part] + tilt[j]) * x[j]
                value = value * weight
                largest = jnp.maximum(largest, jnp.abs(value))
                stage[pl.ds(pl.multiple_of((r * 4 + part) * 8, 8), 8), :] = value
                square = x[0] * (x[0] + lean[0]) + x[1] * (x[1] + lean[1]) + x[2] * (x[2] + lean[2])
                dot = x[0] * toward[0] + x[1] * toward[1] + x[2] * toward[2]
                total_sq = total_sq + weight * square
                total_dot = total_dot + weight * dot
                total_conf = total_conf + weight
            return (total_sq, total_dot, total_conf, largest)

        def run(unit, sums):
            tiny = jnp.full((8, 128), 1e-30, f32)
            start = unit * UNIT_ROWS
            out = lax.fori_loop(start, start + UNIT_ROWS, body, (*sums, tiny))
            return out[:3], out[3]

        def close(sums):
            return (sums[0] + sums[2] * shift_sq, sums[1] + sums[2] * offset)

        return run, close

    empty = (jnp.zeros((8, 128), f32),) * 3
    code_one, unit_one = per_unit[:UNITS], per_unit[UNITS:]
    run_two, close_two = prepare(1, seconds, stage_two)

    def encode(unit, largest):
        unit_one[unit][0] = largest * (1.0 / LEVELS)
        inverse_ref[...] = LEVELS / largest

        def body(e, carry):
            inverse = inverse_ref[pl.ds(e, 1), :]
            for step in range(CHUNK // 16):
                place = unit * (CHUNK // 16) + step
                rows = slice(step * 16, step * 16 + 16)
                value = stage_two[pl.ds(place * 128 + e, 16, stride=8), :] * inverse
                code_one[unit][0, e, rows, :] = jnp.floor(value + 0.5).astype(jnp.int32).astype(jnp.int16)
                weight = conf_f[pl.ds(e * 2 * GROUPS + place * 32 + 1, 16, stride=2), :] * 128.0
                rows = slice(CHUNK + step * 16, CHUNK + step * 16 + 16)
                code_one[unit][0, e, rows, :] = weight.astype(jnp.int32).astype(jnp.int16)
            return carry

        lax.fori_loop(0, PAIR_DEV, body, 0)

    def ahead(axis, d):
        if axis == 0:
            return (my_img, ys[d] * ZS + my_z)
        return (my_img, my_y * ZS + zs[d])

    def remote(src, dst, sems, place, device):
        return pltpu.make_async_remote_copy(
            src_ref=src,
            dst_ref=dst,
            send_sem=sems[0].at[place],
            recv_sem=sems[1].at[place],
            device_id=device,
            device_id_type=MESH,
        )

    def near_copies(unit):
        return [
            remote(code_one[unit].at[0], code_one[unit].at[d], (one_send, one_recv), unit * 4 + d, ahead(unit % 2, d))
            for d in (1, 3)
        ]

    def far_copies(unit):
        half = PAIR_DEV // 2
        return [
            remote(
                code_one[unit].at[d, part], code_one[unit].at[2, part], (one_send, one_recv), unit * 4 + n, ahead(unit % 2, d)
            )
            for d, n, part in ((1, 0, pl.ds(0, half)), (3, 2, pl.ds(half, half)))
        ]

    def scale_copies(unit):
        return [
            remote(unit_one[unit].at[0], unit_one[unit].at[d], (scale_send, scale_recv), unit * 4 + d, ahead(unit % 2, d))
            for d in STEPS
        ]

    def slot_copies(unit, d):
        place = unit * 4 + d
        to = ahead(1 - unit % 2, d)
        return [
            remote(code_two.at[unit, d], code_two.at[unit, OWN_STEPS + d], (two_send, two_recv), place, to),
            remote(unit_two.at[unit, d], unit_two.at[unit, OWN_STEPS + d], (pass_send, pass_recv), place, to),
        ]

    def send(unit, sums):
        sums, largest = run_two(unit, sums)
        encode(unit, largest)
        if unit == 0:
            pl.semaphore_wait(barrier, CHIPS)
        for copy in near_copies(unit) + scale_copies(unit):
            copy.start()
        return sums

    def hand_on(unit):
        for arrived, copy in zip(near_copies(unit), far_copies(unit)):
            arrived.wait_recv()
            copy.start()

    sums = send(0, empty)

    def meta_copy(k):
        return pltpu.make_async_remote_copy(
            src_ref=meta.at[0],
            dst_ref=meta.at[k],
            send_sem=meta_send.at[k],
            recv_sem=meta_recv.at[k],
            device_id=(my_img, pair_at(k, 1)),
            device_id_type=MESH,
        )

    def start_meta(k, carry):
        meta_copy(k).start()
        return carry

    lax.fori_loop(1, OWNERS, start_meta, 0)
    for unit in range(1, UNITS):
        sums = send(unit, sums)
    square_two, dot_two = close_two(sums)
    def depth_of(values):
        return jnp.exp(values.astype(jnp.bfloat16).astype(f32))

    def image_rows(block, v):
        return pl.ds(block * 32 + v, 8, stride=IMG_DEV)

    def block_rows(block):
        return pl.ds(pl.multiple_of(block * 8, 8), 8)

    def first_depth(block, carry):
        for v in range(IMG_DEV):
            value = log_ref[image_rows(block, v), :]
            state_ref[0, v, block_rows(block), :] = value
            depth_ref[v, block_rows(block), :] = depth_of(value)
        return carry

    def fold_moments(block, carry):
        for v in range(IMG_DEV):
            state_ref[1, v, block_rows(block), :] = one_ref[image_rows(block, v), :]
            state_ref[2, v, block_rows(block), :] = two_ref[image_rows(block, v), :]
        return carry

    def pass_on(unit, d):
        place = d if d > 0 else OWN_STEPS
        index = unit % 2 * 4 + d
        sources = [table[3, index * 8 + n] for n in range(8)]
        hots = [[pass_hot[index, v, n : n + 1, :] for v in range(IMG_DEV)] for n in range(8)]
        for n in range(8):
            unit_two[unit, place, n : n + 1, :] = unit_one[unit][n // MOST, pl.ds(sources[n], 1), :]

        def body(step, carry):
            rows = pl.ds(pl.multiple_of(step * 16, 16), 16)
            weight_rows = pl.ds(pl.multiple_of(CHUNK + step * 16, 16), 16)
            totals = [jnp.zeros((16, 128), f32) for v in range(IMG_DEV)]
            for n in range(8):
                code_two[unit, place, n, rows, :] = code_one[unit][n // MOST, sources[n], rows, :]
                weight = code_one[unit][n // MOST, sources[n], weight_rows, :].astype(jnp.int32).astype(f32)
                for v in range(IMG_DEV):
                    totals[v] = totals[v] + weight * hots[n][v]
            for v in range(IMG_DEV):
                code_two[unit, place, 8 + v, rows, :] = totals[v].astype(jnp.int32).astype(jnp.int16)
            return carry

        for step in range(CHUNK // 16):
            body(step, 0)

    def take(unit, d):
        place = OWN_STEPS + d
        slots = []
        for n in range(8):
            step = n // MOST * 4 + d if unit % 2 == 0 else d * 4 + n // MOST
            slots.append(PAIR_DEV + step * MOST + n % MOST)
        units = [unit_two[unit, place, n : n + 1, :] for n in range(8)]
        images = [table[0, slot] for slot in slots]

        def body(step, totals):
            totals = list(totals)
            rows = pl.ds(pl.multiple_of(step * 16, 16), 16)
            full = pl.ds(pl.multiple_of(unit * CHUNK + step * 16, 16), 16)
            for n in range(8):
                cu = code_two[unit, place, n, rows, :].astype(jnp.int32).astype(f32) * units[n]
                cu_ref[slots[n], full, :] = cu
                cu = cu * depth_ref[images[n], full, :]
                totals[n] = totals[n] + (cu[0:8] + cu[8:16])
            for v in range(IMG_DEV):
                weight = code_two[unit, place, 8 + v, rows, :].astype(jnp.int32).astype(f32)
                weight_sum[v, full, :] = weight_sum[v, full, :] + weight * (1.0 / 128.0)
            return tuple(totals)

        totals = (jnp.zeros((8, 128), f32),) * 8
        for step in range(CHUNK // 16):
            totals = body(step, totals)
        for n in range(8):
            row = slice(slots[n] - PAIR_DEV, slots[n] - PAIR_DEV + 1)
            part_ref[unit, row, :] = jnp.sum(totals[n], axis=0, keepdims=True)

    def relay(unit):
        for copy in far_copies(unit) + scale_copies(unit):
            copy.wait_recv()
        for d in STEPS:
            pass_on(unit, d)
            for copy in slot_copies(unit, d):
                copy.start()
    own = [[image_pose[i, my_pair * IMG_DEV + min(v, IMG_DEV - 1)] for v in range(8)] for i in range(7)]
    own_cols = [column(own[i]) for i in range(7)]
    own_rot = rotation(*own_cols[:4])
    for i in range(3):
        tau_ref[i] = sum(own_rot[l][i] * own_cols[4 + l] for l in range(3))

    for k in range(1, OWNERS):
        meta_copy(k).wait_recv()
    known = meta[0]
    for k in range(1, OWNERS):
        known = known + meta[k]
    code_row = jnp.broadcast_to(known[0:1], (8, 128))
    local_row = jnp.broadcast_to(known[1:2], (8, 128))
    from_pair = lane // PAIR_DEV
    step_of = ((my_y - from_pair // ZS + YS) % YS) * ZS + (my_z - from_pair % ZS + ZS) % ZS
    slot_of = jnp.where(code_row // MOST == my_pair, step_of * MOST + code_row % MOST, -1)
    local_first = jnp.zeros((8, 128), jnp.int32)
    for e in range(PAIR_DEV):
        local_first = jnp.where(sub == e, first_local[e], local_first)
    own_mask = jnp.where(lane == my_pair * PAIR_DEV + sub, 1.0, 0.0)
    mask_ref[0:8, :] = own_mask
    for v in range(IMG_DEV):
        hot_ref[v, 0:8, :] = jnp.where(local_first == v, 1.0, 0.0)
    for group in range(SLOTS // 8):
        rows = pl.ds(8 + group * 8, 8)
        held = slot_of == sub + group * 8
        mask_ref[rows, :] = jnp.where(held, 1.0, 0.0)
        for v in range(IMG_DEV):
            found = jnp.where(held & (local_row == v), 1.0, 0.0)
            hot_ref[v, rows, :] = jnp.broadcast_to(jnp.sum(found, axis=1, keepdims=True), (8, 128))

    image_row = jnp.zeros((8, 128), jnp.int32)
    for group in range(VIEWS // 8):
        if group == 0:
            image_col = local_first
        else:
            held = (slot_of == sub + (group - 1) * 8).astype(jnp.int32)
            image_col = jnp.sum(held * (local_row - IMG_DEV), axis=1, keepdims=True) + IMG_DEV
        found = jnp.where(lane == sub + group * 8, image_col, 0)
        image_row = image_row + jnp.broadcast_to(jnp.sum(found, axis=0, keepdims=True), (8, 128))
    order_row = jnp.zeros((8, 128), jnp.int32)
    listed = lane < VIEWS
    for group in range(VIEWS // 8):
        view = sub + group * 8
        found = jnp.where(lane == view, image_row, 0)
        image_col = jnp.sum(found, axis=1, keepdims=True)
        before = listed & ((image_row < image_col) | ((image_row == image_col) & (lane < view)))
        place = jnp.sum(before.astype(jnp.int32), axis=1, keepdims=True)
        found = jnp.where(lane == place, view, 0)
        order_row = order_row + jnp.broadcast_to(jnp.sum(found, axis=0, keepdims=True), (8, 128))
    end_row = jnp.zeros((8, 128), jnp.int32)
    for v in range(IMG_DEV):
        upto = (listed & (image_row <= v)).astype(jnp.int32)
        end_row = jnp.where(lane == v, jnp.sum(upto, axis=1, keepdims=True), end_row)
    image_row = jnp.minimum(image_row, IMG_DEV - 1)

    pass_row = jnp.zeros((8, 128), jnp.int32)
    for half in range(2):
        for d in range(4):
            if half == 0:
                goal = my_y * ZS + zs[d]
                source = ((my_y - sub // MOST + YS) % YS) * ZS + my_z
            else:
                goal = ys[d] * ZS + my_z
                source = my_y * ZS + (my_z - sub // MOST + ZS) % ZS
            match = (from_pair == source) & (code_row == goal * MOST + sub % MOST)
            chosen = jnp.sum(jnp.where(match, lane % PAIR_DEV, 0), axis=1, keepdims=True)
            found = jnp.where(lane == sub + (half * 4 + d) * 8, chosen, 0)
            pass_row = pass_row + jnp.broadcast_to(jnp.sum(found, axis=0, keepdims=True), (8, 128))
            for v in range(IMG_DEV):
                hot = jnp.where(match & (local_row == v), 1.0, 0.0)
                pass_hot[half * 4 + d, v] = jnp.broadcast_to(jnp.sum(hot, axis=1, keepdims=True), (8, 128))
    table_ref[...] = jnp.where(sub == 0, image_row, jnp.where(sub == 1, order_row, jnp.where(sub == 2, end_row, pass_row)))
    table_copy = pltpu.make_async_copy(table_ref, table, table_sem)
    table_copy.start()

    first_load.wait()
    run_one, close_one = prepare(0, firsts, stage_one)
    sums = empty
    for unit in range(UNITS):
        sums, largest = run_one(unit, sums)
    square_one, dot_one = close_one(sums)

    hand_on(0)
    hand_on(1)
    log_load.wait()
    lax.fori_loop(0, BLOCKS, first_depth, 0)
    for copy in state_loads:
        copy.wait()

    lax.fori_loop(0, BLOCKS, fold_moments, 0)

    for unit in range(2, UNITS):
        hand_on(unit)
    table_copy.wait()
    for unit in range(UNITS):
        relay(unit)

    def first_copy(e, carry):
        for block in range(BLOCKS):
            cu_ref[e, block * 8 : block * 8 + 8, :] = stage_one[pl.ds(block * 64 + e, 8, stride=8), :]
        return carry

    lax.fori_loop(0, PAIR_DEV, first_copy, 0)

    def dot_views(step, carry):
        for n in range(4):
            dot_view(step * 4 + n, carry)
        return carry

    def dot_view(r, carry):
        v = table[0, r]
        totals = [jnp.zeros((8, 128), f32) for n in range(PART)]
        for block in range(BLOCKS):
            rows = slice(block * 8, block * 8 + 8)
            totals[block % PART] = totals[block % PART] + cu_ref[r, rows, :] * depth_ref[v, rows, :]
        total = (totals[0] + totals[1]) + (totals[2] + totals[3])
        inner_ref[pl.ds(r, 1), :] = jnp.sum(total, axis=0, keepdims=True)
        return carry

    lax.fori_loop(0, PAIR_DEV // 4, dot_views, 0)

    def first_sums(block, carry):
        sums = [jnp.zeros((8, 128), f32) for v in range(IMG_DEV)]
        for e in range(PAIR_DEV):
            weight = conf_f[pl.ds(e * 2 * GROUPS + block * 16, 8, stride=2), :]
            for v in range(IMG_DEV):
                sums[v] = sums[v] + weight * hot_ref[v, e : e + 1, :]
        for v in range(IMG_DEV):
            weight_sum[v, block_rows(block), :] = sums[v]
        return carry

    lax.fori_loop(0, BLOCKS, first_sums, 0)

    for unit in range(UNITS):
        pass_on(unit, 0)
        take(unit, 0)
    for unit in range(UNITS):
        for d in STEPS:
            for copy in slot_copies(unit, d):
                copy.wait_recv()
            take(unit, d)
    inner_ref[PAIR_DEV:VIEWS, :] = sum(part_ref[unit] for unit in range(1, UNITS)) + part_ref[0]

    def pair_row(col):
        return jnp.sum(jnp.sum(col, axis=1, keepdims=True) * own_mask, axis=0, keepdims=True)

    fixed_row = pair_row(dot_one + dot_two)
    square_row = pair_row(square_one + square_two)

    def core_copy(t):
        return pltpu.make_async_remote_copy(
            src_ref=core_buf.at[t, 0],
            dst_ref=core_buf.at[t, 1],
            send_sem=core_send.at[t],
            recv_sem=core_recv.at[t],
            device_id=(my_img + 1 - 2 * my_core, my_pair),
            device_id_type=MESH,
        )

    def chip_copy(t, n, arrival):
        a, b, c = offsets[n]
        pair = ys[b] * ZS + zs[c]
        place = xs[a] * OWNERS + pair if arrival else my_chip
        return pltpu.make_async_remote_copy(
            src_ref=chip_buf.at[t, place],
            dst_ref=chip_buf.at[t, place],
            send_sem=chip_send.at[t, n],
            recv_sem=chip_recv.at[t, place],
            device_id=(xs[a] * 2 + my_core, pair),
            device_id_type=MESH,
        )

    def sum_all(t, tile, beside):
        core_buf[t, 0] = tile
        core_copy(t).start()
        core_copy(t).wait_recv()
        chip_buf[t, my_chip] = tile + core_buf[t, 1]
        for n in range(CHIPS - 1):
            chip_copy(t, n, False).start()
        beside()
        for n in reversed(range(CHIPS - 1)):
            chip_copy(t, n, True).wait_recv()
        parts = [chip_buf[t, n] for n in range(CHIPS)]
        while len(parts) > 1:
            parts = [parts[n] + parts[n + 1] for n in range(0, len(parts), 2)]
        return parts[0]

    def stores(tile_id):
        rows = pl.ds(pl.multiple_of(tile_id * TILE * 32, 8), TILE * 32)
        pairs = [(log_ref, log_out), (one_ref, one_out), (two_ref, two_out)]
        return [
            pltpu.make_async_copy(a.at[rows], b.at[rows], store_sem.at[tile_id, n])
            for n, (a, b) in enumerate(pairs)
        ]

    scale_store = pltpu.make_async_copy(scale_ref, scale_out, load_sem.at[0])
    def ray_sums():
        def body(block, carry):
            down = (block * 2 + sub // 4).astype(f32) + first_row
            rays_y = (down + 0.5 - ROWS / 2) / COLS
            rays_x = (((sub % 4) * 128 + lane).astype(f32) + 0.5 - COLS / 2) / COLS
            length = rays_x * rays_x + rays_y * rays_y + 1.0
            rows = block_rows(block)
            for v in range(IMG_DEV):
                lever = rays_x * tau_ref[0, v : v + 1, :] + rays_y * tau_ref[1, v : v + 1, :] + tau_ref[2, v : v + 1, :]
                weight = weight_sum[v, rows, :]
                lever_sum[v, rows, :] = lever * weight
                weight_sum[v, rows, :] = length * weight
            return carry

        lax.fori_loop(0, BLOCKS, body, 0)

    denominator = None
    for sweep in range(ITERS):
        row = jnp.zeros((8, 128), f32)
        for group in range(VIEWS // 8):
            rows = slice(group * 8, group * 8 + 8)
            row = row + jnp.sum(inner_ref[rows, :], axis=1, keepdims=True) * mask_ref[rows, :]
        row = jnp.sum(row, axis=0, keepdims=True) + fixed_row
        two = lax.broadcasted_iota(jnp.int32, (2, 128), 0)
        total = sum_all(sweep, jnp.where(two == 0, row, square_row), ray_sums if sweep == 0 else lambda: None)
        if sweep == 0:
            denominator = total[1:2]
        scales = jnp.broadcast_to(total[0:1] / denominator, (8, 128))
        for group in range(VIEWS // 8):
            rows = slice(group * 8, group * 8 + 8)
            held = jnp.sum(scales * mask_ref[rows, :], axis=1, keepdims=True)
            if group == 0 and sweep == ITERS - 1:
                own_row = jnp.sum(jnp.where(lane == sub, held, 0.0), axis=0, keepdims=True)
                scale_ref[...] = own_row[:, 0:PAIR_DEV]
                scale_store.start()
            weight_ref[rows, :] = jnp.broadcast_to(held, (8, 128))

        steps = START + sweep + 1
        bias_one = 1 - beta_one**steps
        bias_two = 1 - beta_two**steps
        last = sweep == ITERS - 1

        def update(tile_id, carry):
            start = tile_id * TILE

            def gather(step, sums):
                sums = list(sums)
                for n in range(UNROLL):
                    q = step * UNROLL + n
                    r = table[1, q]
                    weight = weight_ref[pl.ds(r, 1), :]
                    for m in range(TILE):
                        sums[m] = sums[m] + cu_ref[r, block_rows(start + m), :] * weight
                        prefix_ref[q + 1, m * 8 : m * 8 + 8, :] = sums[m]
                return tuple(sums)

            zero = jnp.zeros((8, 128), f32)
            for m in range(TILE):
                prefix_ref[0, m * 8 : m * 8 + 8, :] = zero
            lax.fori_loop(0, VIEWS // UNROLL, gather, (zero,) * TILE)
            def step_adam(step, carry):
                for m in range(ADAM):
                    n = step * ADAM + m
                    block = start + n
                    here = pl.ds(pl.multiple_of(n * 8, 8), 8)
                    for v in range(IMG_DEV):
                        depth = depth_ref[v, block_rows(block), :]
                        gathered = prefix_ref[table[2, v], here, :]
                        if v > 0:
                            gathered = gathered - prefix_ref[table[2, v - 1], here, :]
                        pull = depth * weight_sum[v, block_rows(block), :] + lever_sum[v, block_rows(block), :] - gathered
                        half_gradient = depth * pull
                        rows = block_rows(block)
                        old_log, old_one, old_two = (state_ref[n, v, rows, :] for n in range(3))
                        new_one = beta_one * old_one + (2 * (1 - beta_one)) * half_gradient
                        new_two = beta_two * old_two + (4 * (1 - beta_two)) * (half_gradient * half_gradient)
                        corrected_two = new_two * (1 / bias_two)
                        root = corrected_two * lax.rsqrt(corrected_two) + adam_eps
                        inverse = pl.reciprocal(root, approx=True)
                        inverse = inverse * (2.0 - root * inverse)
                        new_log = old_log - (learn_rate / bias_one) * (new_one * inverse)
                        if last:
                            rows = image_rows(block, v)
                            log_ref[rows, :] = new_log
                            one_ref[rows, :] = new_one
                            two_ref[rows, :] = new_two
                        else:
                            state_ref[0, v, rows, :] = new_log
                            state_ref[1, v, rows, :] = new_one
                            state_ref[2, v, rows, :] = new_two
                            depth_ref[v, rows, :] = depth_of(new_log)
                return carry

            lax.fori_loop(0, TILE // ADAM, step_adam, 0)
            if last:
                for copy in stores(tile_id):
                    copy.start()
            return carry

        lax.fori_loop(0, BLOCKS // TILE, update, 0)
        if not last:
            lax.fori_loop(0, VIEWS // 4, dot_views, 0)

    scale_store.wait()
    for tile_id in range(BLOCKS // TILE):
        for copy in stores(tile_id):
            copy.wait()

    def finish(k, carry):
        meta_copy(k).wait_send()
        return carry

    lax.fori_loop(1, OWNERS, finish, 0)
    for unit in range(UNITS):
        for copy in near_copies(unit) + far_copies(unit) + scale_copies(unit):
            copy.wait_send()
        for d in STEPS:
            for copy in slot_copies(unit, d):
                copy.wait_send()
    for t in range(ITERS):
        core_copy(t).wait_send()
        for n in range(CHIPS - 1):
            chip_copy(t, n, False).wait_send()


def store(log_in, one_in, two_in, scale_in, log_out, one_out, two_out, scale_out, bands, scale, in_sem, out_sem):
    half = GROUPS * IMG_DEV // 2
    moves = [(scale_in, scale, scale_out)]
    for part in range(2):
        rows = pl.ds(part * half, half)
        for n, (a, b) in enumerate([(log_in, log_out), (one_in, one_out), (two_in, two_out)]):
            moves.append((a.at[rows], bands.at[n, rows], b.at[rows]))
    loads = [pltpu.make_async_copy(a, m, in_sem.at[n]) for n, (a, m, b) in enumerate(moves)]
    stores = [pltpu.make_async_copy(m, b, out_sem.at[n]) for n, (a, m, b) in enumerate(moves)]
    for copy in loads:
        copy.start()
    for arrived, copy in zip(loads, stores):
        arrived.wait()
        copy.start()
    for copy in stores:
        copy.wait()


def shards(
    log_depth,
    moment_one,
    moment_two,
    image_pose,
    pair_points,
    confidence,
    pair_pose,
    first_local,
    second_owner,
    second_local,
):
    def fold(a):
        return a.reshape(IMG_DEV, GROUPS, 128).transpose(1, 0, 2).reshape(GROUPS * IMG_DEV, 128)

    def unfold(a):
        return a.reshape(GROUPS, IMG_DEV, 128).transpose(1, 0, 2).reshape(IMG_DEV, BAND)

    points = pair_points.transpose(1, 0, 2)
    conf = confidence.reshape(PAIR_DEV, 2, GROUPS, 128).transpose(0, 2, 1, 3).reshape(PAIR_DEV * GROUPS * 2, 128)
    hbm = pl.BlockSpec(memory_space=pltpu.HBM)
    band = jax.ShapeDtypeStruct((GROUPS * IMG_DEV, 128), f32)
    dma = pltpu.SemaphoreType.DMA
    out = pl.pallas_call(
        kernel,
        out_shape=(band, band, band, jax.ShapeDtypeStruct((1, PAIR_DEV), f32)),
        in_specs=[hbm] * 10,
        out_specs=(hbm,) * 4,
        scratch_shapes=[
            pltpu.VMEM((1, PAIR_DEV), f32),
            pltpu.VMEM((GROUPS * IMG_DEV, 128), f32),
            pltpu.VMEM((GROUPS * IMG_DEV, 128), f32),
            pltpu.VMEM((GROUPS * IMG_DEV, 128), f32),
            pltpu.VMEM((6, PAIR_DEV, BAND), jnp.bfloat16),
            pltpu.VMEM((PAIR_DEV * GROUPS * 2, 128), jnp.bfloat16),
            pltpu.SMEM((7, IMG_DEV * OWNERS), f32),
            pltpu.SMEM((7, PAIR_DEV), f32),
            pltpu.SMEM((PAIR_DEV,), jnp.int32),
            pltpu.SMEM((PAIR_DEV,), jnp.int32),
            pltpu.SMEM((PAIR_DEV,), jnp.int32),
            pltpu.VMEM((PAIR_DEV * GROUPS * 2, 128), f32),
            pltpu.VMEM((PAIR_DEV * GROUPS, 128), f32),
            pltpu.VMEM((PAIR_DEV * GROUPS, 128), f32),
            pltpu.VMEM((PAIR_DEV, 128), f32),
            pltpu.VMEM((UNITS, 2 * OWN_STEPS, 8 + IMG_DEV, CHUNK, 128), jnp.int16),
            pltpu.VMEM((UNITS, 2 * OWN_STEPS, 8, 128), f32),
            pltpu.VMEM((UNITS, SLOTS, 128), f32),
            pltpu.VMEM((8, IMG_DEV, 8, 128), f32),
            pltpu.VMEM((OWNERS, 8, 128), jnp.int32),
            pltpu.VMEM((VIEWS, GROUPS, 128), f32),
            pltpu.VMEM((VIEWS + 1, TILE * 8, 128), f32),
            pltpu.VMEM((3, IMG_DEV, GROUPS, 128), f32),
            pltpu.VMEM((IMG_DEV, GROUPS, 128), f32),
            pltpu.VMEM((IMG_DEV, GROUPS, 128), f32),
            pltpu.VMEM((IMG_DEV, GROUPS, 128), f32),
            pltpu.VMEM((3, 8, 128), f32),
            pltpu.VMEM((IMG_DEV, VIEWS, 128), f32),
            pltpu.VMEM((VIEWS, 128), f32),
            pltpu.VMEM((VIEWS, 128), f32),
            pltpu.VMEM((VIEWS, 128), f32),
            pltpu.VMEM((ITERS, 2, 2, 128), f32),
            pltpu.VMEM((ITERS, CHIPS, 2, 128), f32),
            pltpu.VMEM((8, 128), jnp.int32),
            pltpu.SMEM((8, 128), jnp.int32),
            dma((11,)),
            dma((BLOCKS // TILE, 3)),
            dma,
            *(dma((UNITS * 4,)) for kind in range(8)),
            dma((OWNERS,)),
            dma((OWNERS,)),
            dma((ITERS,)),
            dma((ITERS,)),
            dma((ITERS, CHIPS)),
            dma((ITERS, CHIPS)),
            *(pltpu.VMEM((4, PAIR_DEV, 2 * CHUNK, 128), jnp.int16) for unit in range(UNITS)),
            *(pltpu.VMEM((4, PAIR_DEV, 128), f32) for unit in range(UNITS)),
        ],
        compiler_params=pltpu.CompilerParams(
            collective_id=0, has_side_effects=True, vmem_limit_bytes=60 * 2**20
        ),
        name="align",
    )(
        fold(log_depth),
        fold(moment_one),
        fold(moment_two),
        points,
        conf,
        image_pose,
        pair_pose,
        first_local,
        second_owner.reshape(PAIR_DEV),
        second_local,
    )
    out = pl.pallas_call(
        store,
        out_shape=(band, band, band, jax.ShapeDtypeStruct((1, PAIR_DEV), f32)),
        in_specs=[hbm] * 4,
        out_specs=(hbm,) * 4,
        scratch_shapes=[
            pltpu.VMEM((3, GROUPS * IMG_DEV, 128), f32),
            pltpu.VMEM((1, PAIR_DEV), f32),
            dma((7,)),
            dma((7,)),
        ],
        compiler_params=pltpu.CompilerParams(vmem_limit_bytes=60 * 2**20),
        name="store",
    )(*out)
    return (unfold(out[0]), unfold(out[1]), unfold(out[2]), out[3].reshape(PAIR_DEV))


def solution(mesh):
    return jax.shard_map(
        shards,
        mesh=mesh,
        in_specs=(
            P("pair", "img"),
            P("pair", "img"),
            P("pair", "img"),
            P(),
            P("pair", None, "img"),
            P("pair", None, "img"),
            P(None, "pair"),
            P("pair"),
            P("pair", None),
            P("pair"),
        ),
        out_specs=(P("pair", "img"), P("pair", "img"), P("pair", "img"), P("pair")),
        check_vma=False,
    )
```

```python
import jax
import jax.numpy as jnp
from jax import lax
from jax.experimental import pallas as pl
from jax.experimental.pallas import tpu as pltpu
from jax.sharding import PartitionSpec as P

ROWS = 384
COLS = 512
ITERS = 3
START = 100
IMG_DEV = 4
PAIR_DEV = 8
MOST = 2
IMGS = 8
OWNERS = 16
XS = 4
YS = 4
ZS = 4
CHIPS = XS * YS * ZS
BAND = ROWS * COLS // IMGS
GROUPS = BAND // 128
BLOCKS = GROUPS // 8
BAND_ROWS = ROWS // IMGS
SLOTS = OWNERS * MOST
VIEWS = PAIR_DEV + SLOTS
UNITS = 4
CHUNK = GROUPS // UNITS
UNIT_ROWS = BAND_ROWS // UNITS
OWN_STEPS = 4
STEPS = (2, 1, 3)
TILE = 24
PART = 4
ADAM = 8
UNROLL = 8
LEVELS = 32700.0

beta_one = 0.9
beta_two = 0.999
learn_rate = 0.01
adam_eps = 1e-08
f32 = jnp.float32
MESH = pl.DeviceIdType.MESH


def rotation(scalar_q, vec_a, vec_b, vec_c):
    magnitude = jnp.sqrt(scalar_q * scalar_q + vec_a * vec_a + vec_b * vec_b + vec_c * vec_c)
    unit_s = scalar_q / magnitude
    unit_a = vec_a / magnitude
    unit_b = vec_b / magnitude
    unit_c = vec_c / magnitude
    return (
        (
            1 - 2 * (unit_b * unit_b + unit_c * unit_c),
            2 * (unit_a * unit_b - unit_s * unit_c),
            2 * (unit_a * unit_c + unit_s * unit_b),
        ),
        (
            2 * (unit_a * unit_b + unit_s * unit_c),
            1 - 2 * (unit_a * unit_a + unit_c * unit_c),
            2 * (unit_b * unit_c - unit_s * unit_a),
        ),
        (
            2 * (unit_a * unit_c - unit_s * unit_b),
            2 * (unit_b * unit_c + unit_s * unit_a),
            1 - 2 * (unit_a * unit_a + unit_b * unit_b),
        ),
    )


def kernel(
    log_hbm,
    one_hbm,
    two_hbm,
    points_hbm,
    conf_hbm,
    image_pose_hbm,
    pair_pose_hbm,
    first_local_hbm,
    second_owner_hbm,
    second_local_hbm,
    log_out,
    one_out,
    two_out,
    scale_out,
    scale_ref,
    log_ref,
    one_ref,
    two_ref,
    points_ref,
    conf_ref,
    image_pose,
    pair_pose,
    first_local,
    second_owner,
    second_local,
    conf_f,
    stage_one,
    stage_two,
    inverse_ref,
    code_two,
    unit_two,
    part_ref,
    pass_hot,
    meta,
    cu_ref,
    prefix_ref,
    state_ref,
    weight_sum,
    lever_sum,
    depth_ref,
    tau_ref,
    hot_ref,
    mask_ref,
    weight_ref,
    inner_ref,
    core_buf,
    chip_buf,
    table_ref,
    table,
    load_sem,
    store_sem,
    table_sem,
    one_send,
    one_recv,
    scale_send,
    scale_recv,
    two_send,
    two_recv,
    pass_send,
    pass_recv,
    meta_send,
    meta_recv,
    core_send,
    core_recv,
    chip_send,
    chip_recv,
    *per_unit,
):
    def load(n, src, dst):
        copy = pltpu.make_async_copy(src, dst, load_sem.at[n])
        copy.start()
        return copy

    small = [
        load(0, second_owner_hbm, second_owner),
        load(1, second_local_hbm, second_local),
        load(2, first_local_hbm, first_local),
        load(3, pair_pose_hbm, pair_pose),
        load(4, image_pose_hbm, image_pose),
    ]
    conf_load = load(5, conf_hbm, conf_ref)
    second_load = load(6, points_hbm.at[pl.ds(3, 3)], points_ref.at[pl.ds(3, 3)])
    first_load = load(7, points_hbm.at[pl.ds(0, 3)], points_ref.at[pl.ds(0, 3)])
    log_load = load(8, log_hbm, log_ref)
    state_loads = [load(9, one_hbm, one_ref), load(10, two_hbm, two_ref)]

    my_img = lax.axis_index("img")
    my_pair = lax.axis_index("pair")
    my_y = my_pair // ZS
    my_z = my_pair % ZS

    def pair_at(k, sign):
        return ((my_y + sign * (k // ZS) + YS) % YS) * ZS + (my_z + sign * (k % ZS) + ZS) % ZS

    barrier = pltpu.get_barrier_semaphore()

    my_x = my_img // 2
    my_core = my_img % 2
    my_chip = my_x * OWNERS + my_pair
    xs = [(my_x + d) % XS for d in range(XS)]
    ys = [(my_y + d) % YS for d in range(YS)]
    zs = [(my_z + d) % ZS for d in range(ZS)]
    offsets = [(a, b, c) for a in range(XS) for b in range(YS) for c in range(ZS) if (a, b, c) != (0, 0, 0)]
    offsets.sort(key=lambda o: -sum(min(d, 4 - d) for d in o))

    pl.semaphore_signal(barrier, 1, device_id=(my_img + 1 - 2 * my_core, my_pair), device_id_type=MESH)
    for a, b, c in offsets:
        pl.semaphore_signal(barrier, 1, device_id=(xs[a] * 2 + my_core, ys[b] * ZS + zs[c]), device_id_type=MESH)

    sub = lax.broadcasted_iota(jnp.int32, (8, 128), 0)
    lane = lax.broadcasted_iota(jnp.int32, (8, 128), 1)

    for copy in small:
        copy.wait()

    owners = [second_owner[e] for e in range(PAIR_DEV)]
    order = []
    for e in range(PAIR_DEV):
        rank = jnp.int32(0)
        for other in range(e):
            rank = rank + jnp.where(owners[other] == owners[e], 1, 0)
        order.append(owners[e] * MOST + rank)
    row = jnp.zeros((8, 128), jnp.int32)
    for e in range(PAIR_DEV):
        here = lane == my_pair * PAIR_DEV + e
        row = jnp.where(here & (sub == 0), order[e], row)
        row = jnp.where(here & (sub == 1), second_local[e], row)
    meta[0] = row

    def column(values):
        out = jnp.zeros((8, 128), f32)
        for e in range(PAIR_DEV):
            out = jnp.where(sub == e, values[e], out)
        return out

    pair_cols = [column([pair_pose[i, e] for e in range(PAIR_DEV)]) for i in range(7)]
    pair_rot = rotation(*pair_cols[:4])
    shift = pair_cols[4:]
    firsts = [my_pair * IMG_DEV + first_local[e] for e in range(PAIR_DEV)]
    seconds = [owners[e] * IMG_DEV + second_local[e] for e in range(PAIR_DEV)]
    lean = [2.0 * sum(pair_rot[i][j] * shift[i] for i in range(3)) for j in range(3)]
    shift_sq = sum(shift[i] * shift[i] for i in range(3))
    first_row = (my_img * BAND_ROWS).astype(f32)
    ray_y0 = (first_row + 0.5 - ROWS / 2) / COLS
    ray_x = [((lane + 128 * part).astype(f32) + 0.5 - COLS / 2) / COLS for part in range(4)]

    def widen(step, carry):
        rows = pl.ds(pl.multiple_of(step * 64, 64), 64)
        conf_f[rows, :] = conf_ref[rows, :].astype(f32)
        return carry

    conf_load.wait()
    lax.fori_loop(0, PAIR_DEV * 2 * GROUPS // 64, widen, 0)
    second_load.wait()

    def prepare(view, images, stage):
        cols = [column([image_pose[i, images[e]] for e in range(PAIR_DEV)]) for i in range(7)]
        rot = rotation(*cols[:4])
        trans = cols[4:]
        both = [[sum(rot[l][i] * pair_rot[l][j] for l in range(3)) for j in range(3)] for i in range(3)]
        moved = [sum(rot[l][i] * shift[l] for l in range(3)) for i in range(3)]
        full = [[both[i][0], both[i][1], both[i][2], moved[i]] for i in range(3)]
        base = [[ray_x[part] * full[0][j] + (full[2][j] + ray_y0 * full[1][j]) for part in range(4)] for j in range(4)]
        slope = [full[1][j] * (1.0 / COLS) for j in range(4)]
        toward = [sum(trans[l] * pair_rot[l][j] for l in range(3)) for j in range(3)]
        offset = sum(trans[l] * shift[l] for l in range(3))

        def body(r, carry):
            total_sq, total_dot, total_conf, largest = carry
            down = r.astype(f32)
            tilt = [slope[j] * down for j in range(4)]
            for part in range(4):
                at = pl.ds(pl.multiple_of(r * COLS + part * 128, 128), 128)
                x = [points_ref[3 * view + j, :, at].astype(f32) for j in range(3)]
                weight = conf_f[pl.ds((r * 4 + part) * 2 + view, 8, stride=2 * GROUPS), :]
                value = base[3][part] + tilt[3]
                for j in range(3):
                    value = value + (base[j][part] + tilt[j]) * x[j]
                value = value * weight
                largest = jnp.maximum(largest, jnp.abs(value))
                stage[pl.ds(pl.multiple_of((r * 4 + part) * 8, 8), 8), :] = value
                square = x[0] * (x[0] + lean[0]) + x[1] * (x[1] + lean[1]) + x[2] * (x[2] + lean[2])
                dot = x[0] * toward[0] + x[1] * toward[1] + x[2] * toward[2]
                total_sq = total_sq + weight * square
                total_dot = total_dot + weight * dot
                total_conf = total_conf + weight
            return (total_sq, total_dot, total_conf, largest)

        def run(unit, sums):
            tiny = jnp.full((8, 128), 1e-30, f32)
            start = unit * UNIT_ROWS
            out = lax.fori_loop(start, start + UNIT_ROWS, body, (*sums, tiny))
            return out[:3], out[3]

        def close(sums):
            return (sums[0] + sums[2] * shift_sq, sums[1] + sums[2] * offset)

        return run, close

    empty = (jnp.zeros((8, 128), f32),) * 3
    code_one, unit_one = per_unit[:UNITS], per_unit[UNITS:]
    run_two, close_two = prepare(1, seconds, stage_two)

    def encode(unit, largest):
        unit_one[unit][0] = largest * (1.0 / LEVELS)
        inverse_ref[...] = LEVELS / largest

        def body(e, carry):
            inverse = inverse_ref[pl.ds(e, 1), :]
            for step in range(CHUNK // 16):
                place = unit * (CHUNK // 16) + step
                rows = slice(step * 16, step * 16 + 16)
                value = stage_two[pl.ds(place * 128 + e, 16, stride=8), :] * inverse
                code_one[unit][0, e, rows, :] = jnp.floor(value + 0.5).astype(jnp.int32).astype(jnp.int16)
                weight = conf_f[pl.ds(e * 2 * GROUPS + place * 32 + 1, 16, stride=2), :] * 128.0
                rows = slice(CHUNK + step * 16, CHUNK + step * 16 + 16)
                code_one[unit][0, e, rows, :] = weight.astype(jnp.int32).astype(jnp.int16)
            return carry

        lax.fori_loop(0, PAIR_DEV, body, 0)

    def ahead(axis, d):
        if axis == 0:
            return (my_img, ys[d] * ZS + my_z)
        return (my_img, my_y * ZS + zs[d])

    def remote(src, dst, sems, place, device):
        return pltpu.make_async_remote_copy(
            src_ref=src,
            dst_ref=dst,
            send_sem=sems[0].at[place],
            recv_sem=sems[1].at[place],
            device_id=device,
            device_id_type=MESH,
        )

    def near_copies(unit):
        return [
            remote(code_one[unit].at[0], code_one[unit].at[d], (one_send, one_recv), unit * 4 + d, ahead(unit % 2, d))
            for d in (1, 3)
        ]

    def far_copies(unit):
        half = PAIR_DEV // 2
        return [
            remote(
                code_one[unit].at[d, part], code_one[unit].at[2, part], (one_send, one_recv), unit * 4 + n, ahead(unit % 2, d)
            )
            for d, n, part in ((1, 0, pl.ds(0, half)), (3, 2, pl.ds(half, half)))
        ]

    def scale_copies(unit):
        return [
            remote(unit_one[unit].at[0], unit_one[unit].at[d], (scale_send, scale_recv), unit * 4 + d, ahead(unit % 2, d))
            for d in STEPS
        ]

    def slot_copies(unit, d):
        place = unit * 4 + d
        to = ahead(1 - unit % 2, d)
        return [
            remote(code_two.at[unit, d], code_two.at[unit, OWN_STEPS + d], (two_send, two_recv), place, to),
            remote(unit_two.at[unit, d], unit_two.at[unit, OWN_STEPS + d], (pass_send, pass_recv), place, to),
        ]

    def send(unit, sums):
        sums, largest = run_two(unit, sums)
        encode(unit, largest)
        if unit == 0:
            pl.semaphore_wait(barrier, CHIPS)
        for copy in near_copies(unit) + scale_copies(unit):
            copy.start()
        return sums

    def hand_on(unit):
        for arrived, copy in zip(near_copies(unit), far_copies(unit)):
            arrived.wait_recv()
            copy.start()

    sums = send(0, empty)

    def meta_copy(k):
        return pltpu.make_async_remote_copy(
            src_ref=meta.at[0],
            dst_ref=meta.at[k],
            send_sem=meta_send.at[k],
            recv_sem=meta_recv.at[k],
            device_id=(my_img, pair_at(k, 1)),
            device_id_type=MESH,
        )

    def start_meta(k, carry):
        meta_copy(k).start()
        return carry

    lax.fori_loop(1, OWNERS, start_meta, 0)
    for unit in range(1, UNITS):
        sums = send(unit, sums)
    square_two, dot_two = close_two(sums)
    def depth_of(values):
        return jnp.exp(values.astype(jnp.bfloat16).astype(f32))

    def image_rows(block, v):
        return pl.ds(block * 32 + v, 8, stride=IMG_DEV)

    def block_rows(block):
        return pl.ds(pl.multiple_of(block * 8, 8), 8)

    def first_depth(block, carry):
        for v in range(IMG_DEV):
            value = log_ref[image_rows(block, v), :]
            state_ref[0, v, block_rows(block), :] = value
            depth_ref[v, block_rows(block), :] = depth_of(value)
        return carry

    def fold_moments(block, carry):
        for v in range(IMG_DEV):
            state_ref[1, v, block_rows(block), :] = one_ref[image_rows(block, v), :]
            state_ref[2, v, block_rows(block), :] = two_ref[image_rows(block, v), :]
        return carry

    def pass_on(unit, d):
        place = d if d > 0 else OWN_STEPS
        index = unit % 2 * 4 + d
        sources = [table[3, index * 8 + n] for n in range(8)]
        hots = [[pass_hot[index, v, n : n + 1, :] for v in range(IMG_DEV)] for n in range(8)]
        for n in range(8):
            unit_two[unit, place, n : n + 1, :] = unit_one[unit][n // MOST, pl.ds(sources[n], 1), :]

        def body(step, carry):
            rows = pl.ds(pl.multiple_of(step * 16, 16), 16)
            weight_rows = pl.ds(pl.multiple_of(CHUNK + step * 16, 16), 16)
            totals = [jnp.zeros((16, 128), f32) for v in range(IMG_DEV)]
            for n in range(8):
                code_two[unit, place, n, rows, :] = code_one[unit][n // MOST, sources[n], rows, :]
                weight = code_one[unit][n // MOST, sources[n], weight_rows, :].astype(jnp.int32).astype(f32)
                for v in range(IMG_DEV):
                    totals[v] = totals[v] + weight * hots[n][v]
            for v in range(IMG_DEV):
                code_two[unit, place, 8 + v, rows, :] = totals[v].astype(jnp.int32).astype(jnp.int16)
            return carry

        for step in range(CHUNK // 16):
            body(step, 0)

    def take(unit, d):
        place = OWN_STEPS + d
        slots = []
        for n in range(8):
            step = n // MOST * 4 + d if unit % 2 == 0 else d * 4 + n // MOST
            slots.append(PAIR_DEV + step * MOST + n % MOST)
        units = [unit_two[unit, place, n : n + 1, :] for n in range(8)]
        images = [table[0, slot] for slot in slots]

        def body(step, totals):
            totals = list(totals)
            rows = pl.ds(pl.multiple_of(step * 16, 16), 16)
            full = pl.ds(pl.multiple_of(unit * CHUNK + step * 16, 16), 16)
            for n in range(8):
                cu = code_two[unit, place, n, rows, :].astype(jnp.int32).astype(f32) * units[n]
                cu_ref[slots[n], full, :] = cu
                cu = cu * depth_ref[images[n], full, :]
                totals[n] = totals[n] + (cu[0:8] + cu[8:16])
            for v in range(IMG_DEV):
                weight = code_two[unit, place, 8 + v, rows, :].astype(jnp.int32).astype(f32)
                weight_sum[v, full, :] = weight_sum[v, full, :] + weight * (1.0 / 128.0)
            return tuple(totals)

        totals = (jnp.zeros((8, 128), f32),) * 8
        for step in range(CHUNK // 16):
            totals = body(step, totals)
        for n in range(8):
            row = slice(slots[n] - PAIR_DEV, slots[n] - PAIR_DEV + 1)
            part_ref[unit, row, :] = jnp.sum(totals[n], axis=0, keepdims=True)

    def relay(unit):
        for copy in far_copies(unit) + scale_copies(unit):
            copy.wait_recv()
        for d in STEPS:
            pass_on(unit, d)
            for copy in slot_copies(unit, d):
                copy.start()
    own = [[image_pose[i, my_pair * IMG_DEV + min(v, IMG_DEV - 1)] for v in range(8)] for i in range(7)]
    own_cols = [column(own[i]) for i in range(7)]
    own_rot = rotation(*own_cols[:4])
    for i in range(3):
        tau_ref[i] = sum(own_rot[l][i] * own_cols[4 + l] for l in range(3))

    for k in range(1, OWNERS):
        meta_copy(k).wait_recv()
    known = meta[0]
    for k in range(1, OWNERS):
        known = known + meta[k]
    code_row = jnp.broadcast_to(known[0:1], (8, 128))
    local_row = jnp.broadcast_to(known[1:2], (8, 128))
    from_pair = lane // PAIR_DEV
    step_of = ((my_y - from_pair // ZS + YS) % YS) * ZS + (my_z - from_pair % ZS + ZS) % ZS
    slot_of = jnp.where(code_row // MOST == my_pair, step_of * MOST + code_row % MOST, -1)
    local_first = jnp.zeros((8, 128), jnp.int32)
    for e in range(PAIR_DEV):
        local_first = jnp.where(sub == e, first_local[e], local_first)
    own_mask = jnp.where(lane == my_pair * PAIR_DEV + sub, 1.0, 0.0)
    mask_ref[0:8, :] = own_mask
    for v in range(IMG_DEV):
        hot_ref[v, 0:8, :] = jnp.where(local_first == v, 1.0, 0.0)
    for group in range(SLOTS // 8):
        rows = pl.ds(8 + group * 8, 8)
        held = slot_of == sub + group * 8
        mask_ref[rows, :] = jnp.where(held, 1.0, 0.0)
        for v in range(IMG_DEV):
            found = jnp.where(held & (local_row == v), 1.0, 0.0)
            hot_ref[v, rows, :] = jnp.broadcast_to(jnp.sum(found, axis=1, keepdims=True), (8, 128))

    image_row = jnp.zeros((8, 128), jnp.int32)
    for group in range(VIEWS // 8):
        if group == 0:
            image_col = local_first
        else:
            held = (slot_of == sub + (group - 1) * 8).astype(jnp.int32)
            image_col = jnp.sum(held * (local_row - IMG_DEV), axis=1, keepdims=True) + IMG_DEV
        found = jnp.where(lane == sub + group * 8, image_col, 0)
        image_row = image_row + jnp.broadcast_to(jnp.sum(found, axis=0, keepdims=True), (8, 128))
    order_row = jnp.zeros((8, 128), jnp.int32)
    listed = lane < VIEWS
    for group in range(VIEWS // 8):
        view = sub + group * 8
        found = jnp.where(lane == view, image_row, 0)
        image_col = jnp.sum(found, axis=1, keepdims=True)
        before = listed & ((image_row < image_col) | ((image_row == image_col) & (lane < view)))
        place = jnp.sum(before.astype(jnp.int32), axis=1, keepdims=True)
        found = jnp.where(lane == place, view, 0)
        order_row = order_row + jnp.broadcast_to(jnp.sum(found, axis=0, keepdims=True), (8, 128))
    end_row = jnp.zeros((8, 128), jnp.int32)
    for v in range(IMG_DEV):
        upto = (listed & (image_row <= v)).astype(jnp.int32)
        end_row = jnp.where(lane == v, jnp.sum(upto, axis=1, keepdims=True), end_row)
    image_row = jnp.minimum(image_row, IMG_DEV - 1)

    pass_row = jnp.zeros((8, 128), jnp.int32)
    for half in range(2):
        for d in range(4):
            if half == 0:
                goal = my_y * ZS + zs[d]
                source = ((my_y - sub // MOST + YS) % YS) * ZS + my_z
            else:
                goal = ys[d] * ZS + my_z
                source = my_y * ZS + (my_z - sub // MOST + ZS) % ZS
            match = (from_pair == source) & (code_row == goal * MOST + sub % MOST)
            chosen = jnp.sum(jnp.where(match, lane % PAIR_DEV, 0), axis=1, keepdims=True)
            found = jnp.where(lane == sub + (half * 4 + d) * 8, chosen, 0)
            pass_row = pass_row + jnp.broadcast_to(jnp.sum(found, axis=0, keepdims=True), (8, 128))
            for v in range(IMG_DEV):
                hot = jnp.where(match & (local_row == v), 1.0, 0.0)
                pass_hot[half * 4 + d, v] = jnp.broadcast_to(jnp.sum(hot, axis=1, keepdims=True), (8, 128))
    table_ref[...] = jnp.where(sub == 0, image_row, jnp.where(sub == 1, order_row, jnp.where(sub == 2, end_row, pass_row)))
    table_copy = pltpu.make_async_copy(table_ref, table, table_sem)
    table_copy.start()

    first_load.wait()
    run_one, close_one = prepare(0, firsts, stage_one)
    sums = empty
    for unit in range(UNITS):
        sums, largest = run_one(unit, sums)
    square_one, dot_one = close_one(sums)

    hand_on(0)
    hand_on(1)
    log_load.wait()
    lax.fori_loop(0, BLOCKS, first_depth, 0)
    for copy in state_loads:
        copy.wait()

    lax.fori_loop(0, BLOCKS, fold_moments, 0)

    for unit in range(2, UNITS):
        hand_on(unit)
    table_copy.wait()
    for unit in range(UNITS):
        relay(unit)

    def first_copy(e, carry):
        for block in range(BLOCKS):
            cu_ref[e, block * 8 : block * 8 + 8, :] = stage_one[pl.ds(block * 64 + e, 8, stride=8), :]
        return carry

    lax.fori_loop(0, PAIR_DEV, first_copy, 0)

    def dot_views(step, carry):
        for n in range(4):
            dot_view(step * 4 + n, carry)
        return carry

    def dot_view(r, carry):
        v = table[0, r]
        totals = [jnp.zeros((8, 128), f32) for n in range(PART)]
        for block in range(BLOCKS):
            rows = slice(block * 8, block * 8 + 8)
            totals[block % PART] = totals[block % PART] + cu_ref[r, rows, :] * depth_ref[v, rows, :]
        total = (totals[0] + totals[1]) + (totals[2] + totals[3])
        inner_ref[pl.ds(r, 1), :] = jnp.sum(total, axis=0, keepdims=True)
        return carry

    lax.fori_loop(0, PAIR_DEV // 4, dot_views, 0)

    def first_sums(block, carry):
        sums = [jnp.zeros((8, 128), f32) for v in range(IMG_DEV)]
        for e in range(PAIR_DEV):
            weight = conf_f[pl.ds(e * 2 * GROUPS + block * 16, 8, stride=2), :]
            for v in range(IMG_DEV):
                sums[v] = sums[v] + weight * hot_ref[v, e : e + 1, :]
        for v in range(IMG_DEV):
            weight_sum[v, block_rows(block), :] = sums[v]
        return carry

    lax.fori_loop(0, BLOCKS, first_sums, 0)

    for unit in range(UNITS):
        pass_on(unit, 0)
        take(unit, 0)
    for unit in range(UNITS):
        for d in STEPS:
            for copy in slot_copies(unit, d):
                copy.wait_recv()
            take(unit, d)
    inner_ref[PAIR_DEV:VIEWS, :] = sum(part_ref[unit] for unit in range(1, UNITS)) + part_ref[0]

    def pair_row(col):
        return jnp.sum(jnp.sum(col, axis=1, keepdims=True) * own_mask, axis=0, keepdims=True)

    fixed_row = pair_row(dot_one + dot_two)
    square_row = pair_row(square_one + square_two)

    def core_copy(t):
        return pltpu.make_async_remote_copy(
            src_ref=core_buf.at[t, 0],
            dst_ref=core_buf.at[t, 1],
            send_sem=core_send.at[t],
            recv_sem=core_recv.at[t],
            device_id=(my_img + 1 - 2 * my_core, my_pair),
            device_id_type=MESH,
        )

    def chip_copy(t, n, arrival):
        a, b, c = offsets[n]
        pair = ys[b] * ZS + zs[c]
        place = xs[a] * OWNERS + pair if arrival else my_chip
        return pltpu.make_async_remote_copy(
            src_ref=chip_buf.at[t, place],
            dst_ref=chip_buf.at[t, place],
            send_sem=chip_send.at[t, n],
            recv_sem=chip_recv.at[t, place],
            device_id=(xs[a] * 2 + my_core, pair),
            device_id_type=MESH,
        )

    def sum_all(t, tile, beside):
        core_buf[t, 0] = tile
        core_copy(t).start()
        core_copy(t).wait_recv()
        chip_buf[t, my_chip] = tile + core_buf[t, 1]
        for n in range(CHIPS - 1):
            chip_copy(t, n, False).start()
        beside()
        for n in reversed(range(CHIPS - 1)):
            chip_copy(t, n, True).wait_recv()
        parts = [chip_buf[t, n] for n in range(CHIPS)]
        while len(parts) > 1:
            parts = [parts[n] + parts[n + 1] for n in range(0, len(parts), 2)]
        return parts[0]

    def stores(tile_id):
        rows = pl.ds(pl.multiple_of(tile_id * TILE * 32, 8), TILE * 32)
        pairs = [(log_ref, log_out), (one_ref, one_out), (two_ref, two_out)]
        return [
            pltpu.make_async_copy(a.at[rows], b.at[rows], store_sem.at[tile_id, n])
            for n, (a, b) in enumerate(pairs)
        ]

    scale_store = pltpu.make_async_copy(scale_ref, scale_out, load_sem.at[0])
    def ray_sums():
        def body(block, carry):
            down = (block * 2 + sub // 4).astype(f32) + first_row
            rays_y = (down + 0.5 - ROWS / 2) / COLS
            rays_x = (((sub % 4) * 128 + lane).astype(f32) + 0.5 - COLS / 2) / COLS
            length = rays_x * rays_x + rays_y * rays_y + 1.0
            rows = block_rows(block)
            for v in range(IMG_DEV):
                lever = rays_x * tau_ref[0, v : v + 1, :] + rays_y * tau_ref[1, v : v + 1, :] + tau_ref[2, v : v + 1, :]
                weight = weight_sum[v, rows, :]
                lever_sum[v, rows, :] = lever * weight
                weight_sum[v, rows, :] = length * weight
            return carry

        lax.fori_loop(0, BLOCKS, body, 0)

    denominator = None
    for sweep in range(ITERS):
        row = jnp.zeros((8, 128), f32)
        for group in range(VIEWS // 8):
            rows = slice(group * 8, group * 8 + 8)
            row = row + jnp.sum(inner_ref[rows, :], axis=1, keepdims=True) * mask_ref[rows, :]
        row = jnp.sum(row, axis=0, keepdims=True) + fixed_row
        two = lax.broadcasted_iota(jnp.int32, (2, 128), 0)
        total = sum_all(sweep, jnp.where(two == 0, row, square_row), ray_sums if sweep == 0 else lambda: None)
        if sweep == 0:
            denominator = total[1:2]
        scales = jnp.broadcast_to(total[0:1] / denominator, (8, 128))
        for group in range(VIEWS // 8):
            rows = slice(group * 8, group * 8 + 8)
            held = jnp.sum(scales * mask_ref[rows, :], axis=1, keepdims=True)
            if group == 0 and sweep == ITERS - 1:
                own_row = jnp.sum(jnp.where(lane == sub, held, 0.0), axis=0, keepdims=True)
                scale_ref[...] = own_row[:, 0:PAIR_DEV]
                scale_store.start()
            weight_ref[rows, :] = jnp.broadcast_to(held, (8, 128))

        steps = START + sweep + 1
        bias_one = 1 - beta_one**steps
        bias_two = 1 - beta_two**steps
        last = sweep == ITERS - 1

        def update(tile_id, carry):
            start = tile_id * TILE

            def gather(step, sums):
                sums = list(sums)
                for n in range(UNROLL):
                    q = step * UNROLL + n
                    r = table[1, q]
                    weight = weight_ref[pl.ds(r, 1), :]
                    for m in range(TILE):
                        sums[m] = sums[m] + cu_ref[r, block_rows(start + m), :] * weight
                        prefix_ref[q + 1, m * 8 : m * 8 + 8, :] = sums[m]
                return tuple(sums)

            zero = jnp.zeros((8, 128), f32)
            for m in range(TILE):
                prefix_ref[0, m * 8 : m * 8 + 8, :] = zero
            lax.fori_loop(0, VIEWS // UNROLL, gather, (zero,) * TILE)
            def step_adam(step, carry):
                for m in range(ADAM):
                    n = step * ADAM + m
                    block = start + n
                    here = pl.ds(pl.multiple_of(n * 8, 8), 8)
                    for v in range(IMG_DEV):
                        depth = depth_ref[v, block_rows(block), :]
                        gathered = prefix_ref[table[2, v], here, :]
                        if v > 0:
                            gathered = gathered - prefix_ref[table[2, v - 1], here, :]
                        pull = depth * weight_sum[v, block_rows(block), :] + lever_sum[v, block_rows(block), :] - gathered
                        half_gradient = depth * pull
                        rows = block_rows(block)
                        old_log, old_one, old_two = (state_ref[n, v, rows, :] for n in range(3))
                        new_one = beta_one * old_one + (2 * (1 - beta_one)) * half_gradient
                        new_two = beta_two * old_two + (4 * (1 - beta_two)) * (half_gradient * half_gradient)
                        corrected_two = new_two * (1 / bias_two)
                        root = corrected_two * lax.rsqrt(corrected_two) + adam_eps
                        inverse = pl.reciprocal(root, approx=True)
                        inverse = inverse * (2.0 - root * inverse)
                        new_log = old_log - (learn_rate / bias_one) * (new_one * inverse)
                        if last:
                            rows = image_rows(block, v)
                            log_ref[rows, :] = new_log
                            one_ref[rows, :] = new_one
                            two_ref[rows, :] = new_two
                        else:
                            state_ref[0, v, rows, :] = new_log
                            state_ref[1, v, rows, :] = new_one
                            state_ref[2, v, rows, :] = new_two
                            depth_ref[v, rows, :] = depth_of(new_log)
                return carry

            lax.fori_loop(0, TILE // ADAM, step_adam, 0)
            if last:
                for copy in stores(tile_id):
                    copy.start()
            return carry

        lax.fori_loop(0, BLOCKS // TILE, update, 0)
        if not last:
            lax.fori_loop(0, VIEWS // 4, dot_views, 0)

    scale_store.wait()
    for tile_id in range(BLOCKS // TILE):
        for copy in stores(tile_id):
            copy.wait()

    def finish(k, carry):
        meta_copy(k).wait_send()
        return carry

    lax.fori_loop(1, OWNERS, finish, 0)
    for unit in range(UNITS):
        for copy in near_copies(unit) + far_copies(unit) + scale_copies(unit):
            copy.wait_send()
        for d in STEPS:
            for copy in slot_copies(unit, d):
                copy.wait_send()
    for t in range(ITERS):
        core_copy(t).wait_send()
        for n in range(CHIPS - 1):
            chip_copy(t, n, False).wait_send()


def store(log_in, one_in, two_in, scale_in, log_out, one_out, two_out, scale_out, bands, scale, in_sem, out_sem):
    half = GROUPS * IMG_DEV // 2
    moves = [(scale_in, scale, scale_out)]
    for part in range(2):
        rows = pl.ds(part * half, half)
        for n, (a, b) in enumerate([(log_in, log_out), (one_in, one_out), (two_in, two_out)]):
            moves.append((a.at[rows], bands.at[n, rows], b.at[rows]))
    loads = [pltpu.make_async_copy(a, m, in_sem.at[n]) for n, (a, m, b) in enumerate(moves)]
    stores = [pltpu.make_async_copy(m, b, out_sem.at[n]) for n, (a, m, b) in enumerate(moves)]
    for copy in loads:
        copy.start()
    for arrived, copy in zip(loads, stores):
        arrived.wait()
        copy.start()
    for copy in stores:
        copy.wait()


def shards(
    log_depth,
    moment_one,
    moment_two,
    image_pose,
    pair_points,
    confidence,
    pair_pose,
    first_local,
    second_owner,
    second_local,
):
    def fold(a):
        return a.reshape(IMG_DEV, GROUPS, 128).transpose(1, 0, 2).reshape(GROUPS * IMG_DEV, 128)

    def unfold(a):
        return a.reshape(GROUPS, IMG_DEV, 128).transpose(1, 0, 2).reshape(IMG_DEV, BAND)

    points = pair_points.transpose(1, 0, 2)
    conf = confidence.reshape(PAIR_DEV, 2, GROUPS, 128).transpose(0, 2, 1, 3).reshape(PAIR_DEV * GROUPS * 2, 128)
    hbm = pl.BlockSpec(memory_space=pltpu.HBM)
    band = jax.ShapeDtypeStruct((GROUPS * IMG_DEV, 128), f32)
    dma = pltpu.SemaphoreType.DMA
    out = pl.pallas_call(
        kernel,
        out_shape=(band, band, band, jax.ShapeDtypeStruct((1, PAIR_DEV), f32)),
        in_specs=[hbm] * 10,
        out_specs=(hbm,) * 4,
        scratch_shapes=[
            pltpu.VMEM((1, PAIR_DEV), f32),
            pltpu.VMEM((GROUPS * IMG_DEV, 128), f32),
            pltpu.VMEM((GROUPS * IMG_DEV, 128), f32),
            pltpu.VMEM((GROUPS * IMG_DEV, 128), f32),
            pltpu.VMEM((6, PAIR_DEV, BAND), jnp.bfloat16),
            pltpu.VMEM((PAIR_DEV * GROUPS * 2, 128), jnp.bfloat16),
            pltpu.SMEM((7, IMG_DEV * OWNERS), f32),
            pltpu.SMEM((7, PAIR_DEV), f32),
            pltpu.SMEM((PAIR_DEV,), jnp.int32),
            pltpu.SMEM((PAIR_DEV,), jnp.int32),
            pltpu.SMEM((PAIR_DEV,), jnp.int32),
            pltpu.VMEM((PAIR_DEV * GROUPS * 2, 128), f32),
            pltpu.VMEM((PAIR_DEV * GROUPS, 128), f32),
            pltpu.VMEM((PAIR_DEV * GROUPS, 128), f32),
            pltpu.VMEM((PAIR_DEV, 128), f32),
            pltpu.VMEM((UNITS, 2 * OWN_STEPS, 8 + IMG_DEV, CHUNK, 128), jnp.int16),
            pltpu.VMEM((UNITS, 2 * OWN_STEPS, 8, 128), f32),
            pltpu.VMEM((UNITS, SLOTS, 128), f32),
            pltpu.VMEM((8, IMG_DEV, 8, 128), f32),
            pltpu.VMEM((OWNERS, 8, 128), jnp.int32),
            pltpu.VMEM((VIEWS, GROUPS, 128), f32),
            pltpu.VMEM((VIEWS + 1, TILE * 8, 128), f32),
            pltpu.VMEM((3, IMG_DEV, GROUPS, 128), f32),
            pltpu.VMEM((IMG_DEV, GROUPS, 128), f32),
            pltpu.VMEM((IMG_DEV, GROUPS, 128), f32),
            pltpu.VMEM((IMG_DEV, GROUPS, 128), f32),
            pltpu.VMEM((3, 8, 128), f32),
            pltpu.VMEM((IMG_DEV, VIEWS, 128), f32),
            pltpu.VMEM((VIEWS, 128), f32),
            pltpu.VMEM((VIEWS, 128), f32),
            pltpu.VMEM((VIEWS, 128), f32),
            pltpu.VMEM((ITERS, 2, 2, 128), f32),
            pltpu.VMEM((ITERS, CHIPS, 2, 128), f32),
            pltpu.VMEM((8, 128), jnp.int32),
            pltpu.SMEM((8, 128), jnp.int32),
            dma((11,)),
            dma((BLOCKS // TILE, 3)),
            dma,
            *(dma((UNITS * 4,)) for kind in range(8)),
            dma((OWNERS,)),
            dma((OWNERS,)),
            dma((ITERS,)),
            dma((ITERS,)),
            dma((ITERS, CHIPS)),
            dma((ITERS, CHIPS)),
            *(pltpu.VMEM((4, PAIR_DEV, 2 * CHUNK, 128), jnp.int16) for unit in range(UNITS)),
            *(pltpu.VMEM((4, PAIR_DEV, 128), f32) for unit in range(UNITS)),
        ],
        compiler_params=pltpu.CompilerParams(
            collective_id=0, has_side_effects=True, vmem_limit_bytes=60 * 2**20
        ),
        name="align",
    )(
        fold(log_depth),
        fold(moment_one),
        fold(moment_two),
        points,
        conf,
        image_pose,
        pair_pose,
        first_local,
        second_owner.reshape(PAIR_DEV),
        second_local,
    )
    out = pl.pallas_call(
        store,
        out_shape=(band, band, band, jax.ShapeDtypeStruct((1, PAIR_DEV), f32)),
        in_specs=[hbm] * 4,
        out_specs=(hbm,) * 4,
        scratch_shapes=[
            pltpu.VMEM((3, GROUPS * IMG_DEV, 128), f32),
            pltpu.VMEM((1, PAIR_DEV), f32),
            dma((7,)),
            dma((7,)),
        ],
        compiler_params=pltpu.CompilerParams(vmem_limit_bytes=60 * 2**20),
        name="store",
    )(*out)
    return (unfold(out[0]), unfold(out[1]), unfold(out[2]), out[3].reshape(PAIR_DEV))


def solution(mesh):
    return jax.shard_map(
        shards,
        mesh=mesh,
        in_specs=(
            P("pair", "img"),
            P("pair", "img"),
            P("pair", "img"),
            P(),
            P("pair", None, "img"),
            P("pair", None, "img"),
            P(None, "pair"),
            P("pair"),
            P("pair", None),
            P("pair"),
        ),
        out_specs=(P("pair", "img"), P("pair", "img"), P("pair", "img"), P("pair")),
        check_vma=False,
    )
```
